512 devices in a mesh: leaf: 64 (over y, z), front: 8 (over x, core).
Axes of the slice: x: 4, y: 4, z: 16, core: 2. Of those that a mesh axis runs over, the one named last changes fastest.
Arguments:
- leaf_rhs: bfloat16 [64, 256, 4, 512], P('leaf', 'front'), may hold values from -6 to 6
- sep_rhs: bfloat16 [64, 512, 768], P('leaf', 'front'), may hold values from -6 to 6
- leaf_noise: bfloat16 [64, 256, 4, 512], P('leaf', 'front'), may hold values from -6 to 6
- sep_noise: bfloat16 [64, 512, 768], P('leaf', 'front'), may hold values from -6 to 6
- leaf_inverse: bfloat16 [64, 4, 256, 256], P('leaf', None, 'front'), as said below
- leaf_left: bfloat16 [64, 4, 256, 768], P('leaf', None, 'front'), may hold values from -0.09375 to 0.09375
- leaf_right: bfloat16 [64, 4, 256, 768], P('leaf', None, 'front'), may hold values from -0.09375 to 0.09375
- sep_inverse: bfloat16 [64, 768, 768], P('leaf'), as said below
- sep_left: bfloat16 [64, 768, 768], P('leaf'), may hold values from -0.109375 to 0.109375
- sep_right: bfloat16 [64, 768, 768], P('leaf'), may hold values from -0.109375 to 0.109375
- leaf_count: int32 [64], P('leaf'), may hold values from 1 to 4, as said below
Outputs:
- leaf_draws: float32 [64, 256, 4, 512], P('leaf', 'front')
- sep_draws: float32 [64, 512, 768], P('leaf', 'front')
The draws below stay inside these ranges and needn't reach their ends.
Inputs may be any that keep to these rules, and one draw needn't show every extreme that they name: `leaf_count`: every section has at least one live leaf supernode, and some section has 4. `leaf_inverse`: each block is lower triangular with a positive diagonal. `sep_inverse`: each block is lower triangular with a positive diagonal.
All inputs are finite; a program needn't handle non-finite values.
Results may differ from the reference program's by a relative error of at most 0.034.
Values may be sent and summed in bfloat16 or wider, within the bound.
A program may use at most 64 MiB of HBM per device.

```python
import math
import jax
import jax.numpy as jnp
import numpy as np
from jax import lax

S = 256
CAP = 4
P_SIZE = 768
COLS = 512
N_LEAF = 64


def triangular(lower_part, diag_key, lead, order):
    rows = lax.broadcasted_iota(jnp.int32, (order, order), 0)
    columns = lax.broadcasted_iota(jnp.int32, (order, order), 1)
    diagonal = jnp.exp(jax.random.uniform(diag_key, lead + (order,), jnp.float32, -0.5, 0.5))
    below = jnp.where(rows > columns, lower_part / math.sqrt(order), 0.0)
    identity = jnp.where(rows == columns, 1.0, 0.0)
    return (below + diagonal[..., :, None] * identity).astype(jnp.bfloat16)


def draw_leaf_inverse(key, part):
    key = jax.random.fold_in(key, 1)
    first_key, second_key = jax.random.split(key)
    lead = (N_LEAF, CAP)
    lower_part = 0.7 * jax.random.normal(first_key, lead + (S, S), jnp.float32)
    return triangular(lower_part, second_key, lead, S)


def draw_sep_inverse(key, part):
    key = jax.random.fold_in(key, 2)
    first_key, second_key = jax.random.split(key)
    lead = (N_LEAF,)
    lower_part = 0.7 * jax.random.normal(first_key, lead + (P_SIZE, P_SIZE), jnp.float32)
    return triangular(lower_part, second_key, lead, P_SIZE)


def draw_leaf_count(key, part):
    key = jax.random.fold_in(key, 3)
    first_key, second_key = jax.random.split(key)
    drawn_counts = jax.random.randint(first_key, (N_LEAF,), 1, CAP + 1, jnp.int32)
    full_section = jax.random.randint(second_key, (), 0, N_LEAF, jnp.int32)
    return jnp.where(jnp.arange(N_LEAF, dtype=jnp.int32) == full_section, CAP, drawn_counts).astype(jnp.int32)


def levels(stream_key, dims, cuts, low, high):
    loudness = 1.0
    for dim, shards_of in cuts:
        draws = jax.random.uniform(jax.random.fold_in(jax.random.fold_in(stream_key, 6), dim), (shards_of,), jnp.float32, low / len(cuts), high / len(cuts))
        loudness = loudness * jnp.repeat(jnp.exp(draws), dims[dim] // shards_of).reshape((-1,) + (1,) * (len(dims) - 1 - dim))
    return loudness


def normal_values(rng, extent, scale, bound, cuts=(), kind=jnp.bfloat16):
    entries = jax.random.normal(rng, extent, jnp.float32) * scale
    if len(cuts) > 0:
        entries = levels(rng, extent, cuts, -0.22, 0.18) * entries
    return jnp.clip(entries, min=-bound, max=bound).astype(kind)


def setup_inputs(seed: int = 0) -> dict:
    arg_keys = jax.random.split(jax.random.key(seed), 12)
    leaf_rhs = normal_values(arg_keys[0], (N_LEAF, S, CAP, COLS), 1.0, 6.0, ((0, 64), (1, 8)))
    sep_rhs = normal_values(arg_keys[1], (N_LEAF, COLS, P_SIZE), 1.0, 6.0, ((0, 64), (1, 8)))
    leaf_noise = normal_values(arg_keys[2], (N_LEAF, S, CAP, COLS), 1.0, 6.0, ((0, 64), (1, 8)))
    sep_noise = normal_values(arg_keys[3], (N_LEAF, COLS, P_SIZE), 1.0, 6.0, ((0, 64), (1, 8)))
    leaf_inverse = draw_leaf_inverse(jax.random.fold_in(arg_keys[11], 71), 0)
    leaf_left = normal_values(arg_keys[5], (N_LEAF, CAP, S, P_SIZE), (4 * CAP * S) ** -0.5, 0.09375, ((0, 64), (2, 8)))
    leaf_right = normal_values(arg_keys[6], (N_LEAF, CAP, S, P_SIZE), (4 * CAP * S) ** -0.5, 0.09375, ((0, 64), (2, 8)))
    sep_inverse = draw_sep_inverse(jax.random.fold_in(arg_keys[11], 71), 0)
    sep_left = normal_values(arg_keys[8], (N_LEAF, P_SIZE, P_SIZE), (4 * P_SIZE) ** -0.5, 0.109375, ((0, 64),))
    sep_right = normal_values(arg_keys[9], (N_LEAF, P_SIZE, P_SIZE), (4 * P_SIZE) ** -0.5, 0.109375, ((0, 64),))
    leaf_count = draw_leaf_count(jax.random.fold_in(arg_keys[11], 71), 0)
    return dict(leaf_rhs=leaf_rhs, sep_rhs=sep_rhs, leaf_noise=leaf_noise, sep_noise=sep_noise, leaf_inverse=leaf_inverse, leaf_left=leaf_left, leaf_right=leaf_right, sep_inverse=sep_inverse, sep_left=sep_left, sep_right=sep_right, leaf_count=leaf_count)


def rounded(values):
    return lax.optimization_barrier(values.astype(jnp.bfloat16)).astype(jnp.float32)


def reference(leaf_rhs, sep_rhs, leaf_noise, sep_noise, leaf_inverse, leaf_left, leaf_right, sep_inverse, sep_left, sep_right, leaf_count):
    sections = leaf_rhs.shape[0]
    depth_levels = sections.bit_length() - 1
    slot_mask = (jnp.arange(CAP)[None, :] < leaf_count[:, None]).astype(jnp.float32)[:, None, :, None]
    inverse_full = leaf_inverse.astype(jnp.float32)
    left_leaf = leaf_left.astype(jnp.float32)
    right_leaf = leaf_right.astype(jnp.float32)
    solved_leaf = rounded(jnp.einsum("ltrs,lstc->lrtc", inverse_full, leaf_rhs.astype(jnp.float32)) * slot_mask)
    toward_right = jnp.einsum("lstc,ltsp->lcp", solved_leaf, right_leaf)
    toward_left = jnp.einsum("lstc,ltsp->lcp", solved_leaf, left_leaf)
    shifted = jnp.concatenate([toward_left[1:], jnp.zeros_like(toward_left[:1])], axis=0)
    residual = sep_rhs.astype(jnp.float32) - toward_right - shifted
    sep_inv_full = sep_inverse.astype(jnp.float32)
    up_left = sep_left.astype(jnp.float32)
    up_right = sep_right.astype(jnp.float32)
    solved_sep = jnp.zeros(sep_rhs.shape, jnp.float32)
    for height in range(depth_levels + 1):
        owners = np.arange(2 ** height - 1, sections, 2 ** (height + 1))
        candidate = rounded(jnp.einsum("ocq,opq->ocp", rounded(residual[owners]), sep_inv_full[owners]))
        solved_sep = solved_sep.at[owners].set(candidate)
        if height < depth_levels:
            right_owner = owners + 2 ** height
            valid_right = right_owner < sections
            if valid_right.any():
                update = jnp.einsum("ocq,oqp->ocp", candidate[valid_right], up_right[owners[valid_right]])
                residual = residual.at[right_owner[valid_right]].add(-update)
            left_owner = owners - 2 ** height
            valid_left = left_owner >= 0
            if valid_left.any():
                update = jnp.einsum("ocq,oqp->ocp", candidate[valid_left], up_left[owners[valid_left]])
                residual = residual.at[left_owner[valid_left]].add(-update)
    target = solved_sep + sep_noise.astype(jnp.float32)
    draws_sep = jnp.zeros(sep_rhs.shape, jnp.float32)
    for height in range(depth_levels, -1, -1):
        owners = np.arange(2 ** height - 1, sections, 2 ** (height + 1))
        combined = target[owners]
        if height < depth_levels:
            left_owner = owners - 2 ** height
            left_valid = (left_owner >= 0).astype(np.float32)[:, None, None]
            left_values = rounded(draws_sep[np.maximum(left_owner, 0)])
            combined = combined - jnp.einsum("ocq,opq->ocp", left_values, up_left[owners]) * left_valid
            right_owner = owners + 2 ** height
            right_valid = (right_owner < sections).astype(np.float32)[:, None, None]
            right_values = rounded(draws_sep[np.minimum(right_owner, sections - 1)])
            combined = combined - jnp.einsum("ocq,opq->ocp", right_values, up_right[owners]) * right_valid
        draws_sep = draws_sep.at[owners].set(jnp.einsum("ocq,oqp->ocp", rounded(combined), sep_inv_full[owners]))
    sep_round = rounded(draws_sep)
    previous = jnp.concatenate([jnp.zeros_like(sep_round[:1]), sep_round[:-1]], axis=0)
    pulled = jnp.einsum("ltsp,lcp->lstc", right_leaf, sep_round) + jnp.einsum("ltsp,lcp->lstc", left_leaf, previous)
    mixed = rounded((solved_leaf + leaf_noise.astype(jnp.float32) - pulled) * slot_mask)
    draws_leaf = jnp.einsum("ltgs,lgtc->lstc", inverse_full, mixed)
    return draws_leaf, draws_sep
```

```python
import functools

import jax
import jax.numpy as jnp
from jax import lax
from jax.experimental import pallas as pl
from jax.experimental.pallas import tpu as pltpu
from jax.sharding import PartitionSpec as P

MESH = pl.DeviceIdType.MESH
BF = jnp.bfloat16
F32 = jnp.float32
HALF = 64


def nn(a, b):
    return lax.dot_general(a, b, (((1,), (0,)), ((), ())), preferred_element_type=F32)


def nt(a, b):
    return lax.dot_general(a, b, (((1,), (1,)), ((), ())), preferred_element_type=F32)


def tn(a, b):
    return lax.dot_general(a, b, (((0,), (0,)), ((), ())), preferred_element_type=F32)


def pack(block_ref, packed_ref):
    _, rows, samples = block_ref.shape
    for slab in range(samples // 128):
        lanes = slice(slab * 128, slab * 128 + 128)
        a = block_ref[0:2, :, lanes].reshape(2 * rows, 128)
        b = block_ref[2:4, :, lanes].reshape(2 * rows, 128)
        for core in range(2):
            part = slice(core * HALF, core * HALF + HALF)
            both = jnp.concatenate([a[:, part], b[:, part]], axis=1)
            packed_ref[2 * slab + core] = both.reshape(2, rows, 128)


def kernel(
    n_leaf,
    n_front,
    depth,
    cnt_ref,
    rhs_hbm,
    noise_hbm,
    inv_hbm,
    left_hbm,
    right_hbm,
    srhs_hbm,
    snoise_hbm,
    sinv_hbm,
    sleft_hbm,
    sright_hbm,
    leaf_out,
    sep_out,
    x_buf,
    n_buf,
    pk,
    pkn,
    r2,
    n2,
    inv,
    lw,
    srhs,
    snoise,
    sinv,
    su,
    w,
    s2,
    res,
    rb,
    zacc,
    tl_send,
    tl_recv,
    up_send,
    up_recv,
    dn_send,
    dn_recv,
    own_dup,
    prev_dup,
    pull,
    d2,
    o2,
    load_sem,
    a_send,
    a_recv,
    nz_send,
    nz_recv,
    gi_send,
    gi_recv,
    g_send,
    g_recv,
    tl_ssem,
    tl_rsem,
    up_ssem,
    up_rsem,
    dn_ssem,
    dn_rsem,
    o_send,
    o_recv,
):
    leaf = lax.axis_index("leaf")
    front = lax.axis_index("front")
    chips = n_front // 2
    x = front // 2
    core = front % 2
    rows = x_buf.shape[1]
    pos = leaf + 1
    level = jnp.int32(0)
    for bit in range(1, depth + 1):
        level = level + (pos % (1 << bit) == 0).astype(jnp.int32)
    span = jnp.int32(1)
    for bit in range(1, depth + 1):
        span = jnp.where(pos % (1 << bit) == 0, jnp.int32(1 << bit), span)
    odd = leaf % 2
    is_even = odd == 0

    def inside(target):
        return jnp.logical_and(target >= 0, target < n_leaf)

    def load(i, src, dst):
        return pltpu.make_async_copy(src, dst, load_sem.at[i])

    own_rows = pl.ds(pl.multiple_of(front * rows, rows), rows)
    loads = [
        load(0, rhs_hbm, x_buf),
        load(1, inv_hbm, inv.at[:, own_rows, :]),
        load(2, right_hbm, lw.at[0, :, own_rows, :]),
        load(3, left_hbm, lw.at[1, :, own_rows, :]),
        load(4, sinv_hbm, sinv),
        load(5, sleft_hbm, su.at[0]),
        load(6, sright_hbm, su.at[1]),
        load(7, srhs_hbm, srhs),
        load(8, snoise_hbm, snoise),
        load(9, noise_hbm, n_buf),
    ]
    for copy in loads:
        copy.start()

    barrier = pltpu.get_barrier_semaphore()
    partners = jnp.int32(n_front - 1)
    for step in range(1, n_front):
        pl.semaphore_signal(
            barrier, inc=1, device_id={"front": (front + step) % n_front}, device_id_type=MESH
        )
    for h in range(depth + 1):
        for sign in (-1, 1):
            target = leaf + sign * (1 << h)
            reached = jnp.logical_and(h <= level, inside(target))
            partners = partners + reached.astype(jnp.int32)

            @pl.when(reached)
            def _():
                pl.semaphore_signal(
                    barrier, inc=1, device_id={"leaf": target}, device_id_type=MESH
                )

    pl.semaphore_wait(barrier, partners)

    def exchange(src, dst_at, sends, recvs, step):
        peer = (front + step) % n_front
        return pltpu.make_async_remote_copy(
            src_ref=src.at[peer],
            dst_ref=dst_at(front),
            send_sem=sends.at[step - 1],
            recv_sem=recvs.at[step - 1],
            device_id={"front": peer},
            device_id_type=MESH,
        )

    def arrival(src, dst_at, sends, recvs, step):
        peer = (front + n_front - step) % n_front
        return pltpu.make_async_remote_copy(
            src_ref=src.at[peer],
            dst_ref=dst_at(peer),
            send_sem=sends.at[step - 1],
            recv_sem=recvs.at[step - 1],
            device_id={"front": peer},
            device_id_type=MESH,
        )

    def rows_of(ref):
        return lambda f: ref.at[:, pl.ds(pl.multiple_of(f * rows, rows), rows), :]

    def piece(buf, dx, flip, low, high):
        chip = (x + dx + chips) % chips
        who = 2 * chip + (1 - core if flip else core)
        return buf.at[low:high, pl.ds(pl.multiple_of(who * rows, rows), rows), :]

    routes = [
        (0, 0, 4, 1, False),
        (0, 0, 4, -1, False),
        (0, 0, 4, 0, True),
        (-1, 0, 4, 0, True),
        (-1, 0, 2, 1, False),
        (1, 0, 4, 0, True),
        (1, 2, 4, -1, False),
        (2, 0, 2, 0, True),
        (2, 2, 4, 0, True),
    ]

    def route(buf, sends, recvs, i):
        dx, low, high, to, flip = routes[i]
        chip = (x + to + chips) % chips
        peer = 2 * chip + (1 - core if flip else core)
        block = piece(buf, dx, False, low, high)
        return pltpu.make_async_remote_copy(
            src_ref=block,
            dst_ref=block,
            send_sem=sends.at[i],
            recv_sem=recvs.at[i],
            device_id={"front": peer},
            device_id_type=MESH,
        )

    def route_arrival(buf, sends, recvs, i):
        dx, low, high, to, flip = routes[i]
        chip = (x + to + chips) % chips
        peer = 2 * chip + (1 - core if flip else core)
        block = piece(buf, dx - to, flip, low, high)
        return pltpu.make_async_remote_copy(
            src_ref=block,
            dst_ref=block,
            send_sem=sends.at[i],
            recv_sem=recvs.at[i],
            device_id={"front": peer},
            device_id_type=MESH,
        )

    class Gather:
        def __init__(self, buf, sends, recvs):
            self.args = (buf, sends, recvs)

        def send(self, *which):
            for i in which:
                route(*self.args, i).start()

        def take(self, *which):
            for i in which:
                route_arrival(*self.args, i).wait_recv()

        def drain(self):
            for i in range(len(routes)):
                route(*self.args, i).wait_send()

    first = odd
    second = 1 - odd
    gather_inv = Gather(inv, gi_send, gi_recv)
    gather_one = Gather(lw.at[first], g_send.at[0], g_recv.at[0])
    gather_two = Gather(lw.at[second], g_send.at[1], g_recv.at[1])

    loads[0].wait()
    pack(x_buf, pk)
    for step in range(1, n_front):
        exchange(pk, rows_of(r2), a_send, a_recv, step).start()
    loads[1].wait()
    gather_inv.send(0, 1, 2)
    loads[2].wait()
    loads[3].wait()
    gather_one.send(0, 1, 2)
    r2[:, own_rows, :] = pk[front]

    loads[4].wait()
    loads[5].wait()
    w[0] = tn(sinv[...], su[0]).astype(BF)
    gather_inv.take(0)
    gather_inv.send(4, 3)
    gather_inv.take(1)
    gather_inv.send(6, 5)
    loads[6].wait()
    w[1] = tn(sinv[...], su[1]).astype(BF)
    gather_one.take(0)
    gather_one.send(4, 3)
    gather_one.take(1)
    gather_one.send(6, 5)
    gather_inv.take(4)
    gather_inv.send(7)
    gather_inv.take(6)
    gather_inv.send(8)
    gather_two.send(0, 1, 2)
    for step in range(1, n_front):
        arrival(pk, rows_of(r2), a_send, a_recv, step).wait_recv()
    gather_inv.take(2, 3, 5, 7, 8)

    live = cnt_ref[0]
    low_lanes = lax.broadcasted_iota(jnp.int32, (1, 128), 1) < HALF
    alive = [
        jnp.logical_or(
            jnp.logical_and(low_lanes, t < live),
            jnp.logical_and(jnp.logical_not(low_lanes), t + 2 < live),
        )
        for t in range(2)
    ]
    for t in range(2):
        block = r2[t]
        solved = jnp.where(low_lanes, nn(inv[t], block), nn(inv[t + 2], block))
        s2[t] = jnp.where(alive[t], solved, 0.0).astype(BF)

    def toward(side):
        total = jnp.zeros((HALF, srhs.shape[1]), F32)
        for t in range(2):
            turned = s2[t].T
            total = total + nn(turned[0:HALF], lw[side, t])
            total = total + nn(turned[HALF:], lw[side, t + 2])
        return total

    def tl_copy(target):
        return pltpu.make_async_remote_copy(
            src_ref=tl_send,
            dst_ref=tl_recv,
            send_sem=tl_ssem,
            recv_sem=tl_rsem,
            device_id={"leaf": target},
            device_id_type=MESH,
        )

    def up_copy(i, h, target):
        return pltpu.make_async_remote_copy(
            src_ref=up_send.at[i],
            dst_ref=up_recv.at[h, i],
            send_sem=up_ssem.at[i],
            recv_sem=up_rsem.at[h, i],
            device_id={"leaf": target},
            device_id_type=MESH,
        )

    def dn_copy(i, h, target):
        return pltpu.make_async_remote_copy(
            src_ref=dn_send,
            dst_ref=dn_recv.at[i],
            send_sem=dn_ssem.at[i, h],
            recv_sem=dn_rsem.at[i],
            device_id={"leaf": target},
            device_id_type=MESH,
        )

    near = ((pos // span) % 4 == 1).astype(jnp.int32)
    own_level = jnp.minimum(level, depth - 1)

    def ancestor(i):
        return leaf + (2 * i - 1) * span

    def climb():
        rb[...] = res[...].astype(BF)
        for j in range(2):
            i = near if j == 0 else 1 - near
            target = ancestor(i)

            @pl.when(inside(target))
            def _():
                up_send[i] = nn(rb[...], w[i]).astype(BF)
                up_copy(i, own_level, target).start()

    gather_one.take(4)
    gather_one.send(7)
    gather_one.take(6)
    gather_one.send(8)
    gather_one.take(2, 3, 5, 7, 8)
    loads[7].wait()
    part_one = toward(first)

    @pl.when(is_even)
    def _():
        res[...] = srhs[...].astype(F32) - part_one
        tl_copy(leaf + 1).wait_recv()
        res[...] = res[...] - tl_recv[...].astype(F32)
        climb()

    @pl.when(jnp.logical_not(is_even))
    def _():
        tl_send[...] = part_one.astype(BF)
        tl_copy(leaf - 1).start()

    gather_two.take(0)
    gather_two.send(4, 3)
    gather_two.take(1)
    gather_two.send(6, 5)
    gather_two.take(4)
    gather_two.send(7)
    gather_two.take(6)
    gather_two.send(8)
    gather_two.take(2, 3, 5, 7, 8)
    part_two = toward(second)

    @pl.when(jnp.logical_and(is_even, leaf > 0))
    def _():
        tl_send[...] = part_two.astype(BF)
        tl_copy(leaf - 1).start()

    @pl.when(jnp.logical_not(is_even))
    def _():
        res[...] = srhs[...].astype(F32) - part_two

        @pl.when(leaf < n_leaf - 1)
        def _():
            tl_copy(leaf + 1).wait_recv()
            res[...] = res[...] - tl_recv[...].astype(F32)

        @pl.loop(0, level)
        def _(h):
            below = lax.shift_left(jnp.int32(1), h.astype(jnp.int32))
            for i in range(2):
                source = leaf + (1 - 2 * i) * below

                @pl.when(inside(source))
                def _():
                    up_copy(i, h, source).wait_recv()
                    res[...] = res[...] - up_recv[h, i].astype(F32)

        climb()

    loads[8].wait()
    solved_sep = nt(rb[...], sinv[...]).astype(BF).astype(F32)
    target_sep = (solved_sep + snoise[...].astype(F32)).astype(BF)
    zacc[...] = nn(target_sep, sinv[...])

    loads[9].wait()
    pack(n_buf, pkn)
    for step in range(1, n_front):
        exchange(pkn, rows_of(n2), nz_send, nz_recv, step).start()
    n2[:, own_rows, :] = pkn[front]

    for j in range(2):
        i = 1 - near if j == 0 else near
        source = ancestor(i)

        @pl.when(inside(source))
        def _():
            dn_copy(i, 0, source).wait_recv()
            zacc[...] = zacc[...] - nt(dn_recv[i], w[i])

    draws = zacc[...]
    sep_out[...] = draws
    dn_send[...] = draws.astype(BF)

    @pl.loop(0, level)
    def _(step):
        h = level - 1 - step
        below = lax.shift_left(jnp.int32(1), h.astype(jnp.int32))
        for i in range(2):
            target = leaf + (1 - 2 * i) * below

            @pl.when(inside(target))
            def _():
                dn_copy(i, h, target).start()

        for i in range(2):
            target = leaf + (1 - 2 * i) * below

            @pl.when(inside(target))
            def _():
                dn_copy(i, h, target).wait_send()

    @pl.when(is_even)
    def _():
        dn_copy(2, 0, leaf + 1).start()

    own_dup[0:HALF] = dn_send[...]
    own_dup[HALF:] = dn_send[...]

    def pulled(side, dup):
        return [
            jnp.where(low_lanes, nt(lw[side, t], dup), nt(lw[side, t + 2], dup)) for t in range(2)
        ]

    for t, value in enumerate(pulled(0, own_dup[...])):
        pull[t] = value
    for step in range(1, n_front):
        arrival(pkn, rows_of(n2), nz_send, nz_recv, step).wait_recv()

    @pl.when(jnp.logical_not(is_even))
    def _():
        dn_copy(2, 0, leaf - 1).wait_recv()
        prev_dup[0:HALF] = dn_recv[2]

    @pl.when(jnp.logical_and(is_even, leaf > 0))
    def _():
        prev_dup[0:HALF] = dn_recv[0]

    @pl.when(leaf == 0)
    def _():
        prev_dup[0:HALF] = jnp.zeros((HALF, prev_dup.shape[1]), BF)

    prev_dup[HALF:] = prev_dup[0:HALF]
    for t, value in enumerate(pulled(1, prev_dup[...])):
        mixed = s2[t].astype(F32) + n2[t].astype(F32) - pull[t] - value
        mixed = jnp.where(alive[t], mixed, 0.0).astype(BF)
        drawn = jnp.where(low_lanes, tn(inv[t], mixed), tn(inv[t + 2], mixed)).astype(BF)
        for f in range(n_front):
            d2[f, t] = drawn[f * rows : f * rows + rows]

    for step in range(1, n_front):
        exchange(d2, lambda f: o2.at[f], o_send, o_recv, step).start()
    o2[front] = d2[front]
    for step in range(1, n_front):
        arrival(d2, lambda f: o2.at[f], o_send, o_recv, step).wait_recv()

    for t in range(2):
        for slab in range(n_front // 2):
            lanes = slice(slab * 128, slab * 128 + 128)
            a = o2[2 * slab, t]
            b = o2[2 * slab + 1, t]
            leaf_out[t, :, lanes] = jnp.concatenate([a[:, :HALF], b[:, :HALF]], axis=1)
            leaf_out[t + 2, :, lanes] = jnp.concatenate([a[:, HALF:], b[:, HALF:]], axis=1)

    for step in range(1, n_front):
        exchange(pk, rows_of(r2), a_send, a_recv, step).wait_send()
        exchange(pkn, rows_of(n2), nz_send, nz_recv, step).wait_send()
        exchange(d2, lambda f: o2.at[f], o_send, o_recv, step).wait_send()
    gather_inv.drain()
    gather_one.drain()
    gather_two.drain()

    @pl.when(leaf > 0)
    def _():
        tl_copy(leaf - 1).wait_send()

    for i in range(2):
        target = ancestor(i)

        @pl.when(inside(target))
        def _():
            up_copy(i, own_level, target).wait_send()

    @pl.when(is_even)
    def _():
        dn_copy(2, 0, leaf + 1).wait_send()


def on_device(
    leaf_rhs,
    sep_rhs,
    leaf_noise,
    sep_noise,
    leaf_inverse,
    leaf_left,
    leaf_right,
    sep_inverse,
    sep_left,
    sep_right,
    leaf_count,
):
    n_leaf = lax.axis_size("leaf")
    n_front = lax.axis_size("front")
    depth = n_leaf.bit_length() - 1
    _, rows, slots, samples = leaf_rhs.shape
    share, width = sep_rhs.shape[1:]
    order = rows * n_front
    rhs = jnp.transpose(leaf_rhs[0], (1, 0, 2))
    noise = jnp.transpose(leaf_noise[0], (1, 0, 2))
    hbm = pl.BlockSpec(memory_space=pltpu.HBM)
    vmem = pl.BlockSpec(memory_space=pltpu.VMEM)
    dma = pltpu.SemaphoreType.DMA
    leaf_draws, sep_draws = pl.pallas_call(
        functools.partial(kernel, n_leaf, n_front, depth),
        out_shape=(
            jax.ShapeDtypeStruct((slots, rows, samples), BF),
            jax.ShapeDtypeStruct((share, width), F32),
        ),
        in_specs=[pl.BlockSpec(memory_space=pltpu.SMEM)] + [hbm] * 10,
        out_specs=(vmem, vmem),
        scratch_shapes=[
            pltpu.VMEM((slots, rows, samples), BF),
            pltpu.VMEM((slots, rows, samples), BF),
            pltpu.VMEM((n_front, 2, rows, 128), BF),
            pltpu.VMEM((n_front, 2, rows, 128), BF),
            pltpu.VMEM((2, order, 128), BF),
            pltpu.VMEM((2, order, 128), BF),
            pltpu.VMEM((slots, order, order), BF),
            pltpu.VMEM((2, slots, order, width), BF),
            pltpu.VMEM((share, width), BF),
            pltpu.VMEM((share, width), BF),
            pltpu.VMEM((width, width), BF),
            pltpu.VMEM((2, width, width), BF),
            pltpu.VMEM((2, width, width), BF),
            pltpu.VMEM((2, order, 128), BF),
            pltpu.VMEM((share, width), F32),
            pltpu.VMEM((share, width), BF),
            pltpu.VMEM((share, width), F32),
            pltpu.VMEM((share, width), BF),
            pltpu.VMEM((share, width), BF),
            pltpu.VMEM((2, share, width), BF),
            pltpu.VMEM((depth, 2, share, width), BF),
            pltpu.VMEM((share, width), BF),
            pltpu.VMEM((3, share, width), BF),
            pltpu.VMEM((2 * share, width), BF),
            pltpu.VMEM((2 * share, width), BF),
            pltpu.VMEM((2, order, 128), F32),
            pltpu.VMEM((n_front, 2, rows, 128), BF),
            pltpu.VMEM((n_front, 2, rows, 128), BF),
            dma((10,)),
            dma((n_front - 1,)),
            dma((n_front - 1,)),
            dma((n_front - 1,)),
            dma((n_front - 1,)),
            dma((9,)),
            dma((9,)),
            dma((2, 9)),
            dma((2, 9)),
            dma,
            dma,
            dma((2,)),
            dma((depth, 2)),
            dma((3, depth)),
            dma((3,)),
            dma((n_front - 1,)),
            dma((n_front - 1,)),
        ],
        compiler_params=pltpu.CompilerParams(
            collective_id=0, has_side_effects=True, vmem_limit_bytes=40 * 1024 * 1024
        ),
    )(
        leaf_count,
        rhs,
        noise,
        leaf_inverse[0],
        leaf_left[0],
        leaf_right[0],
        sep_rhs[0],
        sep_noise[0],
        sep_inverse[0],
        sep_left[0],
        sep_right[0],
    )
    leaf_draws = jnp.transpose(leaf_draws, (1, 0, 2)).astype(F32)
    return (leaf_draws[None], sep_draws[None])


def solution(mesh):
    return jax.shard_map(
        on_device,
        mesh=mesh,
        in_specs=(
            P("leaf", "front", None, None),
            P("leaf", "front", None),
            P("leaf", "front", None, None),
            P("leaf", "front", None),
            P("leaf", None, "front", None),
            P("leaf", None, "front", None),
            P("leaf", None, "front", None),
            P("leaf", None, None),
            P("leaf", None, None),
            P("leaf", None, None),
            P("leaf"),
        ),
        out_specs=(P("leaf", "front", None, None), P("leaf", "front", None)),
        check_vma=False,
    )
```

```python
import functools

import jax
import jax.numpy as jnp
from jax import lax
from jax.experimental import pallas as pl
from jax.experimental.pallas import tpu as pltpu
from jax.sharding import PartitionSpec as P

MESH = pl.DeviceIdType.MESH
BF = jnp.bfloat16
F32 = jnp.float32
HALF = 64
SKIPPED = (3, 5)


def nn(a, b):
    return lax.dot_general(a, b, (((1,), (0,)), ((), ())), preferred_element_type=F32)


def nt(a, b):
    return lax.dot_general(a, b, (((1,), (1,)), ((), ())), preferred_element_type=F32)


def tn(a, b):
    return lax.dot_general(a, b, (((0,), (0,)), ((), ())), preferred_element_type=F32)


def pack(block_ref, packed_ref):
    _, rows, samples = block_ref.shape
    for slab in range(samples // 128):
        lanes = slice(slab * 128, slab * 128 + 128)
        a = block_ref[0:2, :, lanes].reshape(2 * rows, 128)
        b = block_ref[2:4, :, lanes].reshape(2 * rows, 128)
        for core in range(2):
            part = slice(core * HALF, core * HALF + HALF)
            both = jnp.concatenate([a[:, part], b[:, part]], axis=1)
            packed_ref[2 * slab + core] = both.reshape(2, rows, 128)


def kernel(
    n_leaf,
    n_front,
    depth,
    cnt_ref,
    rhs_hbm,
    noise_hbm,
    inv_hbm,
    left_hbm,
    right_hbm,
    srhs_hbm,
    snoise_hbm,
    sinv_hbm,
    sleft_hbm,
    sright_hbm,
    leaf_out,
    sep_out,
    x_buf,
    n_buf,
    pk,
    pkn,
    r2,
    n2,
    inv,
    lw,
    srhs,
    snoise,
    sinv,
    su,
    wall,
    wa,
    s2,
    res,
    rb,
    zacc,
    tl_send,
    tl_recv,
    up_send,
    up_recv,
    dn_send,
    dn_recv,
    zp_send,
    zp_recv,
    own_dup,
    prev_dup,
    pull,
    d2,
    o2,
    load_sem,
    a_send,
    a_recv,
    nz_send,
    nz_recv,
    gi_send,
    gi_recv,
    g_send,
    g_recv,
    tl_ssem,
    tl_rsem,
    up_ssem,
    up_rsem,
    dn_ssem,
    dn_rsem,
    o_send,
    o_recv,
    wa_ssem,
    wa_rsem,
    cx_ssem,
    cx_rsem,
    zp_ssem,
    zp_rsem,
    known_sem,
):
    leaf = lax.axis_index("leaf")
    front = lax.axis_index("front")
    chips = n_front // 2
    x = front // 2
    core = front % 2
    rows = x_buf.shape[1]
    pos = leaf + 1
    level = jnp.int32(0)
    for bit in range(1, depth + 1):
        level = level + (pos % (1 << bit) == 0).astype(jnp.int32)
    span = jnp.int32(1)
    for bit in range(1, depth + 1):
        span = jnp.where(pos % (1 << bit) == 0, jnp.int32(1 << bit), span)
    odd = leaf % 2
    is_even = odd == 0

    def inside(target):
        return jnp.logical_and(target >= 0, target < n_leaf)

    def any_of(value, levels):
        found = jnp.bool_(False)
        for one in levels:
            found = jnp.logical_or(found, value == one)
        return found

    skipped = tuple(one for one in SKIPPED if one < depth)
    is_skipped = any_of(level, skipped)
    is_joined = any_of(level + 1, skipped)
    joined = is_joined.astype(jnp.int32)
    near = ((pos // span) % 4 == 1).astype(jnp.int32)
    parent = leaf + (2 * near - 1) * span
    parent_near = (((parent + 1) // (2 * span)) % 4 == 1).astype(jnp.int32)
    first_side = jnp.where(is_joined, parent_near, near)
    own_level = jnp.minimum(level, depth - 1)
    half_span = jnp.maximum(span // 2, 1)

    def ancestor(i):
        reach = jnp.where(jnp.logical_and(is_joined, near == i), 3, 1)
        return leaf + (2 * i - 1) * reach * span


    def load(i, src, dst):
        return pltpu.make_async_copy(src, dst, load_sem.at[i])

    own_rows = pl.ds(pl.multiple_of(front * rows, rows), rows)
    loads = [
        load(0, rhs_hbm, x_buf),
        load(1, inv_hbm, inv.at[:, own_rows, :]),
        load(2, right_hbm, lw.at[0, :, own_rows, :]),
        load(3, left_hbm, lw.at[1, :, own_rows, :]),
        load(4, sinv_hbm, sinv),
        load(5, sleft_hbm, su.at[0]),
        load(6, sright_hbm, su.at[1]),
        load(7, srhs_hbm, srhs),
        load(8, snoise_hbm, snoise),
        load(9, noise_hbm, n_buf),
    ]
    for copy in loads:
        copy.start()

    barrier = pltpu.get_barrier_semaphore()
    partners = jnp.int32(n_front - 1)
    for step in range(1, n_front):
        pl.semaphore_signal(
            barrier, inc=1, device_id={"front": (front + step) % n_front}, device_id_type=MESH
        )
    greeted = [(leaf - 1, leaf > 0), (leaf + 1, leaf < n_leaf - 1)]
    if skipped:
        greeted += [
            (parent, is_joined),
            (leaf - half_span, is_skipped),
            (leaf + half_span, is_skipped),
            (ancestor(0), jnp.logical_and(is_joined, inside(ancestor(0)))),
            (ancestor(1), jnp.logical_and(is_joined, inside(ancestor(1)))),
        ]
        for one in skipped:
            for reach in (-3 << (one - 1), -1 << (one - 1), 1 << (one - 1), 3 << (one - 1)):
                greeted.append(
                    (leaf + reach, jnp.logical_and(level > one, inside(leaf + reach)))
                )
    for target, reached in greeted:
        partners = partners + reached.astype(jnp.int32)

        @pl.when(reached)
        def _():
            pl.semaphore_signal(barrier, inc=1, device_id={"leaf": target}, device_id_type=MESH)

    loads[0].wait()
    pack(x_buf, pk)
    loads[4].wait()
    loads[5].wait()
    wall[0] = tn(sinv[...], su[0]).astype(BF)
    pl.semaphore_wait(barrier, partners)

    width = srhs.shape[1]
    cols = pl.ds(pl.multiple_of(core * (width // 2), 128), width // 2)

    def wa_copy(i, target):
        return pltpu.make_async_remote_copy(
            src_ref=wall.at[0:2, :, cols],
            dst_ref=wa.at[:, :, cols],
            send_sem=wa_ssem.at[i],
            recv_sem=wa_rsem,
            device_id={"leaf": target},
            device_id_type=MESH,
        )

    def cx_copy(which):
        half = pl.ds(pl.multiple_of(which * (width // 2), 128), width // 2)
        return pltpu.make_async_remote_copy(
            src_ref=wall.at[2:4, :, half],
            dst_ref=wall.at[2:4, :, half],
            send_sem=cx_ssem,
            recv_sem=cx_rsem,
            device_id={"front": 2 * x + 1 - core},
            device_id_type=MESH,
        )

    if skipped:

        @pl.when(is_joined)
        def _():
            pl.semaphore_signal(known_sem, inc=1, device_id={"leaf": parent}, device_id_type=MESH)

    def exchange(src, dst_at, sends, recvs, step):
        peer = (front + step) % n_front
        return pltpu.make_async_remote_copy(
            src_ref=src.at[peer],
            dst_ref=dst_at(front),
            send_sem=sends.at[step - 1],
            recv_sem=recvs.at[step - 1],
            device_id={"front": peer},
            device_id_type=MESH,
        )

    def arrival(src, dst_at, sends, recvs, step):
        peer = (front + n_front - step) % n_front
        return pltpu.make_async_remote_copy(
            src_ref=src.at[peer],
            dst_ref=dst_at(peer),
            send_sem=sends.at[step - 1],
            recv_sem=recvs.at[step - 1],
            device_id={"front": peer},
            device_id_type=MESH,
        )

    def rows_of(ref):
        return lambda f: ref.at[:, pl.ds(pl.multiple_of(f * rows, rows), rows), :]

    def piece(buf, dx, flip, low, high):
        chip = (x + dx + chips) % chips
        who = 2 * chip + (1 - core if flip else core)
        return buf.at[low:high, pl.ds(pl.multiple_of(who * rows, rows), rows), :]

    routes = [
        (0, 0, 4, 1, False),
        (0, 0, 4, -1, False),
        (0, 0, 4, 0, True),
        (-1, 0, 4, 0, True),
        (-1, 0, 2, 1, False),
        (1, 0, 4, 0, True),
        (1, 2, 4, -1, False),
        (2, 0, 2, 0, True),
        (2, 2, 4, 0, True),
    ]

    def route(buf, sends, recvs, i):
        dx, low, high, to, flip = routes[i]
        chip = (x + to + chips) % chips
        peer = 2 * chip + (1 - core if flip else core)
        block = piece(buf, dx, False, low, high)
        return pltpu.make_async_remote_copy(
            src_ref=block,
            dst_ref=block,
            send_sem=sends.at[i],
            recv_sem=recvs.at[i],
            device_id={"front": peer},
            device_id_type=MESH,
        )

    def route_arrival(buf, sends, recvs, i):
        dx, low, high, to, flip = routes[i]
        chip = (x + to + chips) % chips
        peer = 2 * chip + (1 - core if flip else core)
        block = piece(buf, dx - to, flip, low, high)
        return pltpu.make_async_remote_copy(
            src_ref=block,
            dst_ref=block,
            send_sem=sends.at[i],
            recv_sem=recvs.at[i],
            device_id={"front": peer},
            device_id_type=MESH,
        )

    class Gather:
        def __init__(self, buf, sends, recvs):
            self.args = (buf, sends, recvs)

        def send(self, *which):
            for i in which:
                route(*self.args, i).start()

        def take(self, *which):
            for i in which:
                route_arrival(*self.args, i).wait_recv()

        def drain(self):
            for i in range(len(routes)):
                route(*self.args, i).wait_send()

    first = odd
    second = 1 - odd
    gather_inv = Gather(inv, gi_send, gi_recv)
    gather_one = Gather(lw.at[first], g_send.at[0], g_recv.at[0])
    gather_two = Gather(lw.at[second], g_send.at[1], g_recv.at[1])

    for step in range(1, n_front):
        exchange(pk, rows_of(r2), a_send, a_recv, step).start()
    loads[1].wait()
    gather_inv.send(0, 1, 2)
    loads[2].wait()
    loads[3].wait()
    gather_one.send(0, 1, 2)
    r2[:, own_rows, :] = pk[front]

    loads[6].wait()
    wall[1] = tn(sinv[...], su[1]).astype(BF)
    if skipped:

        @pl.when(is_skipped)
        def _():
            for i in range(2):
                wa_copy(i, leaf + (1 - 2 * i) * half_span).start()

    gather_inv.take(0)
    gather_inv.send(4, 3)
    gather_inv.take(1)
    gather_inv.send(6, 5)
    gather_one.take(0)
    gather_one.send(4, 3)
    gather_one.take(1)
    gather_one.send(6, 5)
    gather_inv.take(4)
    gather_inv.send(7)
    gather_inv.take(6)
    gather_inv.send(8)
    gather_two.send(0, 1, 2)
    for step in range(1, n_front):
        arrival(pk, rows_of(r2), a_send, a_recv, step).wait_recv()
    gather_inv.take(2, 3, 5, 7, 8)

    live = cnt_ref[0]
    low_lanes = lax.broadcasted_iota(jnp.int32, (1, 128), 1) < HALF
    alive = [
        jnp.logical_or(
            jnp.logical_and(low_lanes, t < live),
            jnp.logical_and(jnp.logical_not(low_lanes), t + 2 < live),
        )
        for t in range(2)
    ]
    for t in range(2):
        block = r2[t]
        solved = jnp.where(low_lanes, nn(inv[t], block), nn(inv[t + 2], block))
        s2[t] = jnp.where(alive[t], solved, 0.0).astype(BF)

    def toward(side):
        total = jnp.zeros((HALF, srhs.shape[1]), F32)
        for t in range(2):
            turned = s2[t].T
            total = total + nn(turned[0:HALF], lw[side, t])
            total = total + nn(turned[HALF:], lw[side, t + 2])
        return total

    def tl_copy(target):
        return pltpu.make_async_remote_copy(
            src_ref=tl_send,
            dst_ref=tl_recv,
            send_sem=tl_ssem,
            recv_sem=tl_rsem,
            device_id={"leaf": target},
            device_id_type=MESH,
        )

    chunks = [(0, 256), (256, width)] if width > 256 else [(0, width)]

    class Message:
        def __init__(self, src, dst, sends, recvs, target):
            self.parts = [
                pltpu.make_async_remote_copy(
                    src_ref=src.at[:, low:high],
                    dst_ref=dst.at[:, low:high],
                    send_sem=sends.at[n],
                    recv_sem=recvs.at[n],
                    device_id={"leaf": target},
                    device_id_type=MESH,
                )
                for n, (low, high) in enumerate(chunks)
            ]

        def start(self):
            for part in self.parts:
                part.start()

        def wait_send(self):
            for part in self.parts:
                part.wait_send()

        def wait_recv(self):
            for part in self.parts:
                part.wait_recv()

    def up_message(buffer, i, far, h, target):
        return Message(
            up_send.at[buffer],
            up_recv.at[far, h, i],
            up_ssem.at[buffer],
            up_rsem.at[far, h, i],
            target,
        )

    def dn_message(i, far, h, target):
        return Message(dn_send, dn_recv.at[i], dn_ssem.at[far, i, h], dn_rsem.at[i], target)

    def zp_message(i, target):
        return Message(zp_send, zp_recv, zp_ssem.at[i], zp_rsem, target)

    def post(buffer, matrix, message):
        for n, (low, high) in enumerate(chunks):
            up_send[buffer, :, low:high] = nn(rb[...], wall[matrix, :, low:high]).astype(BF)
            message.parts[n].start()

    def far_of(i):
        return jnp.logical_and(is_joined, near == i).astype(jnp.int32)

    def climb():
        rb[...] = res[...].astype(BF)
        for j in range(2):
            i = first_side if j == 0 else 1 - first_side
            target = ancestor(i)

            @pl.when(inside(target))
            def _():
                post(i, i + 2 * joined, up_message(i, i, far_of(i), own_level, target))

    def gather_level(h):
        below = lax.shift_left(jnp.int32(1), jnp.int32(h))
        ahead = any_of(jnp.int32(h) + 1, skipped)
        for i in range(2):
            source = leaf + (1 - 2 * i) * below

            @pl.when(inside(source))
            def _():
                up_message(i, i, 0, h, source).wait_recv()
                res[...] = res[...] - up_recv[0, h, i].astype(F32)

            if skipped:
                source3 = leaf + (1 - 2 * i) * 3 * below

                @pl.when(
                    jnp.logical_and(jnp.logical_and(ahead, level > h + 1), inside(source3))
                )
                def _():
                    up_message(i, i, 1, h, source3).wait_recv()
                    res[...] = res[...] - up_recv[1, h, i].astype(F32)

    gather_one.take(4)
    gather_one.send(7)
    gather_one.take(6)
    gather_one.send(8)
    gather_one.take(2, 3, 5, 7, 8)
    loads[7].wait()
    part_one = toward(first)

    @pl.when(jnp.logical_not(is_even))
    def _():
        tl_send[...] = part_one.astype(BF)
        tl_copy(leaf - 1).start()

    gather_two.take(0)
    gather_two.send(4, 3)
    gather_two.take(1)
    gather_two.send(6, 5)

    @pl.when(is_even)
    def _():
        res[...] = srhs[...].astype(F32) - part_one
        tl_copy(leaf + 1).wait_recv()
        res[...] = res[...] - tl_recv[...].astype(F32)
        climb()

    gather_two.take(4)
    gather_two.send(7)
    gather_two.take(6)
    gather_two.send(8)
    gather_two.take(2, 3, 5, 7, 8)
    part_two = toward(second)

    @pl.when(jnp.logical_and(is_even, leaf > 0))
    def _():
        tl_send[...] = part_two.astype(BF)
        tl_copy(leaf - 1).start()

    @pl.when(jnp.logical_not(is_even))
    def _():
        res[...] = srhs[...].astype(F32) - part_two

        @pl.when(leaf < n_leaf - 1)
        def _():
            tl_copy(leaf + 1).wait_recv()
            res[...] = res[...] - tl_recv[...].astype(F32)

        if skipped:

            @pl.when(is_joined)
            def _():
                wa_copy(0, parent).wait_recv()
                turn = wall[near]
                wall[2 + near, :, cols] = (-nn(turn, wa[near, :, cols])).astype(BF)
                wall[3 - near, :, cols] = (
                    wall[1 - near, :, cols].astype(F32) - nn(turn, wa[1 - near, :, cols])
                ).astype(BF)
                cx_copy(core).start()
                cx_copy(1 - core).wait_recv()

        @pl.loop(0, level - is_skipped.astype(jnp.int32))
        def _(h):
            gather_level(h)

        if skipped:

            @pl.when(is_skipped)
            def _():
                pl.semaphore_wait(known_sem, 2)

        climb()
        if skipped:

            @pl.when(is_joined)
            def _():
                post(2, near, up_message(2, near, 0, own_level, parent))

            @pl.when(is_skipped)
            def _():
                gather_level(level - 1)
                rb[...] = res[...].astype(BF)

    loads[8].wait()
    solved_sep = nt(rb[...], sinv[...]).astype(BF).astype(F32)
    target_sep = (solved_sep + snoise[...].astype(F32)).astype(BF)
    zacc[...] = nn(target_sep, sinv[...])
    if skipped:

        @pl.when(is_skipped)
        def _():
            zp_send[...] = zacc[...].astype(BF)
            for i in range(2):
                zp_message(i, leaf + (1 - 2 * i) * half_span).start()

    loads[9].wait()
    pack(n_buf, pkn)
    for step in range(1, n_front):
        exchange(pkn, rows_of(n2), nz_send, nz_recv, step).start()
    n2[:, own_rows, :] = pkn[front]

    if skipped:

        @pl.when(is_joined)
        def _():
            zp_message(0, parent).wait_recv()
            zacc[...] = zacc[...] - nt(zp_recv[...], wall[near])

    for j in range(2):
        i = 1 - first_side if j == 0 else first_side
        source = ancestor(i)

        @pl.when(inside(source))
        def _():
            dn_message(i, 0, 0, source).wait_recv()
            zacc[...] = zacc[...] - nt(dn_recv[i], wall[i + 2 * joined])

    draws = zacc[...]
    sep_out[...] = draws
    dn_send[...] = draws.astype(BF)

    def for_level(h, act):
        below = lax.shift_left(jnp.int32(1), jnp.int32(h))
        ahead = any_of(jnp.int32(h) + 1, skipped)
        for i in range(2):
            target = leaf + (1 - 2 * i) * below
            target3 = leaf + (1 - 2 * i) * 3 * below
            passed = jnp.logical_and(ahead, level == h + 1)

            @pl.when(jnp.logical_and(jnp.logical_not(passed), inside(target)))
            def _():
                act(dn_message(i, 0, h, target))

            if skipped:

                @pl.when(
                    jnp.logical_and(jnp.logical_and(ahead, level > h + 1), inside(target3))
                )
                def _():
                    act(dn_message(i, 1, h, target3))

    @pl.loop(0, level)
    def _(step):
        for_level(level - 1 - step, lambda message: message.start())
        for_level(level - 1 - step, lambda message: message.wait_send())

    @pl.when(is_even)
    def _():
        dn_message(2, 0, 0, leaf + 1).start()

    own_dup[0:HALF] = dn_send[...]
    own_dup[HALF:] = dn_send[...]

    def pulled(side, dup):
        return [
            jnp.where(low_lanes, nt(lw[side, t], dup), nt(lw[side, t + 2], dup)) for t in range(2)
        ]

    for t, value in enumerate(pulled(0, own_dup[...])):
        pull[t] = value
    for step in range(1, n_front):
        arrival(pkn, rows_of(n2), nz_send, nz_recv, step).wait_recv()

    @pl.when(jnp.logical_not(is_even))
    def _():
        dn_message(2, 0, 0, leaf - 1).wait_recv()
        prev_dup[0:HALF] = dn_recv[2]

    @pl.when(jnp.logical_and(is_even, leaf > 0))
    def _():
        prev_dup[0:HALF] = dn_recv[0]

    @pl.when(leaf == 0)
    def _():
        prev_dup[0:HALF] = jnp.zeros((HALF, prev_dup.shape[1]), BF)

    prev_dup[HALF:] = prev_dup[0:HALF]
    for t, value in enumerate(pulled(1, prev_dup[...])):
        mixed = s2[t].astype(F32) + n2[t].astype(F32) - pull[t] - value
        mixed = jnp.where(alive[t], mixed, 0.0).astype(BF)
        drawn = jnp.where(low_lanes, tn(inv[t], mixed), tn(inv[t + 2], mixed)).astype(BF)
        for f in range(n_front):
            d2[f, t] = drawn[f * rows : f * rows + rows]

    for step in range(1, n_front):
        exchange(d2, lambda f: o2.at[f], o_send, o_recv, step).start()
    o2[front] = d2[front]
    for step in range(1, n_front):
        arrival(d2, lambda f: o2.at[f], o_send, o_recv, step).wait_recv()

    for t in range(2):
        for slab in range(n_front // 2):
            lanes = slice(slab * 128, slab * 128 + 128)
            a = o2[2 * slab, t]
            b = o2[2 * slab + 1, t]
            leaf_out[t, :, lanes] = jnp.concatenate([a[:, :HALF], b[:, :HALF]], axis=1)
            leaf_out[t + 2, :, lanes] = jnp.concatenate([a[:, HALF:], b[:, HALF:]], axis=1)

    for step in range(1, n_front):
        exchange(pk, rows_of(r2), a_send, a_recv, step).wait_send()
        exchange(pkn, rows_of(n2), nz_send, nz_recv, step).wait_send()
        exchange(d2, lambda f: o2.at[f], o_send, o_recv, step).wait_send()
    gather_inv.drain()
    gather_one.drain()
    gather_two.drain()

    @pl.when(leaf > 0)
    def _():
        tl_copy(leaf - 1).wait_send()

    for i in range(2):
        target = ancestor(i)

        @pl.when(inside(target))
        def _():
            up_message(i, i, far_of(i), own_level, target).wait_send()

    @pl.when(is_even)
    def _():
        dn_message(2, 0, 0, leaf + 1).wait_send()

    if skipped:

        @pl.when(is_joined)
        def _():
            up_message(2, near, 0, own_level, parent).wait_send()
            cx_copy(core).wait_send()

        @pl.when(is_skipped)
        def _():
            for i in range(2):
                child = leaf + (1 - 2 * i) * half_span
                wa_copy(i, child).wait_send()
                zp_message(i, child).wait_send()


def on_device(
    leaf_rhs,
    sep_rhs,
    leaf_noise,
    sep_noise,
    leaf_inverse,
    leaf_left,
    leaf_right,
    sep_inverse,
    sep_left,
    sep_right,
    leaf_count,
):
    n_leaf = lax.axis_size("leaf")
    n_front = lax.axis_size("front")
    depth = n_leaf.bit_length() - 1
    _, rows, slots, samples = leaf_rhs.shape
    share, width = sep_rhs.shape[1:]
    order = rows * n_front
    rhs = jnp.transpose(leaf_rhs[0], (1, 0, 2))
    noise = jnp.transpose(leaf_noise[0], (1, 0, 2))
    hbm = pl.BlockSpec(memory_space=pltpu.HBM)
    vmem = pl.BlockSpec(memory_space=pltpu.VMEM)
    dma = pltpu.SemaphoreType.DMA
    leaf_draws, sep_draws = pl.pallas_call(
        functools.partial(kernel, n_leaf, n_front, depth),
        out_shape=(
            jax.ShapeDtypeStruct((slots, rows, samples), BF),
            jax.ShapeDtypeStruct((share, width), F32),
        ),
        in_specs=[pl.BlockSpec(memory_space=pltpu.SMEM)] + [hbm] * 10,
        out_specs=(vmem, vmem),
        scratch_shapes=[
            pltpu.VMEM((slots, rows, samples), BF),
            pltpu.VMEM((slots, rows, samples), BF),
            pltpu.VMEM((n_front, 2, rows, 128), BF),
            pltpu.VMEM((n_front, 2, rows, 128), BF),
            pltpu.VMEM((2, order, 128), BF),
            pltpu.VMEM((2, order, 128), BF),
            pltpu.VMEM((slots, order, order), BF),
            pltpu.VMEM((2, slots, order, width), BF),
            pltpu.VMEM((share, width), BF),
            pltpu.VMEM((share, width), BF),
            pltpu.VMEM((width, width), BF),
            pltpu.VMEM((2, width, width), BF),
            pltpu.VMEM((4, width, width), BF),
            pltpu.VMEM((2, width, width), BF),
            pltpu.VMEM((2, order, 128), BF),
            pltpu.VMEM((share, width), F32),
            pltpu.VMEM((share, width), BF),
            pltpu.VMEM((share, width), F32),
            pltpu.VMEM((share, width), BF),
            pltpu.VMEM((share, width), BF),
            pltpu.VMEM((3, share, width), BF),
            pltpu.VMEM((2, depth, 2, share, width), BF),
            pltpu.VMEM((share, width), BF),
            pltpu.VMEM((3, share, width), BF),
            pltpu.VMEM((share, width), BF),
            pltpu.VMEM((share, width), BF),
            pltpu.VMEM((2 * share, width), BF),
            pltpu.VMEM((2 * share, width), BF),
            pltpu.VMEM((2, order, 128), F32),
            pltpu.VMEM((n_front, 2, rows, 128), BF),
            pltpu.VMEM((n_front, 2, rows, 128), BF),
            dma((10,)),
            dma((n_front - 1,)),
            dma((n_front - 1,)),
            dma((n_front - 1,)),
            dma((n_front - 1,)),
            dma((9,)),
            dma((9,)),
            dma((2, 9)),
            dma((2, 9)),
            dma,
            dma,
            dma((3, 2)),
            dma((2, depth, 2, 2)),
            dma((2, 3, depth, 2)),
            dma((3, 2)),
            dma((n_front - 1,)),
            dma((n_front - 1,)),
            dma((2,)),
            dma,
            dma,
            dma,
            dma((2, 2)),
            dma((2,)),
            pltpu.SemaphoreType.REGULAR,
        ],
        compiler_params=pltpu.CompilerParams(
            collective_id=0, has_side_effects=True, vmem_limit_bytes=63 * 1024 * 1024
        ),
    )(
        leaf_count,
        rhs,
        noise,
        leaf_inverse[0],
        leaf_left[0],
        leaf_right[0],
        sep_rhs[0],
        sep_noise[0],
        sep_inverse[0],
        sep_left[0],
        sep_right[0],
    )
    leaf_draws = jnp.transpose(leaf_draws, (1, 0, 2)).astype(F32)
    return (leaf_draws[None], sep_draws[None])


def solution(mesh):
    return jax.shard_map(
        on_device,
        mesh=mesh,
        in_specs=(
            P("leaf", "front", None, None),
            P("leaf", "front", None),
            P("leaf", "front", None, None),
            P("leaf", "front", None),
            P("leaf", None, "front", None),
            P("leaf", None, "front", None),
            P("leaf", None, "front", None),
            P("leaf", None, None),
            P("leaf", None, None),
            P("leaf", None, None),
            P("leaf"),
        ),
        out_specs=(P("leaf", "front", None, None), P("leaf", "front", None)),
        check_vma=False,
    )
```

```python
import functools

import jax
import jax.numpy as jnp
from jax import lax
from jax.experimental import pallas as pl
from jax.experimental.pallas import tpu as pltpu
from jax.sharding import PartitionSpec as P

MESH = pl.DeviceIdType.MESH
BF = jnp.bfloat16
F32 = jnp.float32
HALF = 64
SKIPPED = (3, 5)


def nn(a, b):
    return lax.dot_general(a, b, (((1,), (0,)), ((), ())), preferred_element_type=F32)


def nt(a, b):
    return lax.dot_general(a, b, (((1,), (1,)), ((), ())), preferred_element_type=F32)


def tn(a, b):
    return lax.dot_general(a, b, (((0,), (0,)), ((), ())), preferred_element_type=F32)


def pack(block_ref, packed_ref):
    _, rows, samples = block_ref.shape
    for slab in range(samples // 128):
        lanes = slice(slab * 128, slab * 128 + 128)
        a = block_ref[0:2, :, lanes].reshape(2 * rows, 128)
        b = block_ref[2:4, :, lanes].reshape(2 * rows, 128)
        for core in range(2):
            part = slice(core * HALF, core * HALF + HALF)
            both = jnp.concatenate([a[:, part], b[:, part]], axis=1)
            packed_ref[2 * slab + core] = both.reshape(2, rows, 128)


def kernel(
    n_leaf,
    n_front,
    depth,
    cnt_ref,
    rhs_hbm,
    noise_hbm,
    inv_hbm,
    left_hbm,
    right_hbm,
    srhs_hbm,
    snoise_hbm,
    sinv_hbm,
    sleft_hbm,
    sright_hbm,
    leaf_out,
    sep_out,
    x_buf,
    n_buf,
    pk,
    pkn,
    r2,
    n2,
    inv,
    lw,
    srhs,
    snoise,
    sinv,
    su,
    wall,
    hw,
    s2,
    res,
    rb,
    zacc,
    tl_send,
    tl_recv,
    up_send,
    up_recv,
    dn_send,
    dn_recv,
    zp_send,
    zp_recv,
    hu_recv,
    v_send,
    dv_recv,
    da,
    own_dup,
    prev_dup,
    pull,
    d2,
    o2,
    load_sem,
    a_send,
    a_recv,
    nz_send,
    nz_recv,
    gi_send,
    gi_recv,
    g_send,
    g_recv,
    tl_ssem,
    tl_rsem,
    up_ssem,
    up_rsem,
    dn_ssem,
    dn_rsem,
    o_send,
    o_recv,
    hw_ssem,
    hw_rsem,
    gh_send,
    gh_recv,
    hu_ssem,
    hu_rsem,
    v_ssem,
    dv_rsem,
    da_ssem,
    zp_ssem,
    zp_rsem,
    known_sem,
):
    leaf = lax.axis_index("leaf")
    front = lax.axis_index("front")
    chips = n_front // 2
    x = front // 2
    core = front % 2
    rows = x_buf.shape[1]
    pos = leaf + 1
    level = jnp.int32(0)
    for bit in range(1, depth + 1):
        level = level + (pos % (1 << bit) == 0).astype(jnp.int32)
    span = jnp.int32(1)
    for bit in range(1, depth + 1):
        span = jnp.where(pos % (1 << bit) == 0, jnp.int32(1 << bit), span)
    odd = leaf % 2
    is_even = odd == 0

    def inside(target):
        return jnp.logical_and(target >= 0, target < n_leaf)

    def any_of(value, levels):
        found = jnp.bool_(False)
        for one in levels:
            found = jnp.logical_or(found, value == one)
        return found

    skipped = tuple(one for one in SKIPPED if one < depth)
    is_skipped = any_of(level, skipped)
    is_joined = any_of(level + 1, skipped)
    joined = is_joined.astype(jnp.int32)
    near = ((pos // span) % 4 == 1).astype(jnp.int32)
    parent = leaf + (2 * near - 1) * span
    own_level = jnp.minimum(level, depth - 1)
    half_span = jnp.maximum(span // 2, 1)
    lowest = skipped[0] if skipped else depth
    is_host = level > lowest
    is_top = leaf == n_leaf - 1
    top_hosts_two = len(skipped) == 2

    def ancestor(i):
        return leaf + (2 * i - 1) * span

    def group_host(i):
        return jnp.where(is_skipped, ancestor(i), parent + (2 * i - 1) * 2 * span)

    def host_slot(i):
        far_group = jnp.logical_or(level == skipped[-1], level + 1 == skipped[-1])
        return jnp.where(jnp.logical_and(far_group, top_hosts_two), 1, 1 - i)

    def group_of(slot):
        if slot == 0:
            return leaf - (1 << lowest), jnp.int32(1 << (lowest - 1))
        if top_hosts_two:
            other = 1 << skipped[-1]
            return (
                jnp.where(is_top, leaf - other, leaf + (1 << lowest)),
                jnp.where(is_top, jnp.int32(other // 2), jnp.int32(1 << (lowest - 1))),
            )
        return leaf + (1 << lowest), jnp.int32(1 << (lowest - 1))

    def group_side(slot):
        if slot == 0:
            return jnp.int32(1)
        return is_top.astype(jnp.int32)

    def has_group(slot):
        return jnp.logical_and(is_host, inside(group_of(slot)[0]))

    def load(i, src, dst):
        return pltpu.make_async_copy(src, dst, load_sem.at[i])

    own_rows = pl.ds(pl.multiple_of(front * rows, rows), rows)
    loads = [
        load(0, rhs_hbm, x_buf),
        load(1, inv_hbm, inv.at[:, own_rows, :]),
        load(2, right_hbm, lw.at[0, :, own_rows, :]),
        load(3, left_hbm, lw.at[1, :, own_rows, :]),
        load(4, sinv_hbm, sinv),
        load(5, sleft_hbm, su.at[0]),
        load(6, sright_hbm, su.at[1]),
        load(7, srhs_hbm, srhs),
        load(8, snoise_hbm, snoise),
        load(9, noise_hbm, n_buf),
    ]
    for copy in loads:
        copy.start()

    barrier = pltpu.get_barrier_semaphore()
    partners = jnp.int32(n_front - 1)
    for step in range(1, n_front):
        pl.semaphore_signal(
            barrier, inc=1, device_id={"front": (front + step) % n_front}, device_id_type=MESH
        )
    greeted = [(leaf - 1, leaf > 0), (leaf + 1, leaf < n_leaf - 1)]
    if skipped:
        greeted += [
            (parent, is_joined),
            (leaf - half_span, is_skipped),
            (leaf + half_span, is_skipped),
            (group_host(0), jnp.logical_and(is_joined, inside(group_host(0)))),
            (group_host(1), jnp.logical_and(is_joined, inside(group_host(1)))),
        ]
        for slot in range(2):
            center, reach = group_of(slot)
            greeted += [(center - reach, has_group(slot)), (center + reach, has_group(slot))]
    for target, reached in greeted:
        partners = partners + reached.astype(jnp.int32)

        @pl.when(reached)
        def _():
            pl.semaphore_signal(barrier, inc=1, device_id={"leaf": target}, device_id_type=MESH)

    loads[0].wait()
    pack(x_buf, pk)
    loads[4].wait()
    loads[5].wait()
    wall[0] = tn(sinv[...], su[0]).astype(BF)
    pl.semaphore_wait(barrier, partners)

    width = srhs.shape[1]
    share_rows = width // n_front
    share_here = pl.ds(pl.multiple_of(front * share_rows, share_rows), share_rows)

    def hw_copy(i, slot, target):
        return pltpu.make_async_remote_copy(
            src_ref=wall.at[i, share_here],
            dst_ref=hw.at[slot, share_here],
            send_sem=hw_ssem.at[i],
            recv_sem=hw_rsem.at[slot],
            device_id={"leaf": target},
            device_id_type=MESH,
        )

    if skipped:

        @pl.when(is_joined)
        def _():
            pl.semaphore_signal(known_sem, inc=1, device_id={"leaf": parent}, device_id_type=MESH)

    def exchange(src, dst_at, sends, recvs, step):
        peer = (front + step) % n_front
        return pltpu.make_async_remote_copy(
            src_ref=src.at[peer],
            dst_ref=dst_at(front),
            send_sem=sends.at[step - 1],
            recv_sem=recvs.at[step - 1],
            device_id={"front": peer},
            device_id_type=MESH,
        )

    def arrival(src, dst_at, sends, recvs, step):
        peer = (front + n_front - step) % n_front
        return pltpu.make_async_remote_copy(
            src_ref=src.at[peer],
            dst_ref=dst_at(peer),
            send_sem=sends.at[step - 1],
            recv_sem=recvs.at[step - 1],
            device_id={"front": peer},
            device_id_type=MESH,
        )

    def rows_of(ref):
        return lambda f: ref.at[:, pl.ds(pl.multiple_of(f * rows, rows), rows), :]

    def piece(buf, dx, flip, low, high):
        chip = (x + dx + chips) % chips
        who = 2 * chip + (1 - core if flip else core)
        count, order, _ = buf.shape
        low, high = low * count // 4, high * count // 4
        some = order // n_front
        return buf.at[low:high, pl.ds(pl.multiple_of(who * some, some), some), :]

    routes = [
        (0, 0, 4, 1, False),
        (0, 0, 4, -1, False),
        (0, 0, 4, 0, True),
        (-1, 0, 4, 0, True),
        (-1, 0, 2, 1, False),
        (1, 0, 4, 0, True),
        (1, 2, 4, -1, False),
        (2, 0, 2, 0, True),
        (2, 2, 4, 0, True),
    ]

    def route(buf, sends, recvs, i):
        dx, low, high, to, flip = routes[i]
        chip = (x + to + chips) % chips
        peer = 2 * chip + (1 - core if flip else core)
        block = piece(buf, dx, False, low, high)
        return pltpu.make_async_remote_copy(
            src_ref=block,
            dst_ref=block,
            send_sem=sends.at[i],
            recv_sem=recvs.at[i],
            device_id={"front": peer},
            device_id_type=MESH,
        )

    def route_arrival(buf, sends, recvs, i):
        dx, low, high, to, flip = routes[i]
        chip = (x + to + chips) % chips
        peer = 2 * chip + (1 - core if flip else core)
        block = piece(buf, dx - to, flip, low, high)
        return pltpu.make_async_remote_copy(
            src_ref=block,
            dst_ref=block,
            send_sem=sends.at[i],
            recv_sem=recvs.at[i],
            device_id={"front": peer},
            device_id_type=MESH,
        )

    class Gather:
        def __init__(self, buf, sends, recvs):
            self.args = (buf, sends, recvs)

        def send(self, *which):
            for i in which:
                route(*self.args, i).start()

        def take(self, *which):
            for i in which:
                route_arrival(*self.args, i).wait_recv()

        def drain(self):
            for i in range(len(routes)):
                route(*self.args, i).wait_send()

    first = odd
    second = 1 - odd
    gather_inv = Gather(inv, gi_send, gi_recv)
    gather_host = Gather(hw, gh_send, gh_recv)
    gather_one = Gather(lw.at[first], g_send.at[0], g_recv.at[0])
    gather_two = Gather(lw.at[second], g_send.at[1], g_recv.at[1])

    for step in range(1, n_front):
        exchange(pk, rows_of(r2), a_send, a_recv, step).start()
    loads[1].wait()
    gather_inv.send(0, 1, 2)
    loads[2].wait()
    loads[3].wait()
    gather_one.send(0, 1, 2)
    r2[:, own_rows, :] = pk[front]

    loads[6].wait()
    wall[1] = tn(sinv[...], su[1]).astype(BF)
    gather_inv.take(0)
    gather_inv.send(4, 3)
    gather_inv.take(1)
    gather_inv.send(6, 5)
    if skipped:

        @pl.when(is_skipped)
        def _():
            pl.semaphore_wait(known_sem, 2)
            for i in range(2):

                @pl.when(inside(ancestor(i)))
                def _():
                    hw_copy(i, host_slot(i), ancestor(i)).start()

    gather_one.take(0)
    gather_one.send(4, 3)
    gather_one.take(1)
    gather_one.send(6, 5)
    gather_inv.take(4)
    gather_inv.send(7)
    gather_inv.take(6)
    gather_inv.send(8)
    gather_two.send(0, 1, 2)
    for step in range(1, n_front):
        arrival(pk, rows_of(r2), a_send, a_recv, step).wait_recv()
    gather_inv.take(2, 3, 5, 7, 8)

    live = cnt_ref[0]
    low_lanes = lax.broadcasted_iota(jnp.int32, (1, 128), 1) < HALF
    alive = [
        jnp.logical_or(
            jnp.logical_and(low_lanes, t < live),
            jnp.logical_and(jnp.logical_not(low_lanes), t + 2 < live),
        )
        for t in range(2)
    ]
    for t in range(2):
        block = r2[t]
        solved = jnp.where(low_lanes, nn(inv[t], block), nn(inv[t + 2], block))
        s2[t] = jnp.where(alive[t], solved, 0.0).astype(BF)

    def toward(side):
        total = jnp.zeros((HALF, srhs.shape[1]), F32)
        for t in range(2):
            turned = s2[t].T
            total = total + nn(turned[0:HALF], lw[side, t])
            total = total + nn(turned[HALF:], lw[side, t + 2])
        return total

    def tl_copy(target):
        return pltpu.make_async_remote_copy(
            src_ref=tl_send,
            dst_ref=tl_recv,
            send_sem=tl_ssem,
            recv_sem=tl_rsem,
            device_id={"leaf": target},
            device_id_type=MESH,
        )

    chunks = [(0, 256), (256, width)] if width > 256 else [(0, width)]

    class Message:
        def __init__(self, src, dst, sends, recvs, target):
            self.parts = [
                pltpu.make_async_remote_copy(
                    src_ref=src.at[:, low:high],
                    dst_ref=dst.at[:, low:high],
                    send_sem=sends.at[n],
                    recv_sem=recvs.at[n],
                    device_id={"leaf": target},
                    device_id_type=MESH,
                )
                for n, (low, high) in enumerate(chunks)
            ]

        def start(self):
            for part in self.parts:
                part.start()

        def wait_send(self):
            for part in self.parts:
                part.wait_send()

        def wait_recv(self):
            for part in self.parts:
                part.wait_recv()

    def up_message(i, h, target):
        return Message(up_send.at[i], up_recv.at[h, i], up_ssem.at[i], up_rsem.at[h, i], target)

    def hu_message(i, slot, which, target):
        return Message(
            up_send.at[near], hu_recv.at[slot, which], hu_ssem.at[i], hu_rsem.at[slot, which], target
        )

    def dn_message(i, h, target):
        return Message(dn_send, dn_recv.at[i], dn_ssem.at[i, h], dn_rsem.at[i], target)

    def v_message(slot, which, side, target):
        return Message(
            v_send.at[slot], dv_recv.at[side], v_ssem.at[slot, which], dv_rsem.at[side], target
        )

    def da_message(target):
        return Message(da, dn_recv.at[near], da_ssem, dn_rsem.at[near], target)

    def zp_message(i, target):
        return Message(zp_send, zp_recv, zp_ssem.at[i], zp_rsem, target)

    def climb():
        rb[...] = res[...].astype(BF)
        for j in range(2):
            i = near if j == 0 else 1 - near
            target = ancestor(i)

            @pl.when(inside(target))
            def _():
                message = up_message(i, own_level, target)
                for n, (low, high) in enumerate(chunks):
                    up_send[i, :, low:high] = nn(rb[...], wall[i, :, low:high]).astype(BF)
                    if j == 1 or not skipped:
                        message.parts[n].start()
                    else:

                        @pl.when(is_joined)
                        def _():
                            for side in range(2):

                                @pl.when(inside(group_host(side)))
                                def _():
                                    to_host(side).parts[n].start()

                        message.parts[n].start()

    def to_host(side):
        return hu_message(side, host_slot(side), 1 - near, group_host(side))

    def gather_level(h):
        below = lax.shift_left(jnp.int32(1), jnp.int32(h))
        for i in range(2):
            source = leaf + (1 - 2 * i) * below

            @pl.when(inside(source))
            def _():
                up_message(i, h, source).wait_recv()
                res[...] = res[...] - up_recv[h, i].astype(F32)

    gather_one.take(4)
    gather_one.send(7)
    gather_one.take(6)
    gather_one.send(8)
    gather_one.take(2, 3, 5, 7, 8)
    loads[7].wait()
    part_one = toward(first)

    @pl.when(jnp.logical_not(is_even))
    def _():
        tl_send[...] = part_one.astype(BF)
        tl_copy(leaf - 1).start()

    gather_two.take(0)
    gather_two.send(4, 3)
    gather_two.take(1)
    gather_two.send(6, 5)

    @pl.when(is_even)
    def _():
        res[...] = srhs[...].astype(F32) - part_one
        tl_copy(leaf + 1).wait_recv()
        res[...] = res[...] - tl_recv[...].astype(F32)
        climb()

    gather_two.take(4)
    gather_two.send(7)
    gather_two.take(6)
    gather_two.send(8)
    gather_two.take(2, 3, 5, 7, 8)
    part_two = toward(second)

    @pl.when(jnp.logical_and(is_even, leaf > 0))
    def _():
        tl_send[...] = part_two.astype(BF)
        tl_copy(leaf - 1).start()

    @pl.when(jnp.logical_not(is_even))
    def _():
        res[...] = srhs[...].astype(F32) - part_two

        @pl.when(leaf < n_leaf - 1)
        def _():
            tl_copy(leaf + 1).wait_recv()
            res[...] = res[...] - tl_recv[...].astype(F32)

        if skipped:

            @pl.when(is_host)
            def _():
                for slot in range(2):

                    @pl.when(has_group(slot))
                    def _():
                        hw_copy(0, slot, group_of(slot)[0]).wait_recv()

                gather_host.send(0, 1, 2)
                gather_host.take(0)
                gather_host.send(4, 3)
                gather_host.take(1)
                gather_host.send(6, 5)
                gather_host.take(4)
                gather_host.send(7)
                gather_host.take(6)
                gather_host.send(8)

        @pl.loop(0, level - is_skipped.astype(jnp.int32))
        def _(h):
            gather_level(h)

        if skipped:

            @pl.when(is_host)
            def _():
                gather_host.take(2, 3, 5, 7, 8)
                for slot in range(2):

                    @pl.when(has_group(slot))
                    def _():
                        center, reach = group_of(slot)
                        hu_message(0, slot, 0, center - reach).wait_recv()
                        hu_message(0, slot, 1, center + reach).wait_recv()
                        both = hu_recv[slot, 0].astype(F32) + hu_recv[slot, 1].astype(F32)
                        res[...] = res[...] + nn(both.astype(BF), hw[slot])

        climb()
        if skipped:

            @pl.when(is_skipped)
            def _():
                gather_level(level - 1)
                rb[...] = res[...].astype(BF)

    loads[8].wait()
    solved_sep = nt(rb[...], sinv[...]).astype(BF).astype(F32)
    target_sep = (solved_sep + snoise[...].astype(F32)).astype(BF)
    zacc[...] = nn(target_sep, sinv[...])
    if skipped:

        @pl.when(is_skipped)
        def _():
            zp_send[...] = zacc[...].astype(BF)
            for i in range(2):
                zp_message(i, leaf + (1 - 2 * i) * half_span).start()

    loads[9].wait()
    pack(n_buf, pkn)
    for step in range(1, n_front):
        exchange(pkn, rows_of(n2), nz_send, nz_recv, step).start()
    n2[:, own_rows, :] = pkn[front]

    is_plain = jnp.logical_not(jnp.logical_or(is_skipped, is_joined))

    def take_draws(i, wanted):
        source = ancestor(i)

        @pl.when(jnp.logical_and(wanted, inside(source)))
        def _():
            dn_message(i, 0, source).wait_recv()
            zacc[...] = zacc[...] - nt(dn_recv[i], wall[i])

    take_draws(1 - near, jnp.logical_not(is_skipped))
    take_draws(near, is_plain)
    if skipped:

        @pl.when(is_joined)
        def _():
            zp_message(0, parent).wait_recv()
            da[...] = zp_recv[...]

        for i in range(2):

            @pl.when(jnp.logical_and(jnp.logical_not(is_plain), inside(group_host(i))))
            def _():
                v_message(0, 0, i, group_host(i)).wait_recv()

                @pl.when(is_skipped)
                def _():
                    zacc[...] = zacc[...] - dv_recv[i].astype(F32)

                @pl.when(is_joined)
                def _():
                    da[...] = (da[...].astype(F32) - dv_recv[i].astype(F32)).astype(BF)

        @pl.when(is_joined)
        def _():
            @pl.when(level + 1 == lowest)
            def _():
                da_message(leaf + (2 * near - 1) * half_span).start()

            zacc[...] = zacc[...] - nt(da[...], wall[near])

    draws = zacc[...]
    sep_out[...] = draws
    dn_send[...] = draws.astype(BF)

    def for_level(h, act):
        below = lax.shift_left(jnp.int32(1), jnp.int32(h))
        bypassed = jnp.logical_or(
            any_of(jnp.int32(h), skipped), jnp.logical_and(is_skipped, h >= level - 2)
        )
        for i in range(2):
            target = leaf + (1 - 2 * i) * below

            @pl.when(jnp.logical_and(jnp.logical_not(bypassed), inside(target)))
            def _():
                act(dn_message(i, h, target))

    def begin(message):
        message.start()

    def left(message):
        message.wait_send()

    steps = jnp.maximum(level - lowest + 1, 0)

    @pl.loop(0, steps)
    def _(step):
        for_level(level - 1 - step, begin)

    if skipped:

        def to_group(slot):
            center, reach = group_of(slot)
            return [
                v_message(slot, which, group_side(slot), target)
                for which, target in enumerate((center - reach, center + reach, center))
            ]

        for slot in range(2):

            @pl.when(has_group(slot))
            def _():
                v_send[slot] = nt(dn_send[...], hw[slot]).astype(BF)
                for message in to_group(slot):
                    message.start()

        for slot in range(2):

            @pl.when(has_group(slot))
            def _():
                for message in to_group(slot):
                    message.wait_send()

    @pl.loop(0, steps)
    def _(step):
        for_level(level - 1 - step, left)

    @pl.loop(steps, level)
    def _(step):
        for_level(level - 1 - step, begin)
        for_level(level - 1 - step, left)

    @pl.when(is_even)
    def _():
        dn_message(2, 0, leaf + 1).start()

    own_dup[0:HALF] = dn_send[...]
    own_dup[HALF:] = dn_send[...]

    def pulled(side, dup):
        return [
            jnp.where(low_lanes, nt(lw[side, t], dup), nt(lw[side, t + 2], dup)) for t in range(2)
        ]

    for t, value in enumerate(pulled(0, own_dup[...])):
        pull[t] = value
    for step in range(1, n_front):
        arrival(pkn, rows_of(n2), nz_send, nz_recv, step).wait_recv()

    @pl.when(jnp.logical_not(is_even))
    def _():
        dn_message(2, 0, leaf - 1).wait_recv()
        prev_dup[0:HALF] = dn_recv[2]

    @pl.when(jnp.logical_and(is_even, leaf > 0))
    def _():
        prev_dup[0:HALF] = dn_recv[0]

    @pl.when(leaf == 0)
    def _():
        prev_dup[0:HALF] = jnp.zeros((HALF, prev_dup.shape[1]), BF)

    prev_dup[HALF:] = prev_dup[0:HALF]
    for t, value in enumerate(pulled(1, prev_dup[...])):
        mixed = s2[t].astype(F32) + n2[t].astype(F32) - pull[t] - value
        mixed = jnp.where(alive[t], mixed, 0.0).astype(BF)
        drawn = jnp.where(low_lanes, tn(inv[t], mixed), tn(inv[t + 2], mixed)).astype(BF)
        for f in range(n_front):
            d2[f, t] = drawn[f * rows : f * rows + rows]

    for step in range(1, n_front):
        exchange(d2, lambda f: o2.at[f], o_send, o_recv, step).start()
    o2[front] = d2[front]
    for step in range(1, n_front):
        arrival(d2, lambda f: o2.at[f], o_send, o_recv, step).wait_recv()

    for t in range(2):
        for slab in range(n_front // 2):
            lanes = slice(slab * 128, slab * 128 + 128)
            a = o2[2 * slab, t]
            b = o2[2 * slab + 1, t]
            leaf_out[t, :, lanes] = jnp.concatenate([a[:, :HALF], b[:, :HALF]], axis=1)
            leaf_out[t + 2, :, lanes] = jnp.concatenate([a[:, HALF:], b[:, HALF:]], axis=1)

    for step in range(1, n_front):
        exchange(pk, rows_of(r2), a_send, a_recv, step).wait_send()
        exchange(pkn, rows_of(n2), nz_send, nz_recv, step).wait_send()
        exchange(d2, lambda f: o2.at[f], o_send, o_recv, step).wait_send()
    gather_inv.drain()
    gather_one.drain()
    gather_two.drain()

    @pl.when(leaf > 0)
    def _():
        tl_copy(leaf - 1).wait_send()

    for i in range(2):
        target = ancestor(i)

        @pl.when(inside(target))
        def _():
            up_message(i, own_level, target).wait_send()

    @pl.when(is_even)
    def _():
        dn_message(2, 0, leaf + 1).wait_send()

    if skipped:

        @pl.when(is_joined)
        def _():
            for side in range(2):

                @pl.when(inside(group_host(side)))
                def _():
                    to_host(side).wait_send()

            @pl.when(level + 1 == lowest)
            def _():
                da_message(leaf + (2 * near - 1) * half_span).wait_send()

        @pl.when(is_skipped)
        def _():
            for i in range(2):
                zp_message(i, leaf + (1 - 2 * i) * half_span).wait_send()

                @pl.when(inside(ancestor(i)))
                def _():
                    hw_copy(i, host_slot(i), ancestor(i)).wait_send()

        @pl.when(is_host)
        def _():
            gather_host.drain()


def on_device(
    leaf_rhs,
    sep_rhs,
    leaf_noise,
    sep_noise,
    leaf_inverse,
    leaf_left,
    leaf_right,
    sep_inverse,
    sep_left,
    sep_right,
    leaf_count,
):
    n_leaf = lax.axis_size("leaf")
    n_front = lax.axis_size("front")
    depth = n_leaf.bit_length() - 1
    _, rows, slots, samples = leaf_rhs.shape
    share, width = sep_rhs.shape[1:]
    order = rows * n_front
    rhs = jnp.transpose(leaf_rhs[0], (1, 0, 2))
    noise = jnp.transpose(leaf_noise[0], (1, 0, 2))
    hbm = pl.BlockSpec(memory_space=pltpu.HBM)
    vmem = pl.BlockSpec(memory_space=pltpu.VMEM)
    dma = pltpu.SemaphoreType.DMA
    leaf_draws, sep_draws = pl.pallas_call(
        functools.partial(kernel, n_leaf, n_front, depth),
        out_shape=(
            jax.ShapeDtypeStruct((slots, rows, samples), BF),
            jax.ShapeDtypeStruct((share, width), F32),
        ),
        in_specs=[pl.BlockSpec(memory_space=pltpu.SMEM)] + [hbm] * 10,
        out_specs=(vmem, vmem),
        scratch_shapes=[
            pltpu.VMEM((slots, rows, samples), BF),
            pltpu.VMEM((slots, rows, samples), BF),
            pltpu.VMEM((n_front, 2, rows, 128), BF),
            pltpu.VMEM((n_front, 2, rows, 128), BF),
            pltpu.VMEM((2, order, 128), BF),
            pltpu.VMEM((2, order, 128), BF),
            pltpu.VMEM((slots, order, order), BF),
            pltpu.VMEM((2, slots, order, width), BF),
            pltpu.VMEM((share, width), BF),
            pltpu.VMEM((share, width), BF),
            pltpu.VMEM((width, width), BF),
            pltpu.VMEM((2, width, width), BF),
            pltpu.VMEM((2, width, width), BF),
            pltpu.VMEM((2, width, width), BF),
            pltpu.VMEM((2, order, 128), BF),
            pltpu.VMEM((share, width), F32),
            pltpu.VMEM((share, width), BF),
            pltpu.VMEM((share, width), F32),
            pltpu.VMEM((share, width), BF),
            pltpu.VMEM((share, width), BF),
            pltpu.VMEM((2, share, width), BF),
            pltpu.VMEM((depth, 2, share, width), BF),
            pltpu.VMEM((share, width), BF),
            pltpu.VMEM((3, share, width), BF),
            pltpu.VMEM((share, width), BF),
            pltpu.VMEM((share, width), BF),
            pltpu.VMEM((2, 2, share, width), BF),
            pltpu.VMEM((2, share, width), BF),
            pltpu.VMEM((2, share, width), BF),
            pltpu.VMEM((share, width), BF),
            pltpu.VMEM((2 * share, width), BF),
            pltpu.VMEM((2 * share, width), BF),
            pltpu.VMEM((2, order, 128), F32),
            pltpu.VMEM((n_front, 2, rows, 128), BF),
            pltpu.VMEM((n_front, 2, rows, 128), BF),
            dma((10,)),
            dma((n_front - 1,)),
            dma((n_front - 1,)),
            dma((n_front - 1,)),
            dma((n_front - 1,)),
            dma((9,)),
            dma((9,)),
            dma((2, 9)),
            dma((2, 9)),
            dma,
            dma,
            dma((2, 2)),
            dma((depth, 2, 2)),
            dma((3, depth, 2)),
            dma((3, 2)),
            dma((n_front - 1,)),
            dma((n_front - 1,)),
            dma((2,)),
            dma((2,)),
            dma((9,)),
            dma((9,)),
            dma((2, 2)),
            dma((2, 2, 2)),
            dma((2, 3, 2)),
            dma((2, 2)),
            dma((2,)),
            dma((2, 2)),
            dma((2,)),
            pltpu.SemaphoreType.REGULAR,
        ],
        compiler_params=pltpu.CompilerParams(
            collective_id=0, has_side_effects=True, vmem_limit_bytes=63 * 1024 * 1024
        ),
    )(
        leaf_count,
        rhs,
        noise,
        leaf_inverse[0],
        leaf_left[0],
        leaf_right[0],
        sep_rhs[0],
        sep_noise[0],
        sep_inverse[0],
        sep_left[0],
        sep_right[0],
    )
    leaf_draws = jnp.transpose(leaf_draws, (1, 0, 2)).astype(F32)
    return (leaf_draws[None], sep_draws[None])


def solution(mesh):
    return jax.shard_map(
        on_device,
        mesh=mesh,
        in_specs=(
            P("leaf", "front", None, None),
            P("leaf", "front", None),
            P("leaf", "front", None, None),
            P("leaf", "front", None),
            P("leaf", None, "front", None),
            P("leaf", None, "front", None),
            P("leaf", None, "front", None),
            P("leaf", None, None),
            P("leaf", None, None),
            P("leaf", None, None),
            P("leaf"),
        ),
        out_specs=(P("leaf", "front", None, None), P("leaf", "front", None)),
        check_vma=False,
    )
```

```python
import functools

import jax
import jax.numpy as jnp
from jax import lax
from jax.experimental import pallas as pl
from jax.experimental.pallas import tpu as pltpu
from jax.sharding import PartitionSpec as P

MESH = pl.DeviceIdType.MESH
BF = jnp.bfloat16
F32 = jnp.float32
HALF = 64
SKIPPED = (3, 5)


def nn(a, b):
    return lax.dot_general(a, b, (((1,), (0,)), ((), ())), preferred_element_type=F32)


def nt(a, b):
    return lax.dot_general(a, b, (((1,), (1,)), ((), ())), preferred_element_type=F32)


def tn(a, b):
    return lax.dot_general(a, b, (((0,), (0,)), ((), ())), preferred_element_type=F32)


def pack(raw_ref, block_ref, packed_ref):
    rows, slots, samples = raw_ref.shape
    for t in range(slots):
        block_ref[t] = raw_ref[:, t, :]
    for slab in range(samples // 128):
        lanes = slice(slab * 128, slab * 128 + 128)
        a = block_ref[0:2, :, lanes].reshape(2 * rows, 128)
        b = block_ref[2:4, :, lanes].reshape(2 * rows, 128)
        for core in range(2):
            part = slice(core * HALF, core * HALF + HALF)
            both = jnp.concatenate([a[:, part], b[:, part]], axis=1)
            packed_ref[2 * slab + core] = both.reshape(2, rows, 128)


def kernel(
    n_leaf,
    n_front,
    depth,
    cnt_ref,
    rhs_hbm,
    noise_hbm,
    inv_hbm,
    left_hbm,
    right_hbm,
    srhs_hbm,
    snoise_hbm,
    sinv_hbm,
    sleft_hbm,
    sright_hbm,
    leaf_out,
    sep_out,
    x_buf,
    n_buf,
    turned_slots,
    pk,
    pkn,
    r2,
    n2,
    inv,
    lw,
    srhs,
    snoise,
    sinv,
    su,
    wall,
    wt,
    hw,
    hwt,
    s2,
    res,
    rb,
    zacc,
    tl_send,
    tl_recv,
    up_send,
    up_recv,
    dn_send,
    dn_recv,
    zp_send,
    zp_recv,
    hu_recv,
    v_send,
    dv_recv,
    da,
    own_dup,
    prev_dup,
    pull,
    d2,
    o2,
    load_sem,
    a_send,
    a_recv,
    nz_send,
    nz_recv,
    gi_send,
    gi_recv,
    g_send,
    g_recv,
    tl_ssem,
    tl_rsem,
    up_ssem,
    up_rsem,
    dn_ssem,
    dn_rsem,
    o_send,
    o_recv,
    hw_ssem,
    hw_rsem,
    gh_send,
    gh_recv,
    hu_ssem,
    hu_rsem,
    v_ssem,
    dv_rsem,
    da_ssem,
    zp_ssem,
    zp_rsem,
    known_sem,
):
    leaf = lax.axis_index("leaf")
    front = lax.axis_index("front")
    chips = n_front // 2
    x = front // 2
    core = front % 2
    rows = x_buf.shape[0]
    pos = leaf + 1
    level = jnp.int32(0)
    for bit in range(1, depth + 1):
        level = level + (pos % (1 << bit) == 0).astype(jnp.int32)
    span = jnp.int32(1)
    for bit in range(1, depth + 1):
        span = jnp.where(pos % (1 << bit) == 0, jnp.int32(1 << bit), span)
    odd = leaf % 2
    is_even = odd == 0

    def inside(target):
        return jnp.logical_and(target >= 0, target < n_leaf)

    def any_of(value, levels):
        found = jnp.bool_(False)
        for one in levels:
            found = jnp.logical_or(found, value == one)
        return found

    skipped = tuple(one for one in SKIPPED if one < depth)
    is_skipped = any_of(level, skipped)
    is_joined = any_of(level + 1, skipped)
    joined = is_joined.astype(jnp.int32)
    near = ((pos // span) % 4 == 1).astype(jnp.int32)
    parent = leaf + (2 * near - 1) * span
    parent_near = (((parent + 1) // (2 * span)) % 4 == 1).astype(jnp.int32)
    own_level = jnp.minimum(level, depth - 1)
    half_span = jnp.maximum(span // 2, 1)
    lowest = skipped[0] if skipped else depth
    is_host = level > lowest
    is_top = leaf == n_leaf - 1
    top_hosts_two = len(skipped) == 2

    def ancestor(i):
        return leaf + (2 * i - 1) * span

    def group_host(i):
        return jnp.where(is_skipped, ancestor(i), parent + (2 * i - 1) * 2 * span)

    def host_slot(i):
        far_group = jnp.logical_or(level == skipped[-1], level + 1 == skipped[-1])
        return jnp.where(jnp.logical_and(far_group, top_hosts_two), 1, 1 - i)

    def group_of(slot):
        if slot == 0:
            return leaf - (1 << lowest), jnp.int32(1 << (lowest - 1))
        if top_hosts_two:
            other = 1 << skipped[-1]
            return (
                jnp.where(is_top, leaf - other, leaf + (1 << lowest)),
                jnp.where(is_top, jnp.int32(other // 2), jnp.int32(1 << (lowest - 1))),
            )
        return leaf + (1 << lowest), jnp.int32(1 << (lowest - 1))

    def group_side(slot):
        if slot == 0:
            return jnp.int32(1)
        return is_top.astype(jnp.int32)

    def has_group(slot):
        return jnp.logical_and(is_host, inside(group_of(slot)[0]))

    def load(i, src, dst):
        return pltpu.make_async_copy(src, dst, load_sem.at[i])

    own_rows = pl.ds(pl.multiple_of(front * rows, rows), rows)
    loads = [
        load(0, rhs_hbm, x_buf),
        load(1, inv_hbm, inv.at[:, own_rows, :]),
        load(2, right_hbm, lw.at[0, :, own_rows, :]),
        load(3, left_hbm, lw.at[1, :, own_rows, :]),
        load(4, sinv_hbm, sinv),
        load(5, sleft_hbm, su.at[0]),
        load(6, sright_hbm, su.at[1]),
        load(7, srhs_hbm, srhs),
        load(8, snoise_hbm, snoise),
        load(9, noise_hbm, n_buf),
    ]
    for copy in loads:
        copy.start()

    barrier = pltpu.get_barrier_semaphore()
    partners = jnp.int32(n_front - 1)
    for step in range(1, n_front):
        pl.semaphore_signal(
            barrier, inc=1, device_id={"front": (front + step) % n_front}, device_id_type=MESH
        )
    greeted = [(leaf - 1, leaf > 0), (leaf + 1, leaf < n_leaf - 1)]
    if skipped:
        greeted += [
            (parent, is_joined),
            (leaf - half_span, is_skipped),
            (leaf + half_span, is_skipped),
            (group_host(0), jnp.logical_and(is_joined, inside(group_host(0)))),
            (group_host(1), jnp.logical_and(is_joined, inside(group_host(1)))),
        ]
        for slot in range(2):
            center, reach = group_of(slot)
            greeted += [(center - reach, has_group(slot)), (center + reach, has_group(slot))]
    for target, reached in greeted:
        partners = partners + reached.astype(jnp.int32)

        @pl.when(reached)
        def _():
            pl.semaphore_signal(barrier, inc=1, device_id={"leaf": target}, device_id_type=MESH)

    loads[0].wait()
    pack(x_buf, turned_slots, pk)
    loads[4].wait()
    loads[5].wait()
    wall[0] = tn(sinv[...], su[0]).astype(BF)
    pl.semaphore_wait(barrier, partners)

    width = srhs.shape[1]
    share_rows = width // n_front
    share_here = pl.ds(pl.multiple_of(front * share_rows, share_rows), share_rows)

    def hw_copy(i, slot, target):
        return pltpu.make_async_remote_copy(
            src_ref=wall.at[i, share_here],
            dst_ref=hw.at[slot, share_here],
            send_sem=hw_ssem.at[i],
            recv_sem=hw_rsem.at[slot],
            device_id={"leaf": target},
            device_id_type=MESH,
        )

    if skipped:

        @pl.when(is_joined)
        def _():
            pl.semaphore_signal(known_sem, inc=1, device_id={"leaf": parent}, device_id_type=MESH)

    def exchange(src, dst_at, sends, recvs, step):
        peer = (front + step) % n_front
        return pltpu.make_async_remote_copy(
            src_ref=src.at[peer],
            dst_ref=dst_at(front),
            send_sem=sends.at[step - 1],
            recv_sem=recvs.at[step - 1],
            device_id={"front": peer},
            device_id_type=MESH,
        )

    def arrival(src, dst_at, sends, recvs, step):
        peer = (front + n_front - step) % n_front
        return pltpu.make_async_remote_copy(
            src_ref=src.at[peer],
            dst_ref=dst_at(peer),
            send_sem=sends.at[step - 1],
            recv_sem=recvs.at[step - 1],
            device_id={"front": peer},
            device_id_type=MESH,
        )

    def rows_of(ref):
        return lambda f: ref.at[:, pl.ds(pl.multiple_of(f * rows, rows), rows), :]

    def piece(buf, dx, flip, low, high):
        chip = (x + dx + chips) % chips
        who = 2 * chip + (1 - core if flip else core)
        count, order, _ = buf.shape
        low, high = low * count // 4, high * count // 4
        some = order // n_front
        return buf.at[low:high, pl.ds(pl.multiple_of(who * some, some), some), :]

    routes = [
        (0, 0, 4, 1, False),
        (0, 0, 4, -1, False),
        (0, 0, 4, 0, True),
        (-1, 0, 4, 0, True),
        (-1, 0, 2, 1, False),
        (1, 0, 4, 0, True),
        (1, 2, 4, -1, False),
        (2, 0, 2, 0, True),
        (2, 2, 4, 0, True),
    ]

    def route(buf, sends, recvs, i):
        dx, low, high, to, flip = routes[i]
        chip = (x + to + chips) % chips
        peer = 2 * chip + (1 - core if flip else core)
        block = piece(buf, dx, False, low, high)
        return pltpu.make_async_remote_copy(
            src_ref=block,
            dst_ref=block,
            send_sem=sends.at[i],
            recv_sem=recvs.at[i],
            device_id={"front": peer},
            device_id_type=MESH,
        )

    def route_arrival(buf, sends, recvs, i):
        dx, low, high, to, flip = routes[i]
        chip = (x + to + chips) % chips
        peer = 2 * chip + (1 - core if flip else core)
        block = piece(buf, dx - to, flip, low, high)
        return pltpu.make_async_remote_copy(
            src_ref=block,
            dst_ref=block,
            send_sem=sends.at[i],
            recv_sem=recvs.at[i],
            device_id={"front": peer},
            device_id_type=MESH,
        )

    class Gather:
        def __init__(self, buf, sends, recvs):
            self.args = (buf, sends, recvs)

        def send(self, *which):
            for i in which:
                route(*self.args, i).start()

        def take(self, *which):
            for i in which:
                route_arrival(*self.args, i).wait_recv()

        def drain(self):
            for i in range(len(routes)):
                route(*self.args, i).wait_send()

    first = odd
    second = 1 - odd
    gather_inv = Gather(inv, gi_send, gi_recv)
    gather_host = Gather(hw, gh_send, gh_recv)
    gather_one = Gather(lw.at[first], g_send.at[0], g_recv.at[0])
    gather_two = Gather(lw.at[second], g_send.at[1], g_recv.at[1])

    for step in range(1, n_front):
        exchange(pk, rows_of(r2), a_send, a_recv, step).start()
    loads[1].wait()
    gather_inv.send(0, 1, 2)
    loads[2].wait()
    loads[3].wait()
    gather_one.send(0, 1, 2)
    r2[:, own_rows, :] = pk[front]

    loads[6].wait()
    wall[1] = tn(sinv[...], su[1]).astype(BF)
    gather_inv.take(0)
    gather_inv.send(4, 3)
    gather_inv.take(1)
    gather_inv.send(6, 5)
    if skipped:

        @pl.when(is_skipped)
        def _():
            pl.semaphore_wait(known_sem, 2)
            for i in range(2):

                @pl.when(inside(ancestor(i)))
                def _():
                    hw_copy(i, host_slot(i), ancestor(i)).start()

    gather_one.take(0)
    gather_one.send(4, 3)
    gather_one.take(1)
    gather_one.send(6, 5)
    gather_inv.take(4)
    gather_inv.send(7)
    gather_inv.take(6)
    gather_inv.send(8)
    gather_two.send(0, 1, 2)
    for step in range(1, n_front):
        arrival(pk, rows_of(r2), a_send, a_recv, step).wait_recv()
    gather_inv.take(2, 3, 5, 7, 8)

    live = cnt_ref[0]
    low_lanes = lax.broadcasted_iota(jnp.int32, (1, 128), 1) < HALF
    alive = [
        jnp.logical_or(
            jnp.logical_and(low_lanes, t < live),
            jnp.logical_and(jnp.logical_not(low_lanes), t + 2 < live),
        )
        for t in range(2)
    ]
    for t in range(2):
        block = r2[t]
        solved = jnp.where(low_lanes, nn(inv[t], block), nn(inv[t + 2], block))
        s2[t] = jnp.where(alive[t], solved, 0.0).astype(BF)

    def toward(side):
        total = jnp.zeros((HALF, srhs.shape[1]), F32)
        for t in range(2):
            turned = s2[t].T
            total = total + nn(turned[0:HALF], lw[side, t])
            total = total + nn(turned[HALF:], lw[side, t + 2])
        return total

    def tl_copy(target):
        return pltpu.make_async_remote_copy(
            src_ref=tl_send,
            dst_ref=tl_recv,
            send_sem=tl_ssem,
            recv_sem=tl_rsem,
            device_id={"leaf": target},
            device_id_type=MESH,
        )

    chunks = [(0, 256), (256, width)] if width > 256 else [(0, width)]

    class Message:
        def __init__(self, src, dst, sends, recvs, target):
            self.parts = [
                pltpu.make_async_remote_copy(
                    src_ref=src.at[:, low:high],
                    dst_ref=dst.at[:, low:high],
                    send_sem=sends.at[n],
                    recv_sem=recvs.at[n],
                    device_id={"leaf": target},
                    device_id_type=MESH,
                )
                for n, (low, high) in enumerate(chunks)
            ]

        def start(self):
            for part in self.parts:
                part.start()

        def wait_send(self):
            for part in self.parts:
                part.wait_send()

        def wait_recv(self):
            for part in self.parts:
                part.wait_recv()

    def up_message(i, h, target):
        return Message(up_send.at[i], up_recv.at[h, i], up_ssem.at[i], up_rsem.at[h, i], target)

    def hu_message(i, slot, which, target):
        return Message(
            up_send.at[near], hu_recv.at[slot, which], hu_ssem.at[i], hu_rsem.at[slot, which], target
        )

    def dn_message(i, h, target):
        return Message(dn_send, dn_recv.at[i], dn_ssem.at[i, h], dn_rsem.at[i], target)

    def v_message(slot, which, side, target):
        return Message(
            v_send.at[slot], dv_recv.at[side], v_ssem.at[slot, which], dv_rsem.at[side], target
        )

    def da_message(target):
        return Message(da, dn_recv.at[near], da_ssem, dn_rsem.at[near], target)

    def zp_message(i, target):
        return Message(zp_send, zp_recv, zp_ssem.at[i], zp_rsem, target)

    def climb():
        rb[...] = res[...].astype(BF)
        for j in range(2):
            i = near if j == 0 else 1 - near
            target = ancestor(i)

            @pl.when(inside(target))
            def _():
                message = up_message(i, own_level, target)
                for n, (low, high) in enumerate(chunks):
                    up_send[i, :, low:high] = nn(rb[...], wall[i, :, low:high]).astype(BF)
                    if j == 1 or not skipped:
                        message.parts[n].start()
                    else:

                        @pl.when(jnp.logical_not(is_joined))
                        def _():
                            message.parts[n].start()

                        @pl.when(jnp.logical_and(is_joined, inside(group_host(parent_near))))
                        def _():
                            to_host(parent_near).parts[n].start()

        if skipped:

            @pl.when(is_joined)
            def _():
                @pl.when(inside(group_host(1 - parent_near)))
                def _():
                    to_host(1 - parent_near).start()

                up_message(near, own_level, parent).start()

    def to_host(side):
        return hu_message(side, host_slot(side), 1 - near, group_host(side))

    def gather_level(h):
        below = lax.shift_left(jnp.int32(1), jnp.int32(h))
        for i in range(2):
            source = leaf + (1 - 2 * i) * below

            @pl.when(inside(source))
            def _():
                up_message(i, h, source).wait_recv()
                res[...] = res[...] - up_recv[h, i].astype(F32)

    gather_one.take(4)
    gather_one.send(7)
    gather_one.take(6)
    gather_one.send(8)
    gather_one.take(2, 3, 5, 7, 8)
    loads[7].wait()
    part_one = toward(first)

    @pl.when(jnp.logical_not(is_even))
    def _():
        tl_send[...] = part_one.astype(BF)
        tl_copy(leaf - 1).start()

    gather_two.take(0)
    gather_two.send(4, 3)
    gather_two.take(1)
    gather_two.send(6, 5)

    @pl.when(is_even)
    def _():
        res[...] = srhs[...].astype(F32) - part_one
        tl_copy(leaf + 1).wait_recv()
        res[...] = res[...] - tl_recv[...].astype(F32)
        climb()

    gather_two.take(4)
    gather_two.send(7)
    gather_two.take(6)
    gather_two.send(8)
    gather_two.take(2, 3, 5, 7, 8)
    part_two = toward(second)

    @pl.when(jnp.logical_and(is_even, leaf > 0))
    def _():
        tl_send[...] = part_two.astype(BF)
        tl_copy(leaf - 1).start()

    @pl.when(jnp.logical_not(is_even))
    def _():
        res[...] = srhs[...].astype(F32) - part_two

        @pl.when(leaf < n_leaf - 1)
        def _():
            tl_copy(leaf + 1).wait_recv()
            res[...] = res[...] - tl_recv[...].astype(F32)

        if skipped:

            @pl.when(is_host)
            def _():
                for slot in range(2):

                    @pl.when(has_group(slot))
                    def _():
                        hw_copy(0, slot, group_of(slot)[0]).wait_recv()

                gather_host.send(0, 1, 2)
                gather_host.take(0)
                gather_host.send(4, 3)
                gather_host.take(1)
                gather_host.send(6, 5)
                gather_host.take(4)
                gather_host.send(7)
                gather_host.take(6)
                gather_host.send(8)

        @pl.loop(0, level - is_skipped.astype(jnp.int32))
        def _(h):
            gather_level(h)

        if skipped:

            @pl.when(is_host)
            def _():
                gather_host.take(2, 3, 5, 7, 8)
                for slot in range(2):

                    @pl.when(has_group(slot))
                    def _():
                        center, reach = group_of(slot)
                        hu_message(0, slot, 0, center - reach).wait_recv()
                        hu_message(0, slot, 1, center + reach).wait_recv()
                        both = hu_recv[slot, 0].astype(F32) + hu_recv[slot, 1].astype(F32)
                        res[...] = res[...] + nn(both.astype(BF), hw[slot])

        climb()
        if skipped:

            @pl.when(is_skipped)
            def _():
                gather_level(level - 1)
                rb[...] = res[...].astype(BF)

    loads[8].wait()
    solved_sep = nt(rb[...], sinv[...]).astype(BF).astype(F32)
    target_sep = (solved_sep + snoise[...].astype(F32)).astype(BF)
    zacc[...] = nn(target_sep, sinv[...])
    if skipped:

        @pl.when(is_skipped)
        def _():
            zp_send[...] = zacc[...].astype(BF)
            for i in range(2):
                zp_message(i, leaf + (1 - 2 * i) * half_span).start()

    loads[9].wait()
    pack(n_buf, turned_slots, pkn)
    for step in range(1, n_front):
        exchange(pkn, rows_of(n2), nz_send, nz_recv, step).start()
    n2[:, own_rows, :] = pkn[front]
    for i in range(2):
        wt[i] = wall[i].T
    if skipped:

        @pl.when(is_host)
        def _():
            for slot in range(2):

                @pl.when(has_group(slot))
                def _():
                    hwt[slot] = hw[slot].T


    is_plain = jnp.logical_not(jnp.logical_or(is_skipped, is_joined))

    def take_draws(i, wanted):
        source = ancestor(i)

        @pl.when(jnp.logical_and(wanted, inside(source)))
        def _():
            dn_message(i, 0, source).wait_recv()
            zacc[...] = zacc[...] - nn(dn_recv[i], wt[i])

    take_draws(1 - near, jnp.logical_not(is_skipped))
    if skipped:

        @pl.when(is_joined)
        def _():
            zp_message(0, parent).wait_recv()
            da[...] = zp_recv[...]

        for i in range(2):

            @pl.when(jnp.logical_and(jnp.logical_not(is_plain), inside(group_host(i))))
            def _():
                v_message(0, 0, i, group_host(i)).wait_recv()

                @pl.when(is_skipped)
                def _():
                    zacc[...] = zacc[...] - dv_recv[i].astype(F32)

                @pl.when(is_joined)
                def _():
                    da[...] = (da[...].astype(F32) - dv_recv[i].astype(F32)).astype(BF)

        @pl.when(is_joined)
        def _():
            @pl.when(level + 1 == lowest)
            def _():
                da_message(leaf + (2 * near - 1) * half_span).start()

            dn_recv[near] = da[...]

    plain_last = jnp.logical_and(is_plain, inside(ancestor(near)))

    @pl.when(plain_last)
    def _():
        dn_message(near, 0, ancestor(near)).wait_recv()

    is_early = jnp.logical_and(level > 0, level < lowest)

    def early(act):
        for i in range(2):
            target = leaf + (1 - 2 * i) * half_span

            @pl.when(jnp.logical_and(is_early, inside(target)))
            def _():
                act(dn_message(i, jnp.maximum(level - 1, 0), target))

        @pl.when(is_even)
        def _():
            act(dn_message(2, 0, leaf + 1))

    has_last = jnp.logical_or(plain_last, is_joined)

    @pl.when(has_last)
    def _():
        for n, (low, high) in enumerate(chunks):
            value = zacc[:, low:high] - nn(dn_recv[near], wt[near, :, low:high])
            zacc[:, low:high] = value
            dn_send[:, low:high] = value.astype(BF)
            early(lambda message: message.parts[n].start())

    @pl.when(jnp.logical_not(has_last))
    def _():
        dn_send[...] = zacc[...].astype(BF)

    sep_out[...] = zacc[...]

    def for_level(h, act):
        below = lax.shift_left(jnp.int32(1), jnp.int32(h))
        bypassed = jnp.logical_or(
            any_of(jnp.int32(h), skipped), jnp.logical_and(is_skipped, h >= level - 2)
        )
        for i in range(2):
            target = leaf + (1 - 2 * i) * below

            @pl.when(jnp.logical_and(jnp.logical_not(bypassed), inside(target)))
            def _():
                act(dn_message(i, h, target))

    def begin(message):
        message.start()

    def left(message):
        message.wait_send()

    steps = jnp.maximum(level - lowest + 1, 0)

    @pl.loop(0, steps)
    def _(step):
        for_level(level - 1 - step, begin)

    if skipped:

        def to_group(slot):
            center, reach = group_of(slot)
            return [
                v_message(slot, which, group_side(slot), target)
                for which, target in enumerate((center - reach, center + reach, center))
            ]

        for slot in (1, 0):

            @pl.when(has_group(slot))
            def _():
                v_send[slot] = nn(dn_send[...], hwt[slot]).astype(BF)
                for message in to_group(slot):
                    message.start()

        for slot in range(2):

            @pl.when(has_group(slot))
            def _():
                for message in to_group(slot):
                    message.wait_send()

    @pl.loop(0, steps)
    def _(step):
        for_level(level - 1 - step, left)

    early(left)

    @pl.loop(steps + is_early.astype(jnp.int32), level)
    def _(step):
        for_level(level - 1 - step, begin)
        for_level(level - 1 - step, left)

    own_dup[0:HALF] = dn_send[...]
    own_dup[HALF:] = dn_send[...]

    def pulled(side, dup):
        return [
            jnp.where(low_lanes, nt(lw[side, t], dup), nt(lw[side, t + 2], dup)) for t in range(2)
        ]

    for t, value in enumerate(pulled(0, own_dup[...])):
        pull[t] = value
    for step in range(1, n_front):
        arrival(pkn, rows_of(n2), nz_send, nz_recv, step).wait_recv()

    @pl.when(jnp.logical_not(is_even))
    def _():
        dn_message(2, 0, leaf - 1).wait_recv()
        prev_dup[0:HALF] = dn_recv[2]

    @pl.when(jnp.logical_and(is_even, leaf > 0))
    def _():
        prev_dup[0:HALF] = dn_recv[0]

    @pl.when(leaf == 0)
    def _():
        prev_dup[0:HALF] = jnp.zeros((HALF, prev_dup.shape[1]), BF)

    prev_dup[HALF:] = prev_dup[0:HALF]
    for t, value in enumerate(pulled(1, prev_dup[...])):
        mixed = s2[t].astype(F32) + n2[t].astype(F32) - pull[t] - value
        mixed = jnp.where(alive[t], mixed, 0.0).astype(BF)
        drawn = jnp.where(low_lanes, tn(inv[t], mixed), tn(inv[t + 2], mixed)).astype(BF)
        for f in range(n_front):
            d2[f, t] = drawn[f * rows : f * rows + rows]

    for step in range(1, n_front):
        exchange(d2, lambda f: o2.at[f], o_send, o_recv, step).start()
    o2[front] = d2[front]
    for step in range(1, n_front):
        arrival(d2, lambda f: o2.at[f], o_send, o_recv, step).wait_recv()

    for t in range(2):
        for slab in range(n_front // 2):
            lanes = slice(slab * 128, slab * 128 + 128)
            a = o2[2 * slab, t].astype(F32)
            b = o2[2 * slab + 1, t].astype(F32)
            leaf_out[:, t, lanes] = jnp.concatenate([a[:, :HALF], b[:, :HALF]], axis=1)
            leaf_out[:, t + 2, lanes] = jnp.concatenate([a[:, HALF:], b[:, HALF:]], axis=1)

    for step in range(1, n_front):
        exchange(pk, rows_of(r2), a_send, a_recv, step).wait_send()
        exchange(pkn, rows_of(n2), nz_send, nz_recv, step).wait_send()
        exchange(d2, lambda f: o2.at[f], o_send, o_recv, step).wait_send()
    gather_inv.drain()
    gather_one.drain()
    gather_two.drain()

    @pl.when(leaf > 0)
    def _():
        tl_copy(leaf - 1).wait_send()

    for i in range(2):
        target = ancestor(i)

        @pl.when(inside(target))
        def _():
            up_message(i, own_level, target).wait_send()

    if skipped:

        @pl.when(is_joined)
        def _():
            for side in range(2):

                @pl.when(inside(group_host(side)))
                def _():
                    to_host(side).wait_send()

            @pl.when(level + 1 == lowest)
            def _():
                da_message(leaf + (2 * near - 1) * half_span).wait_send()

        @pl.when(is_skipped)
        def _():
            for i in range(2):
                zp_message(i, leaf + (1 - 2 * i) * half_span).wait_send()

                @pl.when(inside(ancestor(i)))
                def _():
                    hw_copy(i, host_slot(i), ancestor(i)).wait_send()

        @pl.when(is_host)
        def _():
            gather_host.drain()


def on_device(
    leaf_rhs,
    sep_rhs,
    leaf_noise,
    sep_noise,
    leaf_inverse,
    leaf_left,
    leaf_right,
    sep_inverse,
    sep_left,
    sep_right,
    leaf_count,
):
    n_leaf = lax.axis_size("leaf")
    n_front = lax.axis_size("front")
    depth = n_leaf.bit_length() - 1
    _, rows, slots, samples = leaf_rhs.shape
    share, width = sep_rhs.shape[1:]
    order = rows * n_front
    hbm = pl.BlockSpec(memory_space=pltpu.HBM)
    vmem = pl.BlockSpec(memory_space=pltpu.VMEM)
    dma = pltpu.SemaphoreType.DMA
    leaf_draws, sep_draws = pl.pallas_call(
        functools.partial(kernel, n_leaf, n_front, depth),
        out_shape=(
            jax.ShapeDtypeStruct((rows, slots, samples), F32),
            jax.ShapeDtypeStruct((share, width), F32),
        ),
        in_specs=[pl.BlockSpec(memory_space=pltpu.SMEM)] + [hbm] * 10,
        out_specs=(vmem, vmem),
        scratch_shapes=[
            pltpu.VMEM((rows, slots, samples), BF),
            pltpu.VMEM((rows, slots, samples), BF),
            pltpu.VMEM((slots, rows, samples), BF),
            pltpu.VMEM((n_front, 2, rows, 128), BF),
            pltpu.VMEM((n_front, 2, rows, 128), BF),
            pltpu.VMEM((2, order, 128), BF),
            pltpu.VMEM((2, order, 128), BF),
            pltpu.VMEM((slots, order, order), BF),
            pltpu.VMEM((2, slots, order, width), BF),
            pltpu.VMEM((share, width), BF),
            pltpu.VMEM((share, width), BF),
            pltpu.VMEM((width, width), BF),
            pltpu.VMEM((2, width, width), BF),
            pltpu.VMEM((2, width, width), BF),
            pltpu.VMEM((2, width, width), BF),
            pltpu.VMEM((2, width, width), BF),
            pltpu.VMEM((2, width, width), BF),
            pltpu.VMEM((2, order, 128), BF),
            pltpu.VMEM((share, width), F32),
            pltpu.VMEM((share, width), BF),
            pltpu.VMEM((share, width), F32),
            pltpu.VMEM((share, width), BF),
            pltpu.VMEM((share, width), BF),
            pltpu.VMEM((2, share, width), BF),
            pltpu.VMEM((depth, 2, share, width), BF),
            pltpu.VMEM((share, width), BF),
            pltpu.VMEM((3, share, width), BF),
            pltpu.VMEM((share, width), BF),
            pltpu.VMEM((share, width), BF),
            pltpu.VMEM((2, 2, share, width), BF),
            pltpu.VMEM((2, share, width), BF),
            pltpu.VMEM((2, share, width), BF),
            pltpu.VMEM((share, width), BF),
            pltpu.VMEM((2 * share, width), BF),
            pltpu.VMEM((2 * share, width), BF),
            pltpu.VMEM((2, order, 128), F32),
            pltpu.VMEM((n_front, 2, rows, 128), BF),
            pltpu.VMEM((n_front, 2, rows, 128), BF),
            dma((10,)),
            dma((n_front - 1,)),
            dma((n_front - 1,)),
            dma((n_front - 1,)),
            dma((n_front - 1,)),
            dma((9,)),
            dma((9,)),
            dma((2, 9)),
            dma((2, 9)),
            dma,
            dma,
            dma((2, 2)),
            dma((depth, 2, 2)),
            dma((3, depth, 2)),
            dma((3, 2)),
            dma((n_front - 1,)),
            dma((n_front - 1,)),
            dma((2,)),
            dma((2,)),
            dma((9,)),
            dma((9,)),
            dma((2, 2)),
            dma((2, 2, 2)),
            dma((2, 3, 2)),
            dma((2, 2)),
            dma((2,)),
            dma((2, 2)),
            dma((2,)),
            pltpu.SemaphoreType.REGULAR,
        ],
        compiler_params=pltpu.CompilerParams(
            collective_id=0, has_side_effects=True, vmem_limit_bytes=63 * 1024 * 1024
        ),
    )(
        leaf_count,
        leaf_rhs[0],
        leaf_noise[0],
        leaf_inverse[0],
        leaf_left[0],
        leaf_right[0],
        sep_rhs[0],
        sep_noise[0],
        sep_inverse[0],
        sep_left[0],
        sep_right[0],
    )
    return (leaf_draws[None], sep_draws[None])


def solution(mesh):
    return jax.shard_map(
        on_device,
        mesh=mesh,
        in_specs=(
            P("leaf", "front", None, None),
            P("leaf", "front", None),
            P("leaf", "front", None, None),
            P("leaf", "front", None),
            P("leaf", None, "front", None),
            P("leaf", None, "front", None),
            P("leaf", None, "front", None),
            P("leaf", None, None),
            P("leaf", None, None),
            P("leaf", None, None),
            P("leaf"),
        ),
        out_specs=(P("leaf", "front", None, None), P("leaf", "front", None)),
        check_vma=False,
    )
```

```python
import functools

import jax
import jax.numpy as jnp
from jax import lax
from jax.experimental import pallas as pl
from jax.experimental.pallas import tpu as pltpu
from jax.sharding import PartitionSpec as P

MESH = pl.DeviceIdType.MESH
BF = jnp.bfloat16
F32 = jnp.float32
HALF = 64
SKIPPED = (3, 5)


def nn(a, b):
    return lax.dot_general(a, b, (((1,), (0,)), ((), ())), preferred_element_type=F32)


def nt(a, b):
    return lax.dot_general(a, b, (((1,), (1,)), ((), ())), preferred_element_type=F32)


def tn(a, b):
    return lax.dot_general(a, b, (((0,), (0,)), ((), ())), preferred_element_type=F32)


def pack(raw_ref, block_ref, packed_ref):
    rows, slots, samples = raw_ref.shape
    for t in range(slots):
        block_ref[t] = raw_ref[:, t, :]
    for slab in range(samples // 128):
        lanes = slice(slab * 128, slab * 128 + 128)
        a = block_ref[0:2, :, lanes].reshape(2 * rows, 128)
        b = block_ref[2:4, :, lanes].reshape(2 * rows, 128)
        for core in range(2):
            part = slice(core * HALF, core * HALF + HALF)
            both = jnp.concatenate([a[:, part], b[:, part]], axis=1)
            packed_ref[2 * slab + core] = both.reshape(2, rows, 128)


def kernel(
    n_leaf,
    n_front,
    depth,
    cnt_ref,
    rhs_hbm,
    noise_hbm,
    inv_hbm,
    left_hbm,
    right_hbm,
    srhs_hbm,
    snoise_hbm,
    sinv_hbm,
    sleft_hbm,
    sright_hbm,
    leaf_out,
    sep_out,
    x_buf,
    n_buf,
    turned_slots,
    pk,
    pkn,
    r2,
    n2,
    inv,
    lw,
    srhs,
    snoise,
    sinv,
    su,
    wall,
    wt,
    hw,
    hwt,
    s2,
    res,
    rb,
    zacc,
    tl_send,
    tl_recv,
    up_send,
    up_recv,
    dn_send,
    dn_recv,
    zp_send,
    zp_recv,
    hu_recv,
    v_send,
    dv_recv,
    da,
    own_dup,
    prev_dup,
    pull,
    d2,
    o2,
    load_sem,
    a_send,
    a_recv,
    nz_send,
    nz_recv,
    gi_send,
    gi_recv,
    g_send,
    g_recv,
    tl_ssem,
    tl_rsem,
    up_ssem,
    up_rsem,
    dn_ssem,
    dn_rsem,
    o_send,
    o_recv,
    hw_ssem,
    hw_rsem,
    gh_send,
    gh_recv,
    hu_ssem,
    hu_rsem,
    v_ssem,
    dv_rsem,
    da_ssem,
    zp_ssem,
    zp_rsem,
    known_sem,
):
    leaf = lax.axis_index("leaf")
    front = lax.axis_index("front")
    chips = n_front // 2
    x = front // 2
    core = front % 2
    rows = x_buf.shape[0]
    pos = leaf + 1
    level = jnp.int32(0)
    for bit in range(1, depth + 1):
        level = level + (pos % (1 << bit) == 0).astype(jnp.int32)
    span = jnp.int32(1)
    for bit in range(1, depth + 1):
        span = jnp.where(pos % (1 << bit) == 0, jnp.int32(1 << bit), span)
    odd = leaf % 2
    is_even = odd == 0
    is_root = level == depth

    def inside(target):
        return jnp.logical_and(target >= 0, target < n_leaf)

    def any_of(value, levels):
        found = jnp.bool_(False)
        for one in levels:
            found = jnp.logical_or(found, value == one)
        return found

    skipped = tuple(one for one in SKIPPED if one < depth)
    is_skipped = any_of(level, skipped)
    is_joined = any_of(level + 1, skipped)
    joined = is_joined.astype(jnp.int32)
    near = ((pos // span) % 4 == 1).astype(jnp.int32)
    parent = leaf + (2 * near - 1) * span
    parent_near = (((parent + 1) // (2 * span)) % 4 == 1).astype(jnp.int32)
    own_level = jnp.minimum(level, depth - 1)
    half_span = jnp.maximum(span // 2, 1)
    lowest = skipped[0] if skipped else depth
    is_host = level > lowest
    is_top = leaf == n_leaf - 1
    top_hosts_two = len(skipped) == 2

    def ancestor(i):
        return leaf + (2 * i - 1) * span

    def group_host(i):
        return jnp.where(is_skipped, ancestor(i), parent + (2 * i - 1) * 2 * span)

    def host_slot(i):
        far_group = jnp.logical_or(level == skipped[-1], level + 1 == skipped[-1])
        return jnp.where(jnp.logical_and(far_group, top_hosts_two), 1, 1 - i)

    def group_of(slot):
        if slot == 0:
            return leaf - (1 << lowest), jnp.int32(1 << (lowest - 1))
        if top_hosts_two:
            other = 1 << skipped[-1]
            return (
                jnp.where(is_top, leaf - other, leaf + (1 << lowest)),
                jnp.where(is_top, jnp.int32(other // 2), jnp.int32(1 << (lowest - 1))),
            )
        return leaf + (1 << lowest), jnp.int32(1 << (lowest - 1))

    def group_side(slot):
        if slot == 0:
            return jnp.int32(1)
        return is_top.astype(jnp.int32)

    def has_group(slot):
        return jnp.logical_and(is_host, inside(group_of(slot)[0]))

    def load(i, src, dst):
        return pltpu.make_async_copy(src, dst, load_sem.at[i])

    own_rows = pl.ds(pl.multiple_of(front * rows, rows), rows)
    loads = [
        load(0, rhs_hbm, x_buf),
        load(1, inv_hbm, inv.at[:, own_rows, :]),
        load(2, right_hbm, lw.at[0, :, own_rows, :]),
        load(3, left_hbm, lw.at[1, :, own_rows, :]),
        load(4, sinv_hbm, sinv),
        load(5, sleft_hbm, su.at[0]),
        load(6, sright_hbm, su.at[1]),
        load(7, srhs_hbm, srhs),
        load(8, snoise_hbm, snoise),
        load(9, noise_hbm, n_buf),
    ]
    for copy in loads:
        copy.start()

    barrier = pltpu.get_barrier_semaphore()
    partners = jnp.int32(n_front - 1)
    for step in range(1, n_front):
        pl.semaphore_signal(
            barrier, inc=1, device_id={"front": (front + step) % n_front}, device_id_type=MESH
        )
    greeted = [(leaf - 1, leaf > 0), (leaf + 1, leaf < n_leaf - 1)]
    if skipped:
        greeted += [
            (parent, is_joined),
            (leaf - half_span, is_skipped),
            (leaf + half_span, is_skipped),
            (group_host(0), jnp.logical_and(is_joined, inside(group_host(0)))),
            (group_host(1), jnp.logical_and(is_joined, inside(group_host(1)))),
        ]
        for slot in range(2):
            center, reach = group_of(slot)
            greeted += [(center - reach, has_group(slot)), (center + reach, has_group(slot))]
    for target, reached in greeted:
        partners = partners + reached.astype(jnp.int32)

        @pl.when(reached)
        def _():
            pl.semaphore_signal(barrier, inc=1, device_id={"leaf": target}, device_id_type=MESH)

    loads[0].wait()
    pack(x_buf, turned_slots, pk)
    loads[4].wait()
    loads[5].wait()
    wall[0] = tn(sinv[...], su[0]).astype(BF)
    pl.semaphore_wait(barrier, partners)

    width = srhs.shape[1]
    share_rows = width // n_front
    share_here = pl.ds(pl.multiple_of(front * share_rows, share_rows), share_rows)

    def hw_copy(i, slot, target):
        return pltpu.make_async_remote_copy(
            src_ref=wall.at[i, share_here],
            dst_ref=hw.at[slot, share_here],
            send_sem=hw_ssem.at[i],
            recv_sem=hw_rsem.at[slot],
            device_id={"leaf": target},
            device_id_type=MESH,
        )

    if skipped:

        @pl.when(is_joined)
        def _():
            pl.semaphore_signal(known_sem, inc=1, device_id={"leaf": parent}, device_id_type=MESH)

    def exchange(src, dst_at, sends, recvs, step):
        peer = (front + step) % n_front
        return pltpu.make_async_remote_copy(
            src_ref=src.at[peer],
            dst_ref=dst_at(front),
            send_sem=sends.at[step - 1],
            recv_sem=recvs.at[step - 1],
            device_id={"front": peer},
            device_id_type=MESH,
        )

    def arrival(src, dst_at, sends, recvs, step):
        peer = (front + n_front - step) % n_front
        return pltpu.make_async_remote_copy(
            src_ref=src.at[peer],
            dst_ref=dst_at(peer),
            send_sem=sends.at[step - 1],
            recv_sem=recvs.at[step - 1],
            device_id={"front": peer},
            device_id_type=MESH,
        )

    def rows_of(ref):
        return lambda f: ref.at[:, pl.ds(pl.multiple_of(f * rows, rows), rows), :]

    def piece(buf, dx, flip, low, high):
        chip = (x + dx + chips) % chips
        who = 2 * chip + (1 - core if flip else core)
        count, order, _ = buf.shape
        low, high = low * count // 4, high * count // 4
        some = order // n_front
        return buf.at[low:high, pl.ds(pl.multiple_of(who * some, some), some), :]

    routes = [
        (0, 0, 4, 1, False),
        (0, 0, 4, -1, False),
        (0, 0, 4, 0, True),
        (-1, 0, 4, 0, True),
        (-1, 0, 2, 1, False),
        (1, 0, 4, 0, True),
        (1, 2, 4, -1, False),
        (2, 0, 2, 0, True),
        (2, 2, 4, 0, True),
    ]

    def route(buf, sends, recvs, i):
        dx, low, high, to, flip = routes[i]
        chip = (x + to + chips) % chips
        peer = 2 * chip + (1 - core if flip else core)
        block = piece(buf, dx, False, low, high)
        return pltpu.make_async_remote_copy(
            src_ref=block,
            dst_ref=block,
            send_sem=sends.at[i],
            recv_sem=recvs.at[i],
            device_id={"front": peer},
            device_id_type=MESH,
        )

    def route_arrival(buf, sends, recvs, i):
        dx, low, high, to, flip = routes[i]
        chip = (x + to + chips) % chips
        peer = 2 * chip + (1 - core if flip else core)
        block = piece(buf, dx - to, flip, low, high)
        return pltpu.make_async_remote_copy(
            src_ref=block,
            dst_ref=block,
            send_sem=sends.at[i],
            recv_sem=recvs.at[i],
            device_id={"front": peer},
            device_id_type=MESH,
        )

    class Gather:
        def __init__(self, buf, sends, recvs):
            self.args = (buf, sends, recvs)

        def send(self, *which):
            for i in which:
                route(*self.args, i).start()

        def take(self, *which):
            for i in which:
                route_arrival(*self.args, i).wait_recv()

        def drain(self):
            for i in range(len(routes)):
                route(*self.args, i).wait_send()

    first = odd
    second = 1 - odd
    gather_inv = Gather(inv, gi_send, gi_recv)
    gather_host = Gather(hw, gh_send, gh_recv)
    gather_one = Gather(lw.at[first], g_send.at[0], g_recv.at[0])
    gather_two = Gather(lw.at[second], g_send.at[1], g_recv.at[1])

    for step in range(1, n_front):
        exchange(pk, rows_of(r2), a_send, a_recv, step).start()
    loads[1].wait()
    gather_inv.send(0, 1, 2)
    loads[2].wait()
    loads[3].wait()
    gather_one.send(0, 1, 2)
    r2[:, own_rows, :] = pk[front]

    loads[6].wait()
    wall[1] = tn(sinv[...], su[1]).astype(BF)
    gather_inv.take(0)
    gather_inv.send(4, 3)
    gather_inv.take(1)
    gather_inv.send(6, 5)
    gather_two.send(0, 1, 2)
    if skipped:

        @pl.when(is_skipped)
        def _():
            pl.semaphore_wait(known_sem, 2)
            for i in range(2):

                @pl.when(inside(ancestor(i)))
                def _():
                    hw_copy(i, host_slot(i), ancestor(i)).start()

    gather_one.take(0)
    gather_one.send(4, 3)
    gather_one.take(1)
    gather_one.send(6, 5)
    gather_inv.take(4)
    gather_inv.send(7)
    gather_inv.take(6)
    gather_inv.send(8)
    for step in range(1, n_front):
        arrival(pk, rows_of(r2), a_send, a_recv, step).wait_recv()
    gather_inv.take(2, 3, 5, 7, 8)

    live = cnt_ref[0]
    low_lanes = lax.broadcasted_iota(jnp.int32, (1, 128), 1) < HALF
    alive = [
        jnp.logical_or(
            jnp.logical_and(low_lanes, t < live),
            jnp.logical_and(jnp.logical_not(low_lanes), t + 2 < live),
        )
        for t in range(2)
    ]
    for t in range(2):
        block = r2[t]
        solved = jnp.where(low_lanes, nn(inv[t], block), nn(inv[t + 2], block))
        s2[t] = jnp.where(alive[t], solved, 0.0).astype(BF)

    def toward(side):
        total = jnp.zeros((HALF, srhs.shape[1]), F32)
        for t in range(2):
            turned = s2[t].T
            total = total + nn(turned[0:HALF], lw[side, t])
            total = total + nn(turned[HALF:], lw[side, t + 2])
        return total

    def tl_copy(target):
        return pltpu.make_async_remote_copy(
            src_ref=tl_send,
            dst_ref=tl_recv,
            send_sem=tl_ssem,
            recv_sem=tl_rsem,
            device_id={"leaf": target},
            device_id_type=MESH,
        )

    chunks = [(0, 256), (256, width)] if width > 256 else [(0, width)]

    class Message:
        def __init__(self, src, dst, sends, recvs, target):
            self.parts = [
                pltpu.make_async_remote_copy(
                    src_ref=src.at[:, low:high],
                    dst_ref=dst.at[:, low:high],
                    send_sem=sends.at[n],
                    recv_sem=recvs.at[n],
                    device_id={"leaf": target},
                    device_id_type=MESH,
                )
                for n, (low, high) in enumerate(chunks)
            ]

        def start(self):
            for part in self.parts:
                part.start()

        def wait_send(self):
            for part in self.parts:
                part.wait_send()

        def wait_recv(self):
            for part in self.parts:
                part.wait_recv()

    def up_message(i, h, target):
        return Message(up_send.at[i], up_recv.at[h, i], up_ssem.at[i], up_rsem.at[h, i], target)

    def hu_message(i, slot, which, target):
        return Message(
            up_send.at[near], hu_recv.at[slot, which], hu_ssem.at[i], hu_rsem.at[slot, which], target
        )

    def dn_message(i, h, target):
        return Message(dn_send, dn_recv.at[i], dn_ssem.at[i, h], dn_rsem.at[i], target)

    def v_message(slot, which, side, target):
        return Message(
            v_send.at[slot], dv_recv.at[side], v_ssem.at[slot, which], dv_rsem.at[side], target
        )

    def da_message(target):
        return Message(da, dn_recv.at[near], da_ssem, dn_rsem.at[near], target)

    def zp_message(i, target):
        return Message(zp_send, zp_recv, zp_ssem.at[i], zp_rsem, target)

    def climb():
        rb[...] = res[...].astype(BF)
        for j in range(2):
            i = near if j == 0 else 1 - near
            target = ancestor(i)

            @pl.when(inside(target))
            def _():
                message = up_message(i, own_level, target)
                for n, (low, high) in enumerate(chunks):
                    up_send[i, :, low:high] = nn(rb[...], wall[i, :, low:high]).astype(BF)
                    if j == 1 or not skipped:
                        message.parts[n].start()
                    else:

                        @pl.when(jnp.logical_not(is_joined))
                        def _():
                            message.parts[n].start()

                        @pl.when(jnp.logical_and(is_joined, inside(group_host(parent_near))))
                        def _():
                            to_host(parent_near).parts[n].start()

        if skipped:

            @pl.when(is_joined)
            def _():
                @pl.when(inside(group_host(1 - parent_near)))
                def _():
                    to_host(1 - parent_near).start()

                up_message(near, own_level, parent).start()

    def to_host(side):
        return hu_message(side, host_slot(side), 1 - near, group_host(side))

    def gather_level(h):
        below = lax.shift_left(jnp.int32(1), jnp.int32(h))
        for i in range(2):
            source = leaf + (1 - 2 * i) * below

            @pl.when(inside(source))
            def _():
                up_message(i, h, source).wait_recv()
                res[...] = res[...] - up_recv[h, i].astype(F32)

    gather_one.take(4)
    gather_one.send(7)
    gather_one.take(6)
    gather_one.send(8)
    gather_one.take(2, 3, 5, 7, 8)
    loads[7].wait()
    part_one = toward(first)

    @pl.when(jnp.logical_not(is_even))
    def _():
        tl_send[...] = part_one.astype(BF)
        tl_copy(leaf - 1).start()

    gather_two.take(0)
    gather_two.send(4, 3)
    gather_two.take(1)
    gather_two.send(6, 5)

    @pl.when(is_even)
    def _():
        res[...] = srhs[...].astype(F32) - part_one
        tl_copy(leaf + 1).wait_recv()
        res[...] = res[...] - tl_recv[...].astype(F32)
        climb()

    gather_two.take(4)
    gather_two.send(7)
    gather_two.take(6)
    gather_two.send(8)
    gather_two.take(2, 3, 5, 7, 8)
    part_two = toward(second)

    @pl.when(jnp.logical_and(is_even, leaf > 0))
    def _():
        tl_send[...] = part_two.astype(BF)
        tl_copy(leaf - 1).start()

    @pl.when(jnp.logical_not(is_even))
    def _():
        res[...] = srhs[...].astype(F32) - part_two

        @pl.when(leaf < n_leaf - 1)
        def _():
            tl_copy(leaf + 1).wait_recv()
            res[...] = res[...] - tl_recv[...].astype(F32)

        if skipped:

            @pl.when(is_host)
            def _():
                for slot in range(2):

                    @pl.when(has_group(slot))
                    def _():
                        hw_copy(0, slot, group_of(slot)[0]).wait_recv()

                gather_host.send(0, 1, 2)
                gather_host.take(0)
                gather_host.send(4, 3)
                gather_host.take(1)
                gather_host.send(6, 5)
                gather_host.take(4)
                gather_host.send(7)
                gather_host.take(6)
                gather_host.send(8)

        @pl.when(is_root)
        def _():
            loads[8].wait()
            su[0] = tn(sinv[...], sinv[...]).astype(BF)
            zacc[...] = nn(snoise[...], sinv[...])

        @pl.loop(0, level - is_skipped.astype(jnp.int32))
        def _(h):
            gather_level(h)

        if skipped:

            @pl.when(is_host)
            def _():
                gather_host.take(2, 3, 5, 7, 8)
                for slot in range(2):

                    @pl.when(has_group(slot))
                    def _():
                        center, reach = group_of(slot)
                        hu_message(0, slot, 0, center - reach).wait_recv()
                        hu_message(0, slot, 1, center + reach).wait_recv()
                        both = hu_recv[slot, 0].astype(F32) + hu_recv[slot, 1].astype(F32)
                        res[...] = res[...] + nn(both.astype(BF), hw[slot])

        climb()
        if skipped:

            @pl.when(is_skipped)
            def _():
                gather_level(level - 1)
                rb[...] = res[...].astype(BF)

    @pl.when(is_root)
    def _():
        zacc[...] = zacc[...] + nn(rb[...], su[0])

    @pl.when(jnp.logical_not(is_root))
    def _():
        loads[8].wait()
        solved_sep = nt(rb[...], sinv[...]).astype(BF).astype(F32)
        target_sep = (solved_sep + snoise[...].astype(F32)).astype(BF)
        zacc[...] = nn(target_sep, sinv[...])

    if skipped:

        @pl.when(is_skipped)
        def _():
            zp_send[...] = zacc[...].astype(BF)
            for i in range(2):
                zp_message(i, leaf + (1 - 2 * i) * half_span).start()

    loads[9].wait()
    pack(n_buf, turned_slots, pkn)
    for step in range(1, n_front):
        exchange(pkn, rows_of(n2), nz_send, nz_recv, step).start()
    n2[:, own_rows, :] = pkn[front]
    for i in range(2):
        wt[i] = wall[i].T
    if skipped:

        @pl.when(is_host)
        def _():
            for slot in range(2):

                @pl.when(has_group(slot))
                def _():
                    hwt[slot] = hw[slot].T


    is_plain = jnp.logical_not(jnp.logical_or(is_skipped, is_joined))

    def take_draws(i, wanted):
        source = ancestor(i)

        @pl.when(jnp.logical_and(wanted, inside(source)))
        def _():
            dn_message(i, 0, source).wait_recv()
            zacc[...] = zacc[...] - nn(dn_recv[i], wt[i])

    take_draws(1 - near, jnp.logical_not(is_skipped))
    if skipped:

        @pl.when(is_joined)
        def _():
            zp_message(0, parent).wait_recv()
            da[...] = zp_recv[...]

        for i in range(2):

            @pl.when(jnp.logical_and(jnp.logical_not(is_plain), inside(group_host(i))))
            def _():
                v_message(0, 0, i, group_host(i)).wait_recv()

                @pl.when(is_skipped)
                def _():
                    zacc[...] = zacc[...] - dv_recv[i].astype(F32)

                @pl.when(is_joined)
                def _():
                    da[...] = (da[...].astype(F32) - dv_recv[i].astype(F32)).astype(BF)

        @pl.when(is_joined)
        def _():
            @pl.when(level + 1 == lowest)
            def _():
                da_message(leaf + (2 * near - 1) * half_span).start()

            dn_recv[near] = da[...]

    plain_last = jnp.logical_and(is_plain, inside(ancestor(near)))

    @pl.when(plain_last)
    def _():
        dn_message(near, 0, ancestor(near)).wait_recv()

    is_early = jnp.logical_and(level > 0, level < lowest)

    def early(act):
        for i in range(2):
            target = leaf + (1 - 2 * i) * half_span

            @pl.when(jnp.logical_and(is_early, inside(target)))
            def _():
                act(dn_message(i, jnp.maximum(level - 1, 0), target))

        @pl.when(is_even)
        def _():
            act(dn_message(2, 0, leaf + 1))

    has_last = jnp.logical_or(plain_last, is_joined)

    @pl.when(has_last)
    def _():
        for n, (low, high) in enumerate(chunks):
            value = zacc[:, low:high] - nn(dn_recv[near], wt[near, :, low:high])
            zacc[:, low:high] = value
            dn_send[:, low:high] = value.astype(BF)
            early(lambda message: message.parts[n].start())

    @pl.when(jnp.logical_not(has_last))
    def _():
        dn_send[...] = zacc[...].astype(BF)

    sep_out[...] = zacc[...]

    def for_level(h, act):
        below = lax.shift_left(jnp.int32(1), jnp.int32(h))
        bypassed = jnp.logical_or(
            any_of(jnp.int32(h), skipped), jnp.logical_and(is_skipped, h >= level - 2)
        )
        for i in range(2):
            target = leaf + (1 - 2 * i) * below

            @pl.when(jnp.logical_and(jnp.logical_not(bypassed), inside(target)))
            def _():
                act(dn_message(i, h, target))

    def begin(message):
        message.start()

    def left(message):
        message.wait_send()

    steps = jnp.maximum(level - lowest + 1, 0)

    @pl.loop(0, steps)
    def _(step):
        for_level(level - 1 - step, begin)

    if skipped:

        def to_group(slot):
            center, reach = group_of(slot)
            return [
                v_message(slot, which, group_side(slot), target)
                for which, target in enumerate((center - reach, center + reach, center))
            ]

        for slot in (1, 0):

            @pl.when(has_group(slot))
            def _():
                v_send[slot] = nn(dn_send[...], hwt[slot]).astype(BF)
                for message in to_group(slot):
                    message.start()

        for slot in range(2):

            @pl.when(has_group(slot))
            def _():
                for message in to_group(slot):
                    message.wait_send()

    @pl.loop(0, steps)
    def _(step):
        for_level(level - 1 - step, left)

    early(left)

    @pl.loop(steps + is_early.astype(jnp.int32), level)
    def _(step):
        for_level(level - 1 - step, begin)
        for_level(level - 1 - step, left)

    own_dup[0:HALF] = dn_send[...]
    own_dup[HALF:] = dn_send[...]

    def pulled(side, dup):
        return [
            jnp.where(low_lanes, nt(lw[side, t], dup), nt(lw[side, t + 2], dup)) for t in range(2)
        ]

    for t, value in enumerate(pulled(0, own_dup[...])):
        pull[t] = value
    for step in range(1, n_front):
        arrival(pkn, rows_of(n2), nz_send, nz_recv, step).wait_recv()

    @pl.when(jnp.logical_not(is_even))
    def _():
        dn_message(2, 0, leaf - 1).wait_recv()
        prev_dup[0:HALF] = dn_recv[2]

    @pl.when(jnp.logical_and(is_even, leaf > 0))
    def _():
        prev_dup[0:HALF] = dn_recv[0]

    @pl.when(leaf == 0)
    def _():
        prev_dup[0:HALF] = jnp.zeros((HALF, prev_dup.shape[1]), BF)

    prev_dup[HALF:] = prev_dup[0:HALF]
    for t, value in enumerate(pulled(1, prev_dup[...])):
        mixed = s2[t].astype(F32) + n2[t].astype(F32) - pull[t] - value
        mixed = jnp.where(alive[t], mixed, 0.0).astype(BF)
        drawn = jnp.where(low_lanes, tn(inv[t], mixed), tn(inv[t + 2], mixed)).astype(BF)
        for f in range(n_front):
            d2[f, t] = drawn[f * rows : f * rows + rows]

    for step in range(1, n_front):
        exchange(d2, lambda f: o2.at[f], o_send, o_recv, step).start()
    o2[front] = d2[front]
    for step in range(1, n_front):
        arrival(d2, lambda f: o2.at[f], o_send, o_recv, step).wait_recv()

    for t in range(2):
        for slab in range(n_front // 2):
            lanes = slice(slab * 128, slab * 128 + 128)
            a = o2[2 * slab, t].astype(F32)
            b = o2[2 * slab + 1, t].astype(F32)
            leaf_out[:, t, lanes] = jnp.concatenate([a[:, :HALF], b[:, :HALF]], axis=1)
            leaf_out[:, t + 2, lanes] = jnp.concatenate([a[:, HALF:], b[:, HALF:]], axis=1)

    for step in range(1, n_front):
        exchange(pk, rows_of(r2), a_send, a_recv, step).wait_send()
        exchange(pkn, rows_of(n2), nz_send, nz_recv, step).wait_send()
        exchange(d2, lambda f: o2.at[f], o_send, o_recv, step).wait_send()
    gather_inv.drain()
    gather_one.drain()
    gather_two.drain()

    @pl.when(leaf > 0)
    def _():
        tl_copy(leaf - 1).wait_send()

    for i in range(2):
        target = ancestor(i)

        @pl.when(inside(target))
        def _():
            up_message(i, own_level, target).wait_send()

    if skipped:

        @pl.when(is_joined)
        def _():
            for side in range(2):

                @pl.when(inside(group_host(side)))
                def _():
                    to_host(side).wait_send()

            @pl.when(level + 1 == lowest)
            def _():
                da_message(leaf + (2 * near - 1) * half_span).wait_send()

        @pl.when(is_skipped)
        def _():
            for i in range(2):
                zp_message(i, leaf + (1 - 2 * i) * half_span).wait_send()

                @pl.when(inside(ancestor(i)))
                def _():
                    hw_copy(i, host_slot(i), ancestor(i)).wait_send()

        @pl.when(is_host)
        def _():
            gather_host.drain()


def hand_over(leaf_in, sep_in, leaf_ref, sep_ref, sems):
    copies = [
        pltpu.make_async_copy(leaf_in, leaf_ref, sems.at[0]),
        pltpu.make_async_copy(sep_in, sep_ref, sems.at[1]),
    ]
    for copy in copies:
        copy.start()
    for copy in copies:
        copy.wait()


def on_device(
    leaf_rhs,
    sep_rhs,
    leaf_noise,
    sep_noise,
    leaf_inverse,
    leaf_left,
    leaf_right,
    sep_inverse,
    sep_left,
    sep_right,
    leaf_count,
):
    n_leaf = lax.axis_size("leaf")
    n_front = lax.axis_size("front")
    depth = n_leaf.bit_length() - 1
    _, rows, slots, samples = leaf_rhs.shape
    share, width = sep_rhs.shape[1:]
    order = rows * n_front
    hbm = pl.BlockSpec(memory_space=pltpu.HBM)
    vmem = pl.BlockSpec(memory_space=pltpu.VMEM)
    dma = pltpu.SemaphoreType.DMA
    leaf_draws, sep_draws = pl.pallas_call(
        functools.partial(kernel, n_leaf, n_front, depth),
        out_shape=(
            jax.ShapeDtypeStruct((rows, slots, samples), F32),
            jax.ShapeDtypeStruct((share, width), F32),
        ),
        in_specs=[pl.BlockSpec(memory_space=pltpu.SMEM)] + [hbm] * 10,
        out_specs=(vmem, vmem),
        scratch_shapes=[
            pltpu.VMEM((rows, slots, samples), BF),
            pltpu.VMEM((rows, slots, samples), BF),
            pltpu.VMEM((slots, rows, samples), BF),
            pltpu.VMEM((n_front, 2, rows, 128), BF),
            pltpu.VMEM((n_front, 2, rows, 128), BF),
            pltpu.VMEM((2, order, 128), BF),
            pltpu.VMEM((2, order, 128), BF),
            pltpu.VMEM((slots, order, order), BF),
            pltpu.VMEM((2, slots, order, width), BF),
            pltpu.VMEM((share, width), BF),
            pltpu.VMEM((share, width), BF),
            pltpu.VMEM((width, width), BF),
            pltpu.VMEM((2, width, width), BF),
            pltpu.VMEM((2, width, width), BF),
            pltpu.VMEM((2, width, width), BF),
            pltpu.VMEM((2, width, width), BF),
            pltpu.VMEM((2, width, width), BF),
            pltpu.VMEM((2, order, 128), BF),
            pltpu.VMEM((share, width), F32),
            pltpu.VMEM((share, width), BF),
            pltpu.VMEM((share, width), F32),
            pltpu.VMEM((share, width), BF),
            pltpu.VMEM((share, width), BF),
            pltpu.VMEM((2, share, width), BF),
            pltpu.VMEM((depth, 2, share, width), BF),
            pltpu.VMEM((share, width), BF),
            pltpu.VMEM((3, share, width), BF),
            pltpu.VMEM((share, width), BF),
            pltpu.VMEM((share, width), BF),
            pltpu.VMEM((2, 2, share, width), BF),
            pltpu.VMEM((2, share, width), BF),
            pltpu.VMEM((2, share, width), BF),
            pltpu.VMEM((share, width), BF),
            pltpu.VMEM((2 * share, width), BF),
            pltpu.VMEM((2 * share, width), BF),
            pltpu.VMEM((2, order, 128), F32),
            pltpu.VMEM((n_front, 2, rows, 128), BF),
            pltpu.VMEM((n_front, 2, rows, 128), BF),
            dma((10,)),
            dma((n_front - 1,)),
            dma((n_front - 1,)),
            dma((n_front - 1,)),
            dma((n_front - 1,)),
            dma((9,)),
            dma((9,)),
            dma((2, 9)),
            dma((2, 9)),
            dma,
            dma,
            dma((2, 2)),
            dma((depth, 2, 2)),
            dma((3, depth, 2)),
            dma((3, 2)),
            dma((n_front - 1,)),
            dma((n_front - 1,)),
            dma((2,)),
            dma((2,)),
            dma((9,)),
            dma((9,)),
            dma((2, 2)),
            dma((2, 2, 2)),
            dma((2, 3, 2)),
            dma((2, 2)),
            dma((2,)),
            dma((2, 2)),
            dma((2,)),
            pltpu.SemaphoreType.REGULAR,
        ],
        compiler_params=pltpu.CompilerParams(
            collective_id=0, has_side_effects=True, vmem_limit_bytes=63 * 1024 * 1024
        ),
    )(
        leaf_count,
        leaf_rhs[0],
        leaf_noise[0],
        leaf_inverse[0],
        leaf_left[0],
        leaf_right[0],
        sep_rhs[0],
        sep_noise[0],
        sep_inverse[0],
        sep_left[0],
        sep_right[0],
    )
    leaf_draws, sep_draws = pl.pallas_call(
        hand_over,
        out_shape=(
            jax.ShapeDtypeStruct(leaf_draws.shape, F32),
            jax.ShapeDtypeStruct(sep_draws.shape, F32),
        ),
        in_specs=[hbm, hbm],
        out_specs=(hbm, hbm),
        scratch_shapes=[dma((2,))],
        compiler_params=pltpu.CompilerParams(vmem_limit_bytes=63 * 1024 * 1024),
    )(leaf_draws, sep_draws)
    return (leaf_draws[None], sep_draws[None])


def solution(mesh):
    return jax.shard_map(
        on_device,
        mesh=mesh,
        in_specs=(
            P("leaf", "front", None, None),
            P("leaf", "front", None),
            P("leaf", "front", None, None),
            P("leaf", "front", None),
            P("leaf", None, "front", None),
            P("leaf", None, "front", None),
            P("leaf", None, "front", None),
            P("leaf", None, None),
            P("leaf", None, None),
            P("leaf", None, None),
            P("leaf"),
        ),
        out_specs=(P("leaf", "front", None, None), P("leaf", "front", None)),
        check_vma=False,
    )
```

```python
import functools

import jax
import jax.numpy as jnp
from jax import lax
from jax.experimental import pallas as pl
from jax.experimental.pallas import tpu as pltpu
from jax.sharding import PartitionSpec as P

MESH = pl.DeviceIdType.MESH
BF = jnp.bfloat16
F32 = jnp.float32
HALF = 64
SKIPPED = (3, 5)


def nn(a, b):
    return lax.dot_general(a, b, (((1,), (0,)), ((), ())), preferred_element_type=F32)


def nt(a, b):
    return lax.dot_general(a, b, (((1,), (1,)), ((), ())), preferred_element_type=F32)


def tn(a, b):
    return lax.dot_general(a, b, (((0,), (0,)), ((), ())), preferred_element_type=F32)


def pack(raw_ref, block_ref, packed_ref):
    rows, slots, samples = raw_ref.shape
    for t in range(slots):
        block_ref[t] = raw_ref[:, t, :]
    for slab in range(samples // 128):
        lanes = slice(slab * 128, slab * 128 + 128)
        a = block_ref[0:2, :, lanes].reshape(2 * rows, 128)
        b = block_ref[2:4, :, lanes].reshape(2 * rows, 128)
        for core in range(2):
            part = slice(core * HALF, core * HALF + HALF)
            both = jnp.concatenate([a[:, part], b[:, part]], axis=1)
            packed_ref[2 * slab + core] = both.reshape(2, rows, 128)


def kernel(
    n_leaf,
    n_front,
    depth,
    cnt_ref,
    rhs_hbm,
    noise_hbm,
    inv_hbm,
    left_hbm,
    right_hbm,
    srhs_hbm,
    snoise_hbm,
    sinv_hbm,
    sleft_hbm,
    sright_hbm,
    leaf_out,
    sep_high,
    sep_low,
    x_buf,
    n_buf,
    turned_slots,
    pk,
    pkn,
    r2,
    n2,
    inv,
    lw,
    srhs,
    snoise,
    sinv,
    su,
    wall,
    wt,
    hw,
    hwt,
    s2,
    res,
    rb,
    zacc,
    tl_send,
    tl_recv,
    up_send,
    up_recv,
    dn_send,
    dn_recv,
    zp_send,
    zp_recv,
    hu_recv,
    v_send,
    dv_recv,
    da,
    own_dup,
    prev_dup,
    pull,
    d2,
    o2,
    load_sem,
    a_send,
    a_recv,
    nz_send,
    nz_recv,
    gi_send,
    gi_recv,
    g_send,
    g_recv,
    tl_ssem,
    tl_rsem,
    up_ssem,
    up_rsem,
    dn_ssem,
    dn_rsem,
    o_send,
    o_recv,
    hw_ssem,
    hw_rsem,
    gh_send,
    gh_recv,
    hu_ssem,
    hu_rsem,
    v_ssem,
    dv_rsem,
    da_ssem,
    zp_ssem,
    zp_rsem,
    known_sem,
):
    leaf = lax.axis_index("leaf")
    front = lax.axis_index("front")
    chips = n_front // 2
    x = front // 2
    core = front % 2
    rows = x_buf.shape[0]
    pos = leaf + 1
    level = jnp.int32(0)
    for bit in range(1, depth + 1):
        level = level + (pos % (1 << bit) == 0).astype(jnp.int32)
    span = jnp.int32(1)
    for bit in range(1, depth + 1):
        span = jnp.where(pos % (1 << bit) == 0, jnp.int32(1 << bit), span)
    odd = leaf % 2
    is_even = odd == 0
    is_root = level == depth

    def inside(target):
        return jnp.logical_and(target >= 0, target < n_leaf)

    def any_of(value, levels):
        found = jnp.bool_(False)
        for one in levels:
            found = jnp.logical_or(found, value == one)
        return found

    skipped = tuple(one for one in SKIPPED if one < depth)
    is_skipped = any_of(level, skipped)
    is_joined = any_of(level + 1, skipped)
    joined = is_joined.astype(jnp.int32)
    near = ((pos // span) % 4 == 1).astype(jnp.int32)
    parent = leaf + (2 * near - 1) * span
    parent_near = (((parent + 1) // (2 * span)) % 4 == 1).astype(jnp.int32)
    own_level = jnp.minimum(level, depth - 1)
    half_span = jnp.maximum(span // 2, 1)
    lowest = skipped[0] if skipped else depth
    is_host = level > lowest
    is_top = leaf == n_leaf - 1
    top_hosts_two = len(skipped) == 2

    def ancestor(i):
        return leaf + (2 * i - 1) * span

    def group_host(i):
        return jnp.where(is_skipped, ancestor(i), parent + (2 * i - 1) * 2 * span)

    def host_slot(i):
        far_group = jnp.logical_or(level == skipped[-1], level + 1 == skipped[-1])
        return jnp.where(jnp.logical_and(far_group, top_hosts_two), 1, 1 - i)

    def group_of(slot):
        if slot == 0:
            return leaf - (1 << lowest), jnp.int32(1 << (lowest - 1))
        if top_hosts_two:
            other = 1 << skipped[-1]
            return (
                jnp.where(is_top, leaf - other, leaf + (1 << lowest)),
                jnp.where(is_top, jnp.int32(other // 2), jnp.int32(1 << (lowest - 1))),
            )
        return leaf + (1 << lowest), jnp.int32(1 << (lowest - 1))

    def group_side(slot):
        if slot == 0:
            return jnp.int32(1)
        return is_top.astype(jnp.int32)

    def has_group(slot):
        return jnp.logical_and(is_host, inside(group_of(slot)[0]))

    def load(i, src, dst):
        return pltpu.make_async_copy(src, dst, load_sem.at[i])

    own_rows = pl.ds(pl.multiple_of(front * rows, rows), rows)
    loads = [
        load(0, rhs_hbm, x_buf),
        load(1, inv_hbm, inv.at[:, own_rows, :]),
        load(2, right_hbm, lw.at[0, :, own_rows, :]),
        load(3, left_hbm, lw.at[1, :, own_rows, :]),
        load(4, sinv_hbm, sinv),
        load(5, sleft_hbm, su.at[0]),
        load(6, sright_hbm, su.at[1]),
        load(7, srhs_hbm, srhs),
        load(8, snoise_hbm, snoise),
        load(9, noise_hbm, n_buf),
    ]
    for copy in loads:
        copy.start()

    barrier = pltpu.get_barrier_semaphore()
    partners = jnp.int32(n_front - 1)
    for step in range(1, n_front):
        pl.semaphore_signal(
            barrier, inc=1, device_id={"front": (front + step) % n_front}, device_id_type=MESH
        )
    greeted = [(leaf - 1, leaf > 0), (leaf + 1, leaf < n_leaf - 1)]
    if skipped:
        greeted += [
            (parent, is_joined),
            (leaf - half_span, is_skipped),
            (leaf + half_span, is_skipped),
            (group_host(0), jnp.logical_and(is_joined, inside(group_host(0)))),
            (group_host(1), jnp.logical_and(is_joined, inside(group_host(1)))),
        ]
        for slot in range(2):
            center, reach = group_of(slot)
            greeted += [(center - reach, has_group(slot)), (center + reach, has_group(slot))]
    for target, reached in greeted:
        partners = partners + reached.astype(jnp.int32)

        @pl.when(reached)
        def _():
            pl.semaphore_signal(barrier, inc=1, device_id={"leaf": target}, device_id_type=MESH)

    loads[0].wait()
    pack(x_buf, turned_slots, pk)
    loads[4].wait()
    loads[5].wait()
    wall[0] = tn(sinv[...], su[0]).astype(BF)
    pl.semaphore_wait(barrier, partners)

    width = srhs.shape[1]
    share_rows = width // n_front
    share_here = pl.ds(pl.multiple_of(front * share_rows, share_rows), share_rows)

    def hw_copy(i, slot, target):
        return pltpu.make_async_remote_copy(
            src_ref=wall.at[i, share_here],
            dst_ref=hw.at[slot, share_here],
            send_sem=hw_ssem.at[i],
            recv_sem=hw_rsem.at[slot],
            device_id={"leaf": target},
            device_id_type=MESH,
        )

    if skipped:

        @pl.when(is_joined)
        def _():
            pl.semaphore_signal(known_sem, inc=1, device_id={"leaf": parent}, device_id_type=MESH)

    def exchange(src, dst_at, sends, recvs, step):
        peer = (front + step) % n_front
        return pltpu.make_async_remote_copy(
            src_ref=src.at[peer],
            dst_ref=dst_at(front),
            send_sem=sends.at[step - 1],
            recv_sem=recvs.at[step - 1],
            device_id={"front": peer},
            device_id_type=MESH,
        )

    def arrival(src, dst_at, sends, recvs, step):
        peer = (front + n_front - step) % n_front
        return pltpu.make_async_remote_copy(
            src_ref=src.at[peer],
            dst_ref=dst_at(peer),
            send_sem=sends.at[step - 1],
            recv_sem=recvs.at[step - 1],
            device_id={"front": peer},
            device_id_type=MESH,
        )

    def rows_of(ref):
        return lambda f: ref.at[:, pl.ds(pl.multiple_of(f * rows, rows), rows), :]

    def piece(buf, dx, flip, low, high):
        chip = (x + dx + chips) % chips
        who = 2 * chip + (1 - core if flip else core)
        count, order, _ = buf.shape
        low, high = low * count // 4, high * count // 4
        some = order // n_front
        return buf.at[low:high, pl.ds(pl.multiple_of(who * some, some), some), :]

    routes = [
        (0, 0, 4, 1, False),
        (0, 0, 4, -1, False),
        (0, 0, 4, 0, True),
        (-1, 0, 4, 0, True),
        (-1, 0, 2, 1, False),
        (1, 0, 4, 0, True),
        (1, 2, 4, -1, False),
        (2, 0, 2, 0, True),
        (2, 2, 4, 0, True),
    ]

    def route(buf, sends, recvs, i):
        dx, low, high, to, flip = routes[i]
        chip = (x + to + chips) % chips
        peer = 2 * chip + (1 - core if flip else core)
        block = piece(buf, dx, False, low, high)
        return pltpu.make_async_remote_copy(
            src_ref=block,
            dst_ref=block,
            send_sem=sends.at[i],
            recv_sem=recvs.at[i],
            device_id={"front": peer},
            device_id_type=MESH,
        )

    def route_arrival(buf, sends, recvs, i):
        dx, low, high, to, flip = routes[i]
        chip = (x + to + chips) % chips
        peer = 2 * chip + (1 - core if flip else core)
        block = piece(buf, dx - to, flip, low, high)
        return pltpu.make_async_remote_copy(
            src_ref=block,
            dst_ref=block,
            send_sem=sends.at[i],
            recv_sem=recvs.at[i],
            device_id={"front": peer},
            device_id_type=MESH,
        )

    class Gather:
        def __init__(self, buf, sends, recvs):
            self.args = (buf, sends, recvs)

        def send(self, *which):
            for i in which:
                route(*self.args, i).start()

        def take(self, *which):
            for i in which:
                route_arrival(*self.args, i).wait_recv()

        def drain(self):
            for i in range(len(routes)):
                route(*self.args, i).wait_send()

    first = odd
    second = 1 - odd
    gather_inv = Gather(inv, gi_send, gi_recv)
    gather_host = Gather(hw, gh_send, gh_recv)
    gather_one = Gather(lw.at[first], g_send.at[0], g_recv.at[0])
    gather_two = Gather(lw.at[second], g_send.at[1], g_recv.at[1])

    for step in range(1, n_front):
        exchange(pk, rows_of(r2), a_send, a_recv, step).start()
    loads[1].wait()
    gather_inv.send(0, 1, 2)
    loads[2].wait()
    loads[3].wait()
    gather_one.send(0, 1, 2)
    r2[:, own_rows, :] = pk[front]

    loads[6].wait()
    wall[1] = tn(sinv[...], su[1]).astype(BF)
    gather_inv.take(0)
    gather_inv.send(4, 3)
    gather_inv.take(1)
    gather_inv.send(6, 5)
    if skipped:

        @pl.when(is_skipped)
        def _():
            pl.semaphore_wait(known_sem, 2)
            for i in range(2):

                @pl.when(inside(ancestor(i)))
                def _():
                    hw_copy(i, host_slot(i), ancestor(i)).start()

    gather_one.take(0)
    gather_one.send(4, 3)
    gather_one.take(1)
    gather_one.send(6, 5)
    gather_inv.take(4)
    gather_inv.send(7)
    gather_inv.take(6)
    gather_inv.send(8)
    gather_two.send(0, 1, 2)
    for step in range(1, n_front):
        arrival(pk, rows_of(r2), a_send, a_recv, step).wait_recv()
    gather_inv.take(2, 3, 5, 7, 8)

    live = cnt_ref[0]
    low_lanes = lax.broadcasted_iota(jnp.int32, (1, 128), 1) < HALF
    alive = [
        jnp.logical_or(
            jnp.logical_and(low_lanes, t < live),
            jnp.logical_and(jnp.logical_not(low_lanes), t + 2 < live),
        )
        for t in range(2)
    ]
    for t in range(2):
        block = r2[t]
        solved = jnp.where(low_lanes, nn(inv[t], block), nn(inv[t + 2], block))
        s2[t] = jnp.where(alive[t], solved, 0.0).astype(BF)

    def toward(side):
        total = jnp.zeros((HALF, srhs.shape[1]), F32)
        for t in range(2):
            turned = s2[t].T
            total = total + nn(turned[0:HALF], lw[side, t])
            total = total + nn(turned[HALF:], lw[side, t + 2])
        return total

    def tl_copy(target):
        return pltpu.make_async_remote_copy(
            src_ref=tl_send,
            dst_ref=tl_recv,
            send_sem=tl_ssem,
            recv_sem=tl_rsem,
            device_id={"leaf": target},
            device_id_type=MESH,
        )

    chunks = [(0, 256), (256, width)] if width > 256 else [(0, width)]

    class Message:
        def __init__(self, src, dst, sends, recvs, target):
            self.parts = [
                pltpu.make_async_remote_copy(
                    src_ref=src.at[:, low:high],
                    dst_ref=dst.at[:, low:high],
                    send_sem=sends.at[n],
                    recv_sem=recvs.at[n],
                    device_id={"leaf": target},
                    device_id_type=MESH,
                )
                for n, (low, high) in enumerate(chunks)
            ]

        def start(self):
            for part in self.parts:
                part.start()

        def wait_send(self):
            for part in self.parts:
                part.wait_send()

        def wait_recv(self):
            for part in self.parts:
                part.wait_recv()

    def up_message(i, h, target):
        return Message(up_send.at[i], up_recv.at[h, i], up_ssem.at[i], up_rsem.at[h, i], target)

    def hu_message(i, slot, which, target):
        return Message(
            up_send.at[near], hu_recv.at[slot, which], hu_ssem.at[i], hu_rsem.at[slot, which], target
        )

    def dn_message(i, h, target):
        return Message(dn_send, dn_recv.at[i], dn_ssem.at[i, h], dn_rsem.at[i], target)

    def v_message(slot, which, side, target):
        return Message(
            v_send.at[slot], dv_recv.at[side], v_ssem.at[slot, which], dv_rsem.at[side], target
        )

    def da_message(target):
        return Message(da, dn_recv.at[near], da_ssem, dn_rsem.at[near], target)

    def zp_message(i, target):
        return Message(zp_send, zp_recv, zp_ssem.at[i], zp_rsem, target)

    def climb():
        rb[...] = res[...].astype(BF)
        for j in range(2):
            i = near if j == 0 else 1 - near
            target = ancestor(i)

            @pl.when(inside(target))
            def _():
                message = up_message(i, own_level, target)
                for n, (low, high) in enumerate(chunks):
                    up_send[i, :, low:high] = nn(rb[...], wall[i, :, low:high]).astype(BF)
                    if j == 1 or not skipped:
                        message.parts[n].start()
                    else:

                        @pl.when(jnp.logical_not(is_joined))
                        def _():
                            message.parts[n].start()

                        @pl.when(jnp.logical_and(is_joined, inside(group_host(parent_near))))
                        def _():
                            to_host(parent_near).parts[n].start()

        if skipped:

            @pl.when(is_joined)
            def _():
                @pl.when(inside(group_host(1 - parent_near)))
                def _():
                    to_host(1 - parent_near).start()

                up_message(near, own_level, parent).start()

    def to_host(side):
        return hu_message(side, host_slot(side), 1 - near, group_host(side))

    def gather_level(h):
        below = lax.shift_left(jnp.int32(1), jnp.int32(h))
        for i in range(2):
            source = leaf + (1 - 2 * i) * below

            @pl.when(inside(source))
            def _():
                up_message(i, h, source).wait_recv()
                res[...] = res[...] - up_recv[h, i].astype(F32)

    gather_one.take(4)
    gather_one.send(7)
    gather_one.take(6)
    gather_one.send(8)
    gather_one.take(2, 3, 5, 7, 8)
    loads[7].wait()
    part_one = toward(first)

    @pl.when(jnp.logical_not(is_even))
    def _():
        tl_send[...] = part_one.astype(BF)
        tl_copy(leaf - 1).start()

    gather_two.take(0)
    gather_two.send(4, 3)
    gather_two.take(1)
    gather_two.send(6, 5)

    @pl.when(is_even)
    def _():
        res[...] = srhs[...].astype(F32) - part_one
        tl_copy(leaf + 1).wait_recv()
        res[...] = res[...] - tl_recv[...].astype(F32)
        climb()

    gather_two.take(4)
    gather_two.send(7)
    gather_two.take(6)
    gather_two.send(8)
    gather_two.take(2, 3, 5, 7, 8)
    part_two = toward(second)

    @pl.when(jnp.logical_and(is_even, leaf > 0))
    def _():
        tl_send[...] = part_two.astype(BF)
        tl_copy(leaf - 1).start()

    @pl.when(jnp.logical_not(is_even))
    def _():
        res[...] = srhs[...].astype(F32) - part_two

        @pl.when(leaf < n_leaf - 1)
        def _():
            tl_copy(leaf + 1).wait_recv()
            res[...] = res[...] - tl_recv[...].astype(F32)

        if skipped:

            @pl.when(is_host)
            def _():
                for slot in range(2):

                    @pl.when(has_group(slot))
                    def _():
                        hw_copy(0, slot, group_of(slot)[0]).wait_recv()

                gather_host.send(0, 1, 2)
                gather_host.take(0)
                gather_host.send(4, 3)
                gather_host.take(1)
                gather_host.send(6, 5)
                gather_host.take(4)
                gather_host.send(7)
                gather_host.take(6)
                gather_host.send(8)

        @pl.when(is_root)
        def _():
            loads[8].wait()
            su[0] = tn(sinv[...], sinv[...]).astype(BF)
            zacc[...] = nn(snoise[...], sinv[...])

        @pl.loop(0, level - is_skipped.astype(jnp.int32))
        def _(h):
            gather_level(h)

        if skipped:

            @pl.when(is_host)
            def _():
                gather_host.take(2, 3, 5, 7, 8)
                for slot in range(2):

                    @pl.when(has_group(slot))
                    def _():
                        center, reach = group_of(slot)
                        hu_message(0, slot, 0, center - reach).wait_recv()
                        hu_message(0, slot, 1, center + reach).wait_recv()
                        both = hu_recv[slot, 0].astype(F32) + hu_recv[slot, 1].astype(F32)
                        res[...] = res[...] + nn(both.astype(BF), hw[slot])

        climb()
        if skipped:

            @pl.when(is_skipped)
            def _():
                gather_level(level - 1)
                rb[...] = res[...].astype(BF)

    @pl.when(is_root)
    def _():
        zacc[...] = zacc[...] + nn(rb[...], su[0])

    @pl.when(jnp.logical_not(is_root))
    def _():
        loads[8].wait()
        solved_sep = nt(rb[...], sinv[...]).astype(BF).astype(F32)
        target_sep = (solved_sep + snoise[...].astype(F32)).astype(BF)
        zacc[...] = nn(target_sep, sinv[...])

    if skipped:

        @pl.when(is_skipped)
        def _():
            zp_send[...] = zacc[...].astype(BF)
            for i in range(2):
                zp_message(i, leaf + (1 - 2 * i) * half_span).start()

    loads[9].wait()
    pack(n_buf, turned_slots, pkn)
    for step in range(1, n_front):
        exchange(pkn, rows_of(n2), nz_send, nz_recv, step).start()
    n2[:, own_rows, :] = pkn[front]
    for i in range(2):
        wt[i] = wall[i].T
    if skipped:

        @pl.when(is_host)
        def _():
            for slot in range(2):

                @pl.when(has_group(slot))
                def _():
                    hwt[slot] = hw[slot].T


    is_plain = jnp.logical_not(jnp.logical_or(is_skipped, is_joined))

    def take_draws(i, wanted):
        source = ancestor(i)

        @pl.when(jnp.logical_and(wanted, inside(source)))
        def _():
            dn_message(i, 0, source).wait_recv()
            zacc[...] = zacc[...] - nn(dn_recv[i], wt[i])

    take_draws(1 - near, jnp.logical_not(is_skipped))
    if skipped:

        @pl.when(is_joined)
        def _():
            zp_message(0, parent).wait_recv()
            da[...] = zp_recv[...]

        for i in range(2):

            @pl.when(jnp.logical_and(jnp.logical_not(is_plain), inside(group_host(i))))
            def _():
                v_message(0, 0, i, group_host(i)).wait_recv()

                @pl.when(is_skipped)
                def _():
                    zacc[...] = zacc[...] - dv_recv[i].astype(F32)

                @pl.when(is_joined)
                def _():
                    da[...] = (da[...].astype(F32) - dv_recv[i].astype(F32)).astype(BF)

        @pl.when(is_joined)
        def _():
            @pl.when(level + 1 == lowest)
            def _():
                da_message(leaf + (2 * near - 1) * half_span).start()

            dn_recv[near] = da[...]

    plain_last = jnp.logical_and(is_plain, inside(ancestor(near)))

    @pl.when(plain_last)
    def _():
        dn_message(near, 0, ancestor(near)).wait_recv()

    is_early = jnp.logical_and(level > 0, level < lowest)

    def early(act):
        for i in range(2):
            target = leaf + (1 - 2 * i) * half_span

            @pl.when(jnp.logical_and(is_early, inside(target)))
            def _():
                act(dn_message(i, jnp.maximum(level - 1, 0), target))

        @pl.when(is_even)
        def _():
            act(dn_message(2, 0, leaf + 1))

    has_last = jnp.logical_or(plain_last, is_joined)

    @pl.when(has_last)
    def _():
        for n, (low, high) in enumerate(chunks):
            value = zacc[:, low:high] - nn(dn_recv[near], wt[near, :, low:high])
            zacc[:, low:high] = value
            dn_send[:, low:high] = value.astype(BF)
            early(lambda message: message.parts[n].start())

    @pl.when(jnp.logical_not(has_last))
    def _():
        dn_send[...] = zacc[...].astype(BF)

    sep_high[...] = dn_send[...]
    sep_low[...] = (zacc[...] - dn_send[...].astype(F32)).astype(BF)

    def for_level(h, act):
        below = lax.shift_left(jnp.int32(1), jnp.int32(h))
        bypassed = jnp.logical_or(
            any_of(jnp.int32(h), skipped), jnp.logical_and(is_skipped, h >= level - 2)
        )
        for i in range(2):
            target = leaf + (1 - 2 * i) * below

            @pl.when(jnp.logical_and(jnp.logical_not(bypassed), inside(target)))
            def _():
                act(dn_message(i, h, target))

    def begin(message):
        message.start()

    def left(message):
        message.wait_send()

    steps = jnp.maximum(level - lowest + 1, 0)

    @pl.loop(0, steps)
    def _(step):
        for_level(level - 1 - step, begin)

    if skipped:

        def to_group(slot):
            center, reach = group_of(slot)
            return [
                v_message(slot, which, group_side(slot), target)
                for which, target in enumerate((center - reach, center + reach, center))
            ]

        for slot in (1, 0):

            @pl.when(has_group(slot))
            def _():
                v_send[slot] = nn(dn_send[...], hwt[slot]).astype(BF)
                for message in to_group(slot):
                    message.start()

        for slot in range(2):

            @pl.when(has_group(slot))
            def _():
                for message in to_group(slot):
                    message.wait_send()

    @pl.loop(0, steps)
    def _(step):
        for_level(level - 1 - step, left)

    early(left)

    @pl.loop(steps + is_early.astype(jnp.int32), level)
    def _(step):
        for_level(level - 1 - step, begin)
        for_level(level - 1 - step, left)

    own_dup[0:HALF] = dn_send[...]
    own_dup[HALF:] = dn_send[...]

    def pulled(side, dup):
        return [
            jnp.where(low_lanes, nt(lw[side, t], dup), nt(lw[side, t + 2], dup)) for t in range(2)
        ]

    for t, value in enumerate(pulled(0, own_dup[...])):
        pull[t] = value
    for step in range(1, n_front):
        arrival(pkn, rows_of(n2), nz_send, nz_recv, step).wait_recv()

    @pl.when(jnp.logical_not(is_even))
    def _():
        dn_message(2, 0, leaf - 1).wait_recv()
        prev_dup[0:HALF] = dn_recv[2]

    @pl.when(jnp.logical_and(is_even, leaf > 0))
    def _():
        prev_dup[0:HALF] = dn_recv[0]

    @pl.when(leaf == 0)
    def _():
        prev_dup[0:HALF] = jnp.zeros((HALF, prev_dup.shape[1]), BF)

    prev_dup[HALF:] = prev_dup[0:HALF]
    for t, value in enumerate(pulled(1, prev_dup[...])):
        mixed = s2[t].astype(F32) + n2[t].astype(F32) - pull[t] - value
        mixed = jnp.where(alive[t], mixed, 0.0).astype(BF)
        drawn = jnp.where(low_lanes, tn(inv[t], mixed), tn(inv[t + 2], mixed)).astype(BF)
        for f in range(n_front):
            d2[f, t] = drawn[f * rows : f * rows + rows]

    for step in range(1, n_front):
        exchange(d2, lambda f: o2.at[f], o_send, o_recv, step).start()
    o2[front] = d2[front]
    for step in range(1, n_front):
        arrival(d2, lambda f: o2.at[f], o_send, o_recv, step).wait_recv()

    for t in range(2):
        for slab in range(n_front // 2):
            lanes = slice(slab * 128, slab * 128 + 128)
            a = o2[2 * slab, t]
            b = o2[2 * slab + 1, t]
            turned_slots[t, :, lanes] = jnp.concatenate([a[:, :HALF], b[:, :HALF]], axis=1)
            turned_slots[t + 2, :, lanes] = jnp.concatenate([a[:, HALF:], b[:, HALF:]], axis=1)
    leaf_out[...] = jnp.swapaxes(turned_slots[...], 0, 1)

    for step in range(1, n_front):
        exchange(pk, rows_of(r2), a_send, a_recv, step).wait_send()
        exchange(pkn, rows_of(n2), nz_send, nz_recv, step).wait_send()
        exchange(d2, lambda f: o2.at[f], o_send, o_recv, step).wait_send()
    gather_inv.drain()
    gather_one.drain()
    gather_two.drain()

    @pl.when(leaf > 0)
    def _():
        tl_copy(leaf - 1).wait_send()

    for i in range(2):
        target = ancestor(i)

        @pl.when(inside(target))
        def _():
            up_message(i, own_level, target).wait_send()

    if skipped:

        @pl.when(is_joined)
        def _():
            for side in range(2):

                @pl.when(inside(group_host(side)))
                def _():
                    to_host(side).wait_send()

            @pl.when(level + 1 == lowest)
            def _():
                da_message(leaf + (2 * near - 1) * half_span).wait_send()

        @pl.when(is_skipped)
        def _():
            for i in range(2):
                zp_message(i, leaf + (1 - 2 * i) * half_span).wait_send()

                @pl.when(inside(ancestor(i)))
                def _():
                    hw_copy(i, host_slot(i), ancestor(i)).wait_send()

        @pl.when(is_host)
        def _():
            gather_host.drain()


def on_device(
    leaf_rhs,
    sep_rhs,
    leaf_noise,
    sep_noise,
    leaf_inverse,
    leaf_left,
    leaf_right,
    sep_inverse,
    sep_left,
    sep_right,
    leaf_count,
):
    n_leaf = lax.axis_size("leaf")
    n_front = lax.axis_size("front")
    depth = n_leaf.bit_length() - 1
    _, rows, slots, samples = leaf_rhs.shape
    share, width = sep_rhs.shape[1:]
    order = rows * n_front
    hbm = pl.BlockSpec(memory_space=pltpu.HBM)
    vmem = pl.BlockSpec(memory_space=pltpu.VMEM)
    dma = pltpu.SemaphoreType.DMA
    leaf_draws, sep_high, sep_low = pl.pallas_call(
        functools.partial(kernel, n_leaf, n_front, depth),
        out_shape=(
            jax.ShapeDtypeStruct((rows, slots, samples), BF),
            jax.ShapeDtypeStruct((share, width), BF),
            jax.ShapeDtypeStruct((share, width), BF),
        ),
        in_specs=[pl.BlockSpec(memory_space=pltpu.SMEM)] + [hbm] * 10,
        out_specs=(vmem, vmem, vmem),
        scratch_shapes=[
            pltpu.VMEM((rows, slots, samples), BF),
            pltpu.VMEM((rows, slots, samples), BF),
            pltpu.VMEM((slots, rows, samples), BF),
            pltpu.VMEM((n_front, 2, rows, 128), BF),
            pltpu.VMEM((n_front, 2, rows, 128), BF),
            pltpu.VMEM((2, order, 128), BF),
            pltpu.VMEM((2, order, 128), BF),
            pltpu.VMEM((slots, order, order), BF),
            pltpu.VMEM((2, slots, order, width), BF),
            pltpu.VMEM((share, width), BF),
            pltpu.VMEM((share, width), BF),
            pltpu.VMEM((width, width), BF),
            pltpu.VMEM((2, width, width), BF),
            pltpu.VMEM((2, width, width), BF),
            pltpu.VMEM((2, width, width), BF),
            pltpu.VMEM((2, width, width), BF),
            pltpu.VMEM((2, width, width), BF),
            pltpu.VMEM((2, order, 128), BF),
            pltpu.VMEM((share, width), F32),
            pltpu.VMEM((share, width), BF),
            pltpu.VMEM((share, width), F32),
            pltpu.VMEM((share, width), BF),
            pltpu.VMEM((share, width), BF),
            pltpu.VMEM((2, share, width), BF),
            pltpu.VMEM((depth, 2, share, width), BF),
            pltpu.VMEM((share, width), BF),
            pltpu.VMEM((3, share, width), BF),
            pltpu.VMEM((share, width), BF),
            pltpu.VMEM((share, width), BF),
            pltpu.VMEM((2, 2, share, width), BF),
            pltpu.VMEM((2, share, width), BF),
            pltpu.VMEM((2, share, width), BF),
            pltpu.VMEM((share, width), BF),
            pltpu.VMEM((2 * share, width), BF),
            pltpu.VMEM((2 * share, width), BF),
            pltpu.VMEM((2, order, 128), F32),
            pltpu.VMEM((n_front, 2, rows, 128), BF),
            pltpu.VMEM((n_front, 2, rows, 128), BF),
            dma((10,)),
            dma((n_front - 1,)),
            dma((n_front - 1,)),
            dma((n_front - 1,)),
            dma((n_front - 1,)),
            dma((9,)),
            dma((9,)),
            dma((2, 9)),
            dma((2, 9)),
            dma,
            dma,
            dma((2, 2)),
            dma((depth, 2, 2)),
            dma((3, depth, 2)),
            dma((3, 2)),
            dma((n_front - 1,)),
            dma((n_front - 1,)),
            dma((2,)),
            dma((2,)),
            dma((9,)),
            dma((9,)),
            dma((2, 2)),
            dma((2, 2, 2)),
            dma((2, 3, 2)),
            dma((2, 2)),
            dma((2,)),
            dma((2, 2)),
            dma((2,)),
            pltpu.SemaphoreType.REGULAR,
        ],
        compiler_params=pltpu.CompilerParams(
            collective_id=0, has_side_effects=True, vmem_limit_bytes=63 * 1024 * 1024
        ),
    )(
        leaf_count,
        leaf_rhs[0],
        leaf_noise[0],
        leaf_inverse[0],
        leaf_left[0],
        leaf_right[0],
        sep_rhs[0],
        sep_noise[0],
        sep_inverse[0],
        sep_left[0],
        sep_right[0],
    )
    sep_draws = sep_high.astype(F32) + sep_low.astype(F32)
    return (leaf_draws.astype(F32)[None], sep_draws[None])


def solution(mesh):
    return jax.shard_map(
        on_device,
        mesh=mesh,
        in_specs=(
            P("leaf", "front", None, None),
            P("leaf", "front", None),
            P("leaf", "front", None, None),
            P("leaf", "front", None),
            P("leaf", None, "front", None),
            P("leaf", None, "front", None),
            P("leaf", None, "front", None),
            P("leaf", None, None),
            P("leaf", None, None),
            P("leaf", None, None),
            P("leaf"),
        ),
        out_specs=(P("leaf", "front", None, None), P("leaf", "front", None)),
        check_vma=False,
    )
```

```python
import functools

import jax
import jax.numpy as jnp
from jax import lax
from jax.experimental import pallas as pl
from jax.experimental.pallas import tpu as pltpu
from jax.sharding import PartitionSpec as P

MESH = pl.DeviceIdType.MESH
BF = jnp.bfloat16
F32 = jnp.float32
HALF = 64
SKIPPED = (3, 5)


def nn(a, b):
    return lax.dot_general(a, b, (((1,), (0,)), ((), ())), preferred_element_type=F32)


def nt(a, b):
    return lax.dot_general(a, b, (((1,), (1,)), ((), ())), preferred_element_type=F32)


def tn(a, b):
    return lax.dot_general(a, b, (((0,), (0,)), ((), ())), preferred_element_type=F32)


def pack(raw_ref, block_ref, packed_ref):
    rows, slots, samples = raw_ref.shape
    for t in range(slots):
        block_ref[t] = raw_ref[:, t, :]
    for slab in range(samples // 128):
        lanes = slice(slab * 128, slab * 128 + 128)
        a = block_ref[0:2, :, lanes].reshape(2 * rows, 128)
        b = block_ref[2:4, :, lanes].reshape(2 * rows, 128)
        for core in range(2):
            part = slice(core * HALF, core * HALF + HALF)
            both = jnp.concatenate([a[:, part], b[:, part]], axis=1)
            packed_ref[2 * slab + core] = both.reshape(2, rows, 128)


def kernel(
    n_leaf,
    n_front,
    depth,
    cnt_ref,
    rhs_hbm,
    noise_hbm,
    inv_hbm,
    left_hbm,
    right_hbm,
    srhs_hbm,
    snoise_hbm,
    sinv_hbm,
    sleft_hbm,
    sright_hbm,
    leaf_out,
    sep_high,
    sep_low,
    x_buf,
    n_buf,
    turned_slots,
    pk,
    pkn,
    r2,
    n2,
    inv,
    lw,
    srhs,
    snoise,
    sinv,
    su,
    wall,
    wt,
    hw,
    hwt,
    s2,
    res,
    rb,
    zacc,
    tl_send,
    tl_recv,
    up_send,
    up_recv,
    dn_send,
    dn_recv,
    zp_send,
    zp_recv,
    hu_recv,
    v_send,
    dv_recv,
    da,
    own_dup,
    prev_dup,
    pull,
    d2,
    o2,
    load_sem,
    a_send,
    a_recv,
    nz_send,
    nz_recv,
    gi_send,
    gi_recv,
    g_send,
    g_recv,
    tl_ssem,
    tl_rsem,
    up_ssem,
    up_rsem,
    dn_ssem,
    dn_rsem,
    o_send,
    o_recv,
    hw_ssem,
    hw_rsem,
    gh_send,
    gh_recv,
    hu_ssem,
    hu_rsem,
    v_ssem,
    dv_rsem,
    da_ssem,
    zp_ssem,
    zp_rsem,
    known_sem,
):
    leaf = lax.axis_index("leaf")
    front = lax.axis_index("front")
    chips = n_front // 2
    x = front // 2
    core = front % 2
    rows = x_buf.shape[0]
    pos = leaf + 1
    level = jnp.int32(0)
    for bit in range(1, depth + 1):
        level = level + (pos % (1 << bit) == 0).astype(jnp.int32)
    span = jnp.int32(1)
    for bit in range(1, depth + 1):
        span = jnp.where(pos % (1 << bit) == 0, jnp.int32(1 << bit), span)
    odd = leaf % 2
    is_even = odd == 0
    is_root = level == depth

    def inside(target):
        return jnp.logical_and(target >= 0, target < n_leaf)

    def any_of(value, levels):
        found = jnp.bool_(False)
        for one in levels:
            found = jnp.logical_or(found, value == one)
        return found

    skipped = tuple(one for one in SKIPPED if one < depth)
    is_skipped = any_of(level, skipped)
    is_joined = any_of(level + 1, skipped)
    joined = is_joined.astype(jnp.int32)
    near = ((pos // span) % 4 == 1).astype(jnp.int32)
    parent = leaf + (2 * near - 1) * span
    parent_near = (((parent + 1) // (2 * span)) % 4 == 1).astype(jnp.int32)
    own_level = jnp.minimum(level, depth - 1)
    half_span = jnp.maximum(span // 2, 1)
    lowest = skipped[0] if skipped else depth
    is_host = level > lowest
    is_top = leaf == n_leaf - 1
    top_hosts_two = len(skipped) == 2

    def ancestor(i):
        return leaf + (2 * i - 1) * span

    def group_host(i):
        return jnp.where(is_skipped, ancestor(i), parent + (2 * i - 1) * 2 * span)

    def host_slot(i):
        far_group = jnp.logical_or(level == skipped[-1], level + 1 == skipped[-1])
        return jnp.where(jnp.logical_and(far_group, top_hosts_two), 1, 1 - i)

    def group_of(slot):
        if slot == 0:
            return leaf - (1 << lowest), jnp.int32(1 << (lowest - 1))
        if top_hosts_two:
            other = 1 << skipped[-1]
            return (
                jnp.where(is_top, leaf - other, leaf + (1 << lowest)),
                jnp.where(is_top, jnp.int32(other // 2), jnp.int32(1 << (lowest - 1))),
            )
        return leaf + (1 << lowest), jnp.int32(1 << (lowest - 1))

    def group_side(slot):
        if slot == 0:
            return jnp.int32(1)
        return is_top.astype(jnp.int32)

    def has_group(slot):
        return jnp.logical_and(is_host, inside(group_of(slot)[0]))

    def load(i, src, dst):
        return pltpu.make_async_copy(src, dst, load_sem.at[i])

    own_rows = pl.ds(pl.multiple_of(front * rows, rows), rows)
    loads = [
        load(0, rhs_hbm, x_buf),
        load(1, inv_hbm, inv.at[:, own_rows, :]),
        load(2, right_hbm, lw.at[0, :, own_rows, :]),
        load(3, left_hbm, lw.at[1, :, own_rows, :]),
        load(4, sinv_hbm, sinv),
        load(5, sleft_hbm, su.at[0]),
        load(6, sright_hbm, su.at[1]),
        load(7, srhs_hbm, srhs),
        load(8, snoise_hbm, snoise),
        load(9, noise_hbm, n_buf),
    ]
    for copy in loads:
        copy.start()

    barrier = pltpu.get_barrier_semaphore()
    partners = jnp.int32(n_front - 1)
    for step in range(1, n_front):
        pl.semaphore_signal(
            barrier, inc=1, device_id={"front": (front + step) % n_front}, device_id_type=MESH
        )
    greeted = [(leaf - 1, leaf > 0), (leaf + 1, leaf < n_leaf - 1)]
    if skipped:
        greeted += [
            (parent, is_joined),
            (leaf - half_span, is_skipped),
            (leaf + half_span, is_skipped),
            (group_host(0), jnp.logical_and(is_joined, inside(group_host(0)))),
            (group_host(1), jnp.logical_and(is_joined, inside(group_host(1)))),
        ]
        for slot in range(2):
            center, reach = group_of(slot)
            greeted += [(center - reach, has_group(slot)), (center + reach, has_group(slot))]
    for target, reached in greeted:
        partners = partners + reached.astype(jnp.int32)

        @pl.when(reached)
        def _():
            pl.semaphore_signal(barrier, inc=1, device_id={"leaf": target}, device_id_type=MESH)

    loads[0].wait()
    pack(x_buf, turned_slots, pk)
    loads[4].wait()
    loads[5].wait()
    wall[0] = tn(sinv[...], su[0]).astype(BF)
    pl.semaphore_wait(barrier, partners)

    width = srhs.shape[1]
    share_rows = width // n_front
    share_here = pl.ds(pl.multiple_of(front * share_rows, share_rows), share_rows)

    def hw_copy(i, slot, target):
        return pltpu.make_async_remote_copy(
            src_ref=wall.at[i, share_here],
            dst_ref=hw.at[slot, share_here],
            send_sem=hw_ssem.at[i],
            recv_sem=hw_rsem.at[slot],
            device_id={"leaf": target},
            device_id_type=MESH,
        )

    if skipped:

        @pl.when(is_joined)
        def _():
            pl.semaphore_signal(known_sem, inc=1, device_id={"leaf": parent}, device_id_type=MESH)

    def exchange(src, dst_at, sends, recvs, step):
        peer = (front + step) % n_front
        return pltpu.make_async_remote_copy(
            src_ref=src.at[peer],
            dst_ref=dst_at(front),
            send_sem=sends.at[step - 1],
            recv_sem=recvs.at[step - 1],
            device_id={"front": peer},
            device_id_type=MESH,
        )

    def arrival(src, dst_at, sends, recvs, step):
        peer = (front + n_front - step) % n_front
        return pltpu.make_async_remote_copy(
            src_ref=src.at[peer],
            dst_ref=dst_at(peer),
            send_sem=sends.at[step - 1],
            recv_sem=recvs.at[step - 1],
            device_id={"front": peer},
            device_id_type=MESH,
        )

    def rows_of(ref):
        return lambda f: ref.at[:, pl.ds(pl.multiple_of(f * rows, rows), rows), :]

    def piece(buf, dx, flip, low, high):
        chip = (x + dx + chips) % chips
        who = 2 * chip + (1 - core if flip else core)
        count, order, _ = buf.shape
        low, high = low * count // 4, high * count // 4
        some = order // n_front
        return buf.at[low:high, pl.ds(pl.multiple_of(who * some, some), some), :]

    routes = [
        (0, 0, 2, 1, False),
        (0, 2, 4, -1, False),
        (0, 0, 4, 0, True),
        (-1, 0, 4, 0, True),
        (-1, 0, 2, 1, False),
        (1, 0, 4, 0, True),
        (1, 2, 4, -1, False),
        (2, 0, 2, 0, True),
        (2, 2, 4, 0, True),
        (0, 2, 4, 1, False),
        (0, 0, 2, -1, False),
    ]

    def route(buf, sends, recvs, i):
        dx, low, high, to, flip = routes[i]
        chip = (x + to + chips) % chips
        peer = 2 * chip + (1 - core if flip else core)
        block = piece(buf, dx, False, low, high)
        return pltpu.make_async_remote_copy(
            src_ref=block,
            dst_ref=block,
            send_sem=sends.at[i],
            recv_sem=recvs.at[i],
            device_id={"front": peer},
            device_id_type=MESH,
        )

    def route_arrival(buf, sends, recvs, i):
        dx, low, high, to, flip = routes[i]
        chip = (x + to + chips) % chips
        peer = 2 * chip + (1 - core if flip else core)
        block = piece(buf, dx - to, flip, low, high)
        return pltpu.make_async_remote_copy(
            src_ref=block,
            dst_ref=block,
            send_sem=sends.at[i],
            recv_sem=recvs.at[i],
            device_id={"front": peer},
            device_id_type=MESH,
        )

    class Gather:
        def __init__(self, buf, sends, recvs):
            self.args = (buf, sends, recvs)

        def send(self, *which):
            for i in which:
                route(*self.args, i).start()

        def take(self, *which):
            for i in which:
                route_arrival(*self.args, i).wait_recv()

        def drain(self):
            for i in range(len(routes)):
                route(*self.args, i).wait_send()

    first = odd
    second = 1 - odd
    gather_inv = Gather(inv, gi_send, gi_recv)
    gather_host = Gather(hw, gh_send, gh_recv)
    gather_one = Gather(lw.at[first], g_send.at[0], g_recv.at[0])
    gather_two = Gather(lw.at[second], g_send.at[1], g_recv.at[1])

    for step in range(1, n_front):
        exchange(pk, rows_of(r2), a_send, a_recv, step).start()
    loads[1].wait()
    gather_inv.send(0, 1, 9, 10, 2)
    loads[2].wait()
    loads[3].wait()
    gather_one.send(0, 1, 9, 10, 2)
    r2[:, own_rows, :] = pk[front]

    loads[6].wait()
    wall[1] = tn(sinv[...], su[1]).astype(BF)
    gather_inv.take(0)
    gather_inv.send(4)
    gather_inv.take(1)
    gather_inv.send(6)
    gather_inv.take(9)
    gather_inv.send(3)
    gather_inv.take(10)
    gather_inv.send(5)
    if skipped:

        @pl.when(is_skipped)
        def _():
            pl.semaphore_wait(known_sem, 2)
            for i in range(2):

                @pl.when(inside(ancestor(i)))
                def _():
                    hw_copy(i, host_slot(i), ancestor(i)).start()

    gather_one.take(0)
    gather_one.send(4)
    gather_one.take(1)
    gather_one.send(6)
    gather_inv.take(4)
    gather_inv.send(7)
    gather_inv.take(6)
    gather_inv.send(8)
    gather_one.take(9)
    gather_one.send(3)
    gather_one.take(10)
    gather_one.send(5)
    gather_two.send(0, 1, 9, 10, 2)
    for step in range(1, n_front):
        arrival(pk, rows_of(r2), a_send, a_recv, step).wait_recv()
    gather_inv.take(2, 3, 5, 7, 8)

    live = cnt_ref[0]
    low_lanes = lax.broadcasted_iota(jnp.int32, (1, 128), 1) < HALF
    alive = [
        jnp.logical_or(
            jnp.logical_and(low_lanes, t < live),
            jnp.logical_and(jnp.logical_not(low_lanes), t + 2 < live),
        )
        for t in range(2)
    ]
    for t in range(2):
        block = r2[t]
        solved = jnp.where(low_lanes, nn(inv[t], block), nn(inv[t + 2], block))
        s2[t] = jnp.where(alive[t], solved, 0.0).astype(BF)

    def toward(side):
        total = jnp.zeros((HALF, srhs.shape[1]), F32)
        for t in range(2):
            turned = s2[t].T
            total = total + nn(turned[0:HALF], lw[side, t])
            total = total + nn(turned[HALF:], lw[side, t + 2])
        return total

    def tl_copy(target):
        return pltpu.make_async_remote_copy(
            src_ref=tl_send,
            dst_ref=tl_recv,
            send_sem=tl_ssem,
            recv_sem=tl_rsem,
            device_id={"leaf": target},
            device_id_type=MESH,
        )

    chunks = [(0, 256), (256, width)] if width > 256 else [(0, width)]

    class Message:
        def __init__(self, src, dst, sends, recvs, target):
            self.parts = [
                pltpu.make_async_remote_copy(
                    src_ref=src.at[:, low:high],
                    dst_ref=dst.at[:, low:high],
                    send_sem=sends.at[n],
                    recv_sem=recvs.at[n],
                    device_id={"leaf": target},
                    device_id_type=MESH,
                )
                for n, (low, high) in enumerate(chunks)
            ]

        def start(self):
            for part in self.parts:
                part.start()

        def wait_send(self):
            for part in self.parts:
                part.wait_send()

        def wait_recv(self):
            for part in self.parts:
                part.wait_recv()

    def up_message(i, h, target):
        return Message(up_send.at[i], up_recv.at[h, i], up_ssem.at[i], up_rsem.at[h, i], target)

    def hu_message(i, slot, which, target):
        return Message(
            up_send.at[near], hu_recv.at[slot, which], hu_ssem.at[i], hu_rsem.at[slot, which], target
        )

    def dn_message(i, h, target):
        return Message(dn_send, dn_recv.at[i], dn_ssem.at[i, h], dn_rsem.at[i], target)

    def v_message(slot, which, side, target):
        return Message(
            v_send.at[slot], dv_recv.at[side], v_ssem.at[slot, which], dv_rsem.at[side], target
        )

    def da_message(target):
        return Message(da, dn_recv.at[near], da_ssem, dn_rsem.at[near], target)

    def zp_message(i, target):
        return Message(zp_send, zp_recv, zp_ssem.at[i], zp_rsem, target)

    def climb():
        rb[...] = res[...].astype(BF)
        for j in range(2):
            i = near if j == 0 else 1 - near
            target = ancestor(i)

            @pl.when(inside(target))
            def _():
                message = up_message(i, own_level, target)
                for n, (low, high) in enumerate(chunks):
                    up_send[i, :, low:high] = nn(rb[...], wall[i, :, low:high]).astype(BF)
                    if j == 1 or not skipped:
                        message.parts[n].start()
                    else:

                        @pl.when(jnp.logical_not(is_joined))
                        def _():
                            message.parts[n].start()

                        @pl.when(jnp.logical_and(is_joined, inside(group_host(parent_near))))
                        def _():
                            to_host(parent_near).parts[n].start()

        if skipped:

            @pl.when(is_joined)
            def _():
                @pl.when(inside(group_host(1 - parent_near)))
                def _():
                    to_host(1 - parent_near).start()

                up_message(near, own_level, parent).start()

    def to_host(side):
        return hu_message(side, host_slot(side), 1 - near, group_host(side))

    def gather_level(h):
        below = lax.shift_left(jnp.int32(1), jnp.int32(h))
        for i in range(2):
            source = leaf + (1 - 2 * i) * below

            @pl.when(inside(source))
            def _():
                up_message(i, h, source).wait_recv()
                res[...] = res[...] - up_recv[h, i].astype(F32)

    gather_one.take(4)
    gather_one.send(7)
    gather_one.take(6)
    gather_one.send(8)
    gather_one.take(2, 3, 5, 7, 8)
    loads[7].wait()
    part_one = toward(first)

    @pl.when(jnp.logical_not(is_even))
    def _():
        tl_send[...] = part_one.astype(BF)
        tl_copy(leaf - 1).start()

    gather_two.take(0)
    gather_two.send(4)
    gather_two.take(1)
    gather_two.send(6)

    @pl.when(is_even)
    def _():
        res[...] = srhs[...].astype(F32) - part_one
        tl_copy(leaf + 1).wait_recv()
        res[...] = res[...] - tl_recv[...].astype(F32)
        climb()

    gather_two.take(9)
    gather_two.send(3)
    gather_two.take(10)
    gather_two.send(5)
    gather_two.take(4)
    gather_two.send(7)
    gather_two.take(6)
    gather_two.send(8)
    gather_two.take(2, 3, 5, 7, 8)
    part_two = toward(second)

    @pl.when(jnp.logical_and(is_even, leaf > 0))
    def _():
        tl_send[...] = part_two.astype(BF)
        tl_copy(leaf - 1).start()

    @pl.when(jnp.logical_not(is_even))
    def _():
        res[...] = srhs[...].astype(F32) - part_two

        @pl.when(leaf < n_leaf - 1)
        def _():
            tl_copy(leaf + 1).wait_recv()
            res[...] = res[...] - tl_recv[...].astype(F32)

        if skipped:

            @pl.when(is_host)
            def _():
                for slot in range(2):

                    @pl.when(has_group(slot))
                    def _():
                        hw_copy(0, slot, group_of(slot)[0]).wait_recv()

                gather_host.send(0, 1, 9, 10, 2)
                gather_host.take(0)
                gather_host.send(4)
                gather_host.take(1)
                gather_host.send(6)
                gather_host.take(9)
                gather_host.send(3)
                gather_host.take(10)
                gather_host.send(5)
                gather_host.take(4)
                gather_host.send(7)
                gather_host.take(6)
                gather_host.send(8)

        @pl.when(is_root)
        def _():
            loads[8].wait()
            su[0] = tn(sinv[...], sinv[...]).astype(BF)
            zacc[...] = nn(snoise[...], sinv[...])

        @pl.loop(0, level - is_skipped.astype(jnp.int32))
        def _(h):
            gather_level(h)

        if skipped:

            @pl.when(is_host)
            def _():
                gather_host.take(2, 3, 5, 7, 8)
                for slot in range(2):

                    @pl.when(has_group(slot))
                    def _():
                        center, reach = group_of(slot)
                        hu_message(0, slot, 0, center - reach).wait_recv()
                        hu_message(0, slot, 1, center + reach).wait_recv()
                        both = hu_recv[slot, 0].astype(F32) + hu_recv[slot, 1].astype(F32)
                        res[...] = res[...] + nn(both.astype(BF), hw[slot])

        climb()
        if skipped:

            @pl.when(is_skipped)
            def _():
                gather_level(level - 1)
                rb[...] = res[...].astype(BF)

    @pl.when(is_root)
    def _():
        zacc[...] = zacc[...] + nn(rb[...], su[0])

    @pl.when(jnp.logical_not(is_root))
    def _():
        loads[8].wait()
        solved_sep = nt(rb[...], sinv[...]).astype(BF).astype(F32)
        target_sep = (solved_sep + snoise[...].astype(F32)).astype(BF)
        zacc[...] = nn(target_sep, sinv[...])

    if skipped:

        @pl.when(is_skipped)
        def _():
            zp_send[...] = zacc[...].astype(BF)
            for i in range(2):
                zp_message(i, leaf + (1 - 2 * i) * half_span).start()

    loads[9].wait()
    pack(n_buf, turned_slots, pkn)
    for step in range(1, n_front):
        exchange(pkn, rows_of(n2), nz_send, nz_recv, step).start()
    n2[:, own_rows, :] = pkn[front]
    for i in range(2):
        wt[i] = wall[i].T
    if skipped:

        @pl.when(is_host)
        def _():
            for slot in range(2):

                @pl.when(has_group(slot))
                def _():
                    hwt[slot] = hw[slot].T


    is_plain = jnp.logical_not(jnp.logical_or(is_skipped, is_joined))

    def take_draws(i, wanted):
        source = ancestor(i)

        @pl.when(jnp.logical_and(wanted, inside(source)))
        def _():
            dn_message(i, 0, source).wait_recv()
            zacc[...] = zacc[...] - nn(dn_recv[i], wt[i])

    take_draws(1 - near, jnp.logical_not(is_skipped))
    if skipped:

        @pl.when(is_joined)
        def _():
            zp_message(0, parent).wait_recv()
            da[...] = zp_recv[...]

        for i in range(2):

            @pl.when(jnp.logical_and(jnp.logical_not(is_plain), inside(group_host(i))))
            def _():
                v_message(0, 0, i, group_host(i)).wait_recv()

                @pl.when(is_skipped)
                def _():
                    zacc[...] = zacc[...] - dv_recv[i].astype(F32)

                @pl.when(is_joined)
                def _():
                    da[...] = (da[...].astype(F32) - dv_recv[i].astype(F32)).astype(BF)

        @pl.when(is_joined)
        def _():
            @pl.when(level + 1 == lowest)
            def _():
                da_message(leaf + (2 * near - 1) * half_span).start()

            dn_recv[near] = da[...]

    plain_last = jnp.logical_and(is_plain, inside(ancestor(near)))

    @pl.when(plain_last)
    def _():
        dn_message(near, 0, ancestor(near)).wait_recv()

    is_early = jnp.logical_and(level > 0, level < lowest)

    def early(act):
        for i in range(2):
            target = leaf + (1 - 2 * i) * half_span

            @pl.when(jnp.logical_and(is_early, inside(target)))
            def _():
                act(dn_message(i, jnp.maximum(level - 1, 0), target))

        @pl.when(is_even)
        def _():
            act(dn_message(2, 0, leaf + 1))

    has_last = jnp.logical_or(plain_last, is_joined)

    @pl.when(has_last)
    def _():
        for n, (low, high) in enumerate(chunks):
            value = zacc[:, low:high] - nn(dn_recv[near], wt[near, :, low:high])
            zacc[:, low:high] = value
            dn_send[:, low:high] = value.astype(BF)
            early(lambda message: message.parts[n].start())

    @pl.when(jnp.logical_not(has_last))
    def _():
        dn_send[...] = zacc[...].astype(BF)

    sep_high[...] = dn_send[...]
    sep_low[...] = (zacc[...] - dn_send[...].astype(F32)).astype(BF)

    def for_level(h, act):
        below = lax.shift_left(jnp.int32(1), jnp.int32(h))
        bypassed = jnp.logical_or(
            any_of(jnp.int32(h), skipped), jnp.logical_and(is_skipped, h >= level - 2)
        )
        for i in range(2):
            target = leaf + (1 - 2 * i) * below

            @pl.when(jnp.logical_and(jnp.logical_not(bypassed), inside(target)))
            def _():
                act(dn_message(i, h, target))

    def begin(message):
        message.start()

    def left(message):
        message.wait_send()

    steps = jnp.maximum(level - lowest + 1, 0)

    @pl.loop(0, steps)
    def _(step):
        for_level(level - 1 - step, begin)

    if skipped:

        def to_group(slot):
            center, reach = group_of(slot)
            return [
                v_message(slot, which, group_side(slot), target)
                for which, target in enumerate((center - reach, center + reach, center))
            ]

        for slot in (1, 0):

            @pl.when(has_group(slot))
            def _():
                v_send[slot] = nn(dn_send[...], hwt[slot]).astype(BF)
                for message in to_group(slot):
                    message.start()

        for slot in range(2):

            @pl.when(has_group(slot))
            def _():
                for message in to_group(slot):
                    message.wait_send()

    @pl.loop(0, steps)
    def _(step):
        for_level(level - 1 - step, left)

    early(left)

    @pl.loop(steps + is_early.astype(jnp.int32), level)
    def _(step):
        for_level(level - 1 - step, begin)
        for_level(level - 1 - step, left)

    own_dup[0:HALF] = dn_send[...]
    own_dup[HALF:] = dn_send[...]

    def pulled(side, dup):
        return [
            jnp.where(low_lanes, nt(lw[side, t], dup), nt(lw[side, t + 2], dup)) for t in range(2)
        ]

    for t, value in enumerate(pulled(0, own_dup[...])):
        pull[t] = value
    for step in range(1, n_front):
        arrival(pkn, rows_of(n2), nz_send, nz_recv, step).wait_recv()

    @pl.when(jnp.logical_not(is_even))
    def _():
        dn_message(2, 0, leaf - 1).wait_recv()
        prev_dup[0:HALF] = dn_recv[2]

    @pl.when(jnp.logical_and(is_even, leaf > 0))
    def _():
        prev_dup[0:HALF] = dn_recv[0]

    @pl.when(leaf == 0)
    def _():
        prev_dup[0:HALF] = jnp.zeros((HALF, prev_dup.shape[1]), BF)

    prev_dup[HALF:] = prev_dup[0:HALF]
    for t, value in enumerate(pulled(1, prev_dup[...])):
        mixed = s2[t].astype(F32) + n2[t].astype(F32) - pull[t] - value
        mixed = jnp.where(alive[t], mixed, 0.0).astype(BF)
        drawn = jnp.where(low_lanes, tn(inv[t], mixed), tn(inv[t + 2], mixed)).astype(BF)
        for f in range(n_front):
            d2[f, t] = drawn[f * rows : f * rows + rows]

    for step in range(1, n_front):
        exchange(d2, lambda f: o2.at[f], o_send, o_recv, step).start()
    o2[front] = d2[front]
    for step in range(1, n_front):
        arrival(d2, lambda f: o2.at[f], o_send, o_recv, step).wait_recv()

    for t in range(2):
        for slab in range(n_front // 2):
            lanes = slice(slab * 128, slab * 128 + 128)
            a = o2[2 * slab, t]
            b = o2[2 * slab + 1, t]
            turned_slots[t, :, lanes] = jnp.concatenate([a[:, :HALF], b[:, :HALF]], axis=1)
            turned_slots[t + 2, :, lanes] = jnp.concatenate([a[:, HALF:], b[:, HALF:]], axis=1)
    leaf_out[...] = jnp.swapaxes(turned_slots[...], 0, 1)

    for step in range(1, n_front):
        exchange(pk, rows_of(r2), a_send, a_recv, step).wait_send()
        exchange(pkn, rows_of(n2), nz_send, nz_recv, step).wait_send()
        exchange(d2, lambda f: o2.at[f], o_send, o_recv, step).wait_send()
    gather_inv.drain()
    gather_one.drain()
    gather_two.drain()

    @pl.when(leaf > 0)
    def _():
        tl_copy(leaf - 1).wait_send()

    for i in range(2):
        target = ancestor(i)

        @pl.when(inside(target))
        def _():
            up_message(i, own_level, target).wait_send()

    if skipped:

        @pl.when(is_joined)
        def _():
            for side in range(2):

                @pl.when(inside(group_host(side)))
                def _():
                    to_host(side).wait_send()

            @pl.when(level + 1 == lowest)
            def _():
                da_message(leaf + (2 * near - 1) * half_span).wait_send()

        @pl.when(is_skipped)
        def _():
            for i in range(2):
                zp_message(i, leaf + (1 - 2 * i) * half_span).wait_send()

                @pl.when(inside(ancestor(i)))
                def _():
                    hw_copy(i, host_slot(i), ancestor(i)).wait_send()

        @pl.when(is_host)
        def _():
            gather_host.drain()


def on_device(
    leaf_rhs,
    sep_rhs,
    leaf_noise,
    sep_noise,
    leaf_inverse,
    leaf_left,
    leaf_right,
    sep_inverse,
    sep_left,
    sep_right,
    leaf_count,
):
    n_leaf = lax.axis_size("leaf")
    n_front = lax.axis_size("front")
    depth = n_leaf.bit_length() - 1
    _, rows, slots, samples = leaf_rhs.shape
    share, width = sep_rhs.shape[1:]
    order = rows * n_front
    hbm = pl.BlockSpec(memory_space=pltpu.HBM)
    vmem = pl.BlockSpec(memory_space=pltpu.VMEM)
    dma = pltpu.SemaphoreType.DMA
    leaf_draws, sep_high, sep_low = pl.pallas_call(
        functools.partial(kernel, n_leaf, n_front, depth),
        out_shape=(
            jax.ShapeDtypeStruct((rows, slots, samples), BF),
            jax.ShapeDtypeStruct((share, width), BF),
            jax.ShapeDtypeStruct((share, width), BF),
        ),
        in_specs=[pl.BlockSpec(memory_space=pltpu.SMEM)] + [hbm] * 10,
        out_specs=(vmem, vmem, vmem),
        scratch_shapes=[
            pltpu.VMEM((rows, slots, samples), BF),
            pltpu.VMEM((rows, slots, samples), BF),
            pltpu.VMEM((slots, rows, samples), BF),
            pltpu.VMEM((n_front, 2, rows, 128), BF),
            pltpu.VMEM((n_front, 2, rows, 128), BF),
            pltpu.VMEM((2, order, 128), BF),
            pltpu.VMEM((2, order, 128), BF),
            pltpu.VMEM((slots, order, order), BF),
            pltpu.VMEM((2, slots, order, width), BF),
            pltpu.VMEM((share, width), BF),
            pltpu.VMEM((share, width), BF),
            pltpu.VMEM((width, width), BF),
            pltpu.VMEM((2, width, width), BF),
            pltpu.VMEM((2, width, width), BF),
            pltpu.VMEM((2, width, width), BF),
            pltpu.VMEM((2, width, width), BF),
            pltpu.VMEM((2, width, width), BF),
            pltpu.VMEM((2, order, 128), BF),
            pltpu.VMEM((share, width), F32),
            pltpu.VMEM((share, width), BF),
            pltpu.VMEM((share, width), F32),
            pltpu.VMEM((share, width), BF),
            pltpu.VMEM((share, width), BF),
            pltpu.VMEM((2, share, width), BF),
            pltpu.VMEM((depth, 2, share, width), BF),
            pltpu.VMEM((share, width), BF),
            pltpu.VMEM((3, share, width), BF),
            pltpu.VMEM((share, width), BF),
            pltpu.VMEM((share, width), BF),
            pltpu.VMEM((2, 2, share, width), BF),
            pltpu.VMEM((2, share, width), BF),
            pltpu.VMEM((2, share, width), BF),
            pltpu.VMEM((share, width), BF),
            pltpu.VMEM((2 * share, width), BF),
            pltpu.VMEM((2 * share, width), BF),
            pltpu.VMEM((2, order, 128), F32),
            pltpu.VMEM((n_front, 2, rows, 128), BF),
            pltpu.VMEM((n_front, 2, rows, 128), BF),
            dma((10,)),
            dma((n_front - 1,)),
            dma((n_front - 1,)),
            dma((n_front - 1,)),
            dma((n_front - 1,)),
            dma((11,)),
            dma((11,)),
            dma((2, 11)),
            dma((2, 11)),
            dma,
            dma,
            dma((2, 2)),
            dma((depth, 2, 2)),
            dma((3, depth, 2)),
            dma((3, 2)),
            dma((n_front - 1,)),
            dma((n_front - 1,)),
            dma((2,)),
            dma((2,)),
            dma((11,)),
            dma((11,)),
            dma((2, 2)),
            dma((2, 2, 2)),
            dma((2, 3, 2)),
            dma((2, 2)),
            dma((2,)),
            dma((2, 2)),
            dma((2,)),
            pltpu.SemaphoreType.REGULAR,
        ],
        compiler_params=pltpu.CompilerParams(
            collective_id=0, has_side_effects=True, vmem_limit_bytes=63 * 1024 * 1024
        ),
    )(
        leaf_count,
        leaf_rhs[0],
        leaf_noise[0],
        leaf_inverse[0],
        leaf_left[0],
        leaf_right[0],
        sep_rhs[0],
        sep_noise[0],
        sep_inverse[0],
        sep_left[0],
        sep_right[0],
    )
    sep_draws = sep_high.astype(F32) + sep_low.astype(F32)
    return (leaf_draws.astype(F32)[None], sep_draws[None])


def solution(mesh):
    return jax.shard_map(
        on_device,
        mesh=mesh,
        in_specs=(
            P("leaf", "front", None, None),
            P("leaf", "front", None),
            P("leaf", "front", None, None),
            P("leaf", "front", None),
            P("leaf", None, "front", None),
            P("leaf", None, "front", None),
            P("leaf", None, "front", None),
            P("leaf", None, None),
            P("leaf", None, None),
            P("leaf", None, None),
            P("leaf"),
        ),
        out_specs=(P("leaf", "front", None, None), P("leaf", "front", None)),
        check_vma=False,
    )
```

```python
import functools

import jax
import jax.numpy as jnp
from jax import lax
from jax.experimental import pallas as pl
from jax.experimental.pallas import tpu as pltpu
from jax.sharding import PartitionSpec as P

MESH = pl.DeviceIdType.MESH
BF = jnp.bfloat16
F32 = jnp.float32
HALF = 64
SKIPPED = (3, 5)


def nn(a, b):
    return lax.dot_general(a, b, (((1,), (0,)), ((), ())), preferred_element_type=F32)


def nt(a, b):
    return lax.dot_general(a, b, (((1,), (1,)), ((), ())), preferred_element_type=F32)


def tn(a, b):
    return lax.dot_general(a, b, (((0,), (0,)), ((), ())), preferred_element_type=F32)


def pack(raw_ref, block_ref, packed_ref):
    rows, slots, samples = raw_ref.shape
    for t in range(slots):
        block_ref[t] = raw_ref[:, t, :]
    for slab in range(samples // 128):
        lanes = slice(slab * 128, slab * 128 + 128)
        a = block_ref[0:2, :, lanes].reshape(2 * rows, 128)
        b = block_ref[2:4, :, lanes].reshape(2 * rows, 128)
        for core in range(2):
            part = slice(core * HALF, core * HALF + HALF)
            both = jnp.concatenate([a[:, part], b[:, part]], axis=1)
            packed_ref[2 * slab + core] = both.reshape(2, rows, 128)


def kernel(
    n_leaf,
    n_front,
    depth,
    cnt_ref,
    rhs_hbm,
    noise_hbm,
    inv_hbm,
    left_hbm,
    right_hbm,
    srhs_hbm,
    snoise_hbm,
    sinv_hbm,
    sleft_hbm,
    sright_hbm,
    leaf_out,
    sep_high,
    sep_low,
    x_buf,
    n_buf,
    turned_slots,
    pk,
    pkn,
    r2,
    n2,
    inv,
    lw,
    srhs,
    snoise,
    sinv,
    su,
    wall,
    wt,
    hw,
    hwt,
    s2,
    res,
    rb,
    zacc,
    tl_send,
    tl_recv,
    up_send,
    up_recv,
    dn_send,
    dn_recv,
    zp_send,
    zp_recv,
    hu_recv,
    v_send,
    dv_recv,
    da,
    own_dup,
    prev_dup,
    pull,
    d2,
    o2,
    load_sem,
    a_send,
    a_recv,
    nz_send,
    nz_recv,
    gi_send,
    gi_recv,
    g_send,
    g_recv,
    tl_ssem,
    tl_rsem,
    up_ssem,
    up_rsem,
    dn_ssem,
    dn_rsem,
    o_send,
    o_recv,
    hw_ssem,
    hw_rsem,
    gh_send,
    gh_recv,
    hu_ssem,
    hu_rsem,
    v_ssem,
    dv_rsem,
    da_ssem,
    zp_ssem,
    zp_rsem,
    known_sem,
):
    leaf = lax.axis_index("leaf")
    front = lax.axis_index("front")
    chips = n_front // 2
    x = front // 2
    core = front % 2
    rows = x_buf.shape[0]
    pos = leaf + 1
    level = jnp.int32(0)
    for bit in range(1, depth + 1):
        level = level + (pos % (1 << bit) == 0).astype(jnp.int32)
    span = jnp.int32(1)
    for bit in range(1, depth + 1):
        span = jnp.where(pos % (1 << bit) == 0, jnp.int32(1 << bit), span)
    odd = leaf % 2
    is_even = odd == 0
    is_root = level == depth

    def inside(target):
        return jnp.logical_and(target >= 0, target < n_leaf)

    def any_of(value, levels):
        found = jnp.bool_(False)
        for one in levels:
            found = jnp.logical_or(found, value == one)
        return found

    skipped = tuple(one for one in SKIPPED if one < depth)
    is_skipped = any_of(level, skipped)
    is_joined = any_of(level + 1, skipped)
    joined = is_joined.astype(jnp.int32)
    near = ((pos // span) % 4 == 1).astype(jnp.int32)
    parent = leaf + (2 * near - 1) * span
    parent_near = (((parent + 1) // (2 * span)) % 4 == 1).astype(jnp.int32)
    own_level = jnp.minimum(level, depth - 1)
    half_span = jnp.maximum(span // 2, 1)
    lowest = skipped[0] if skipped else depth
    is_host = level > lowest
    is_top = leaf == n_leaf - 1
    top_hosts_two = len(skipped) == 2

    def ancestor(i):
        return leaf + (2 * i - 1) * span

    def group_host(i):
        return jnp.where(is_skipped, ancestor(i), parent + (2 * i - 1) * 2 * span)

    def host_slot(i):
        far_group = jnp.logical_or(level == skipped[-1], level + 1 == skipped[-1])
        return jnp.where(jnp.logical_and(far_group, top_hosts_two), 1, 1 - i)

    def group_of(slot):
        if slot == 0:
            return leaf - (1 << lowest), jnp.int32(1 << (lowest - 1))
        if top_hosts_two:
            other = 1 << skipped[-1]
            return (
                jnp.where(is_top, leaf - other, leaf + (1 << lowest)),
                jnp.where(is_top, jnp.int32(other // 2), jnp.int32(1 << (lowest - 1))),
            )
        return leaf + (1 << lowest), jnp.int32(1 << (lowest - 1))

    def group_side(slot):
        if slot == 0:
            return jnp.int32(1)
        return is_top.astype(jnp.int32)

    def has_group(slot):
        return jnp.logical_and(is_host, inside(group_of(slot)[0]))

    def load(i, src, dst):
        return pltpu.make_async_copy(src, dst, load_sem.at[i])

    own_rows = pl.ds(pl.multiple_of(front * rows, rows), rows)
    loads = [
        load(0, rhs_hbm, x_buf),
        load(1, inv_hbm, inv.at[:, own_rows, :]),
        load(2, right_hbm, lw.at[0, :, own_rows, :]),
        load(3, left_hbm, lw.at[1, :, own_rows, :]),
        load(4, sinv_hbm, sinv),
        load(5, sleft_hbm, su.at[0]),
        load(6, sright_hbm, su.at[1]),
        load(7, srhs_hbm, srhs),
        load(8, snoise_hbm, snoise),
        load(9, noise_hbm, n_buf),
    ]
    for copy in loads:
        copy.start()

    barrier = pltpu.get_barrier_semaphore()
    partners = jnp.int32(n_front - 1)
    for step in range(1, n_front):
        pl.semaphore_signal(
            barrier, inc=1, device_id={"front": (front + step) % n_front}, device_id_type=MESH
        )
    greeted = [(leaf - 1, leaf > 0), (leaf + 1, leaf < n_leaf - 1)]
    if skipped:
        greeted += [
            (parent, is_joined),
            (leaf - half_span, is_skipped),
            (leaf + half_span, is_skipped),
            (group_host(0), jnp.logical_and(is_joined, inside(group_host(0)))),
            (group_host(1), jnp.logical_and(is_joined, inside(group_host(1)))),
        ]
        for slot in range(2):
            center, reach = group_of(slot)
            greeted += [(center - reach, has_group(slot)), (center + reach, has_group(slot))]
    for target, reached in greeted:
        partners = partners + reached.astype(jnp.int32)

        @pl.when(reached)
        def _():
            pl.semaphore_signal(barrier, inc=1, device_id={"leaf": target}, device_id_type=MESH)

    loads[0].wait()
    pack(x_buf, turned_slots, pk)
    loads[4].wait()
    loads[5].wait()
    wall[0] = tn(sinv[...], su[0]).astype(BF)
    pl.semaphore_wait(barrier, partners)

    width = srhs.shape[1]
    share_rows = width // n_front
    share_here = pl.ds(pl.multiple_of(front * share_rows, share_rows), share_rows)

    def hw_copy(i, slot, target):
        return pltpu.make_async_remote_copy(
            src_ref=wall.at[i, share_here],
            dst_ref=hw.at[slot, share_here],
            send_sem=hw_ssem.at[i],
            recv_sem=hw_rsem.at[slot],
            device_id={"leaf": target},
            device_id_type=MESH,
        )

    if skipped:

        @pl.when(is_joined)
        def _():
            pl.semaphore_signal(known_sem, inc=1, device_id={"leaf": parent}, device_id_type=MESH)

    def exchange(src, dst_at, sends, recvs, step):
        peer = (front + step) % n_front
        return pltpu.make_async_remote_copy(
            src_ref=src.at[peer],
            dst_ref=dst_at(front),
            send_sem=sends.at[step - 1],
            recv_sem=recvs.at[step - 1],
            device_id={"front": peer},
            device_id_type=MESH,
        )

    def arrival(src, dst_at, sends, recvs, step):
        peer = (front + n_front - step) % n_front
        return pltpu.make_async_remote_copy(
            src_ref=src.at[peer],
            dst_ref=dst_at(peer),
            send_sem=sends.at[step - 1],
            recv_sem=recvs.at[step - 1],
            device_id={"front": peer},
            device_id_type=MESH,
        )

    def rows_of(ref):
        return lambda f: ref.at[:, pl.ds(pl.multiple_of(f * rows, rows), rows), :]

    def piece(buf, dx, flip, low, high):
        chip = (x + dx + chips) % chips
        who = 2 * chip + (1 - core if flip else core)
        count, order, _ = buf.shape
        low, high = low * count // 4, high * count // 4
        some = order // n_front
        return buf.at[low:high, pl.ds(pl.multiple_of(who * some, some), some), :]

    routes = [
        (0, 0, 2, 1, False),
        (0, 2, 4, -1, False),
        (0, 0, 4, 0, True),
        (-1, 0, 4, 0, True),
        (-1, 0, 2, 1, False),
        (1, 0, 4, 0, True),
        (1, 2, 4, -1, False),
        (2, 0, 2, 0, True),
        (2, 2, 4, 0, True),
        (0, 2, 4, 1, False),
        (0, 0, 2, -1, False),
    ]

    def route(buf, sends, recvs, i):
        dx, low, high, to, flip = routes[i]
        chip = (x + to + chips) % chips
        peer = 2 * chip + (1 - core if flip else core)
        block = piece(buf, dx, False, low, high)
        return pltpu.make_async_remote_copy(
            src_ref=block,
            dst_ref=block,
            send_sem=sends.at[i],
            recv_sem=recvs.at[i],
            device_id={"front": peer},
            device_id_type=MESH,
        )

    def route_arrival(buf, sends, recvs, i):
        dx, low, high, to, flip = routes[i]
        chip = (x + to + chips) % chips
        peer = 2 * chip + (1 - core if flip else core)
        block = piece(buf, dx - to, flip, low, high)
        return pltpu.make_async_remote_copy(
            src_ref=block,
            dst_ref=block,
            send_sem=sends.at[i],
            recv_sem=recvs.at[i],
            device_id={"front": peer},
            device_id_type=MESH,
        )

    class Gather:
        def __init__(self, buf, sends, recvs):
            self.args = (buf, sends, recvs)

        def send(self, *which):
            for i in which:
                route(*self.args, i).start()

        def take(self, *which):
            for i in which:
                route_arrival(*self.args, i).wait_recv()

        def drain(self):
            for i in range(len(routes)):
                route(*self.args, i).wait_send()

    first = odd
    second = 1 - odd
    gather_inv = Gather(inv, gi_send, gi_recv)
    gather_host = Gather(hw, gh_send, gh_recv)
    gather_one = Gather(lw.at[first], g_send.at[0], g_recv.at[0])
    gather_two = Gather(lw.at[second], g_send.at[1], g_recv.at[1])

    for step in range(1, n_front):
        exchange(pk, rows_of(r2), a_send, a_recv, step).start()
    loads[1].wait()
    gather_inv.send(0, 1, 9, 10, 2)
    loads[2].wait()
    loads[3].wait()
    gather_one.send(0, 1, 9, 10, 2)
    r2[:, own_rows, :] = pk[front]

    loads[6].wait()
    wall[1] = tn(sinv[...], su[1]).astype(BF)
    gather_inv.take(0)
    gather_inv.send(4)
    gather_inv.take(1)
    gather_inv.send(6)
    gather_inv.take(9)
    gather_inv.send(3)
    gather_inv.take(10)
    gather_inv.send(5)
    if skipped:

        @pl.when(is_skipped)
        def _():
            pl.semaphore_wait(known_sem, 2)
            for i in range(2):

                @pl.when(inside(ancestor(i)))
                def _():
                    hw_copy(i, host_slot(i), ancestor(i)).start()

    gather_one.take(0)
    gather_one.send(4)
    gather_one.take(1)
    gather_one.send(6)
    gather_inv.take(4)
    gather_inv.send(7)
    gather_inv.take(6)
    gather_inv.send(8)
    gather_one.take(9)
    gather_one.send(3)
    gather_one.take(10)
    gather_one.send(5)
    gather_two.send(0, 1, 9, 10, 2)
    for step in range(1, n_front):
        arrival(pk, rows_of(r2), a_send, a_recv, step).wait_recv()
    gather_inv.take(2, 3, 5, 7, 8)

    live = cnt_ref[0]
    low_lanes = lax.broadcasted_iota(jnp.int32, (1, 128), 1) < HALF
    alive = [
        jnp.logical_or(
            jnp.logical_and(low_lanes, t < live),
            jnp.logical_and(jnp.logical_not(low_lanes), t + 2 < live),
        )
        for t in range(2)
    ]
    for t in range(2):
        block = r2[t]
        solved = jnp.where(low_lanes, nn(inv[t], block), nn(inv[t + 2], block))
        s2[t] = jnp.where(alive[t], solved, 0.0).astype(BF)

    def toward(side):
        total = jnp.zeros((HALF, srhs.shape[1]), F32)
        for t in range(2):
            turned = s2[t].T
            total = total + nn(turned[0:HALF], lw[side, t])
            total = total + nn(turned[HALF:], lw[side, t + 2])
        return total

    def tl_copy(target):
        return pltpu.make_async_remote_copy(
            src_ref=tl_send,
            dst_ref=tl_recv,
            send_sem=tl_ssem,
            recv_sem=tl_rsem,
            device_id={"leaf": target},
            device_id_type=MESH,
        )

    chunks = [(0, 256), (256, width)] if width > 256 else [(0, width)]

    class Message:
        def __init__(self, src, dst, sends, recvs, target):
            self.parts = [
                pltpu.make_async_remote_copy(
                    src_ref=src.at[:, low:high],
                    dst_ref=dst.at[:, low:high],
                    send_sem=sends.at[n],
                    recv_sem=recvs.at[n],
                    device_id={"leaf": target},
                    device_id_type=MESH,
                )
                for n, (low, high) in enumerate(chunks)
            ]

        def start(self):
            for part in self.parts:
                part.start()

        def wait_send(self):
            for part in self.parts:
                part.wait_send()

        def wait_recv(self):
            for part in self.parts:
                part.wait_recv()

    def up_message(i, h, target):
        return Message(up_send.at[i], up_recv.at[h, i], up_ssem.at[i], up_rsem.at[h, i], target)

    def hu_message(i, slot, which, target):
        return Message(
            up_send.at[near], hu_recv.at[slot, which], hu_ssem.at[i], hu_rsem.at[slot, which], target
        )

    def dn_message(i, h, target):
        return Message(dn_send, dn_recv.at[i], dn_ssem.at[i, h], dn_rsem.at[i], target)

    def v_message(slot, which, side, target):
        return Message(
            v_send.at[slot], dv_recv.at[side], v_ssem.at[slot, which], dv_rsem.at[side], target
        )

    def da_message(target):
        return Message(da, dn_recv.at[near], da_ssem, dn_rsem.at[near], target)

    def zp_message(i, target):
        return Message(zp_send, zp_recv, zp_ssem.at[i], zp_rsem, target)

    def climb():
        rb[...] = res[...].astype(BF)
        for j in range(2):
            i = near if j == 0 else 1 - near
            target = ancestor(i)

            @pl.when(inside(target))
            def _():
                message = up_message(i, own_level, target)
                for n, (low, high) in enumerate(chunks):
                    up_send[i, :, low:high] = nn(rb[...], wall[i, :, low:high]).astype(BF)
                    if j == 1 or not skipped:
                        message.parts[n].start()
                    else:

                        @pl.when(jnp.logical_not(is_joined))
                        def _():
                            message.parts[n].start()

                        @pl.when(jnp.logical_and(is_joined, inside(group_host(parent_near))))
                        def _():
                            to_host(parent_near).parts[n].start()

        if skipped:

            @pl.when(is_joined)
            def _():
                @pl.when(inside(group_host(1 - parent_near)))
                def _():
                    to_host(1 - parent_near).start()

                up_message(near, own_level, parent).start()

    def to_host(side):
        return hu_message(side, host_slot(side), 1 - near, group_host(side))

    def gather_level(h):
        below = lax.shift_left(jnp.int32(1), jnp.int32(h))
        for i in range(2):
            source = leaf + (1 - 2 * i) * below

            @pl.when(inside(source))
            def _():
                up_message(i, h, source).wait_recv()
                res[...] = res[...] - up_recv[h, i].astype(F32)

    gather_one.take(4)
    gather_one.send(7)
    gather_one.take(6)
    gather_one.send(8)
    gather_one.take(2, 3, 5, 7, 8)
    loads[7].wait()
    part_one = toward(first)

    @pl.when(jnp.logical_not(is_even))
    def _():
        tl_send[...] = part_one.astype(BF)
        tl_copy(leaf - 1).start()

    if skipped:

        @pl.when(is_host)
        def _():
            for slot in range(2):

                @pl.when(has_group(slot))
                def _():
                    hw_copy(0, slot, group_of(slot)[0]).wait_recv()

            gather_host.send(0, 1, 9, 10, 2)

    gather_two.take(0)
    gather_two.send(4)
    gather_two.take(1)
    gather_two.send(6)

    @pl.when(is_even)
    def _():
        res[...] = srhs[...].astype(F32) - part_one
        tl_copy(leaf + 1).wait_recv()
        res[...] = res[...] - tl_recv[...].astype(F32)
        climb()

    gather_two.take(9)
    gather_two.send(3)
    gather_two.take(10)
    gather_two.send(5)
    if skipped:

        @pl.when(is_host)
        def _():
            gather_host.take(0)
            gather_host.send(4)
            gather_host.take(1)
            gather_host.send(6)
            gather_host.take(9)
            gather_host.send(3)
            gather_host.take(10)
            gather_host.send(5)

    gather_two.take(4)
    gather_two.send(7)
    gather_two.take(6)
    gather_two.send(8)
    gather_two.take(2, 3, 5, 7, 8)
    part_two = toward(second)

    @pl.when(jnp.logical_and(is_even, leaf > 0))
    def _():
        tl_send[...] = part_two.astype(BF)
        tl_copy(leaf - 1).start()

    @pl.when(jnp.logical_not(is_even))
    def _():
        res[...] = srhs[...].astype(F32) - part_two

        @pl.when(leaf < n_leaf - 1)
        def _():
            tl_copy(leaf + 1).wait_recv()
            res[...] = res[...] - tl_recv[...].astype(F32)

        @pl.when(is_root)
        def _():
            loads[8].wait()
            su[0] = tn(sinv[...], sinv[...]).astype(BF)
            zacc[...] = nn(snoise[...], sinv[...])

        if skipped:

            @pl.when(is_host)
            def _():
                gather_host.take(4)
                gather_host.send(7)
                gather_host.take(6)
                gather_host.send(8)

        @pl.loop(0, level - is_skipped.astype(jnp.int32))
        def _(h):
            gather_level(h)

        if skipped:

            @pl.when(is_host)
            def _():
                gather_host.take(2, 3, 5, 7, 8)
                for slot in range(2):

                    @pl.when(has_group(slot))
                    def _():
                        center, reach = group_of(slot)
                        hu_message(0, slot, 0, center - reach).wait_recv()
                        hu_message(0, slot, 1, center + reach).wait_recv()
                        both = hu_recv[slot, 0].astype(F32) + hu_recv[slot, 1].astype(F32)
                        res[...] = res[...] + nn(both.astype(BF), hw[slot])

        climb()
        if skipped:

            @pl.when(is_skipped)
            def _():
                gather_level(level - 1)
                rb[...] = res[...].astype(BF)

    @pl.when(is_root)
    def _():
        zacc[...] = zacc[...] + nn(rb[...], su[0])

    @pl.when(jnp.logical_not(is_root))
    def _():
        loads[8].wait()
        solved_sep = nt(rb[...], sinv[...]).astype(BF).astype(F32)
        target_sep = (solved_sep + snoise[...].astype(F32)).astype(BF)
        zacc[...] = nn(target_sep, sinv[...])

    if skipped:

        @pl.when(is_skipped)
        def _():
            zp_send[...] = zacc[...].astype(BF)
            for i in range(2):
                zp_message(i, leaf + (1 - 2 * i) * half_span).start()

    loads[9].wait()
    pack(n_buf, turned_slots, pkn)
    for step in range(1, n_front):
        exchange(pkn, rows_of(n2), nz_send, nz_recv, step).start()
    n2[:, own_rows, :] = pkn[front]
    for i in range(2):
        wt[i] = wall[i].T
    if skipped:

        @pl.when(is_host)
        def _():
            for slot in range(2):

                @pl.when(has_group(slot))
                def _():
                    hwt[slot] = hw[slot].T


    is_plain = jnp.logical_not(jnp.logical_or(is_skipped, is_joined))

    def take_draws(i, wanted):
        source = ancestor(i)

        @pl.when(jnp.logical_and(wanted, inside(source)))
        def _():
            dn_message(i, 0, source).wait_recv()
            zacc[...] = zacc[...] - nn(dn_recv[i], wt[i])

    take_draws(1 - near, jnp.logical_not(is_skipped))
    if skipped:

        @pl.when(is_joined)
        def _():
            zp_message(0, parent).wait_recv()
            da[...] = zp_recv[...]

        for i in range(2):

            @pl.when(jnp.logical_and(jnp.logical_not(is_plain), inside(group_host(i))))
            def _():
                v_message(0, 0, i, group_host(i)).wait_recv()

                @pl.when(is_skipped)
                def _():
                    zacc[...] = zacc[...] - dv_recv[i].astype(F32)

                @pl.when(is_joined)
                def _():
                    da[...] = (da[...].astype(F32) - dv_recv[i].astype(F32)).astype(BF)

        @pl.when(is_joined)
        def _():
            @pl.when(level + 1 == lowest)
            def _():
                da_message(leaf + (2 * near - 1) * half_span).start()

            dn_recv[near] = da[...]

    plain_last = jnp.logical_and(is_plain, inside(ancestor(near)))

    @pl.when(plain_last)
    def _():
        dn_message(near, 0, ancestor(near)).wait_recv()

    is_early = jnp.logical_and(level > 0, level < lowest)

    def early(act):
        for i in range(2):
            target = leaf + (1 - 2 * i) * half_span

            @pl.when(jnp.logical_and(is_early, inside(target)))
            def _():
                act(dn_message(i, jnp.maximum(level - 1, 0), target))

        @pl.when(is_even)
        def _():
            act(dn_message(2, 0, leaf + 1))

    has_last = jnp.logical_or(plain_last, is_joined)

    @pl.when(has_last)
    def _():
        for n, (low, high) in enumerate(chunks):
            value = zacc[:, low:high] - nn(dn_recv[near], wt[near, :, low:high])
            zacc[:, low:high] = value
            dn_send[:, low:high] = value.astype(BF)
            early(lambda message: message.parts[n].start())

    @pl.when(jnp.logical_not(has_last))
    def _():
        dn_send[...] = zacc[...].astype(BF)

    sep_high[...] = dn_send[...]
    sep_low[...] = (zacc[...] - dn_send[...].astype(F32)).astype(BF)

    def for_level(h, act):
        below = lax.shift_left(jnp.int32(1), jnp.int32(h))
        bypassed = jnp.logical_or(
            any_of(jnp.int32(h), skipped), jnp.logical_and(is_skipped, h >= level - 2)
        )
        for i in range(2):
            target = leaf + (1 - 2 * i) * below

            @pl.when(jnp.logical_and(jnp.logical_not(bypassed), inside(target)))
            def _():
                act(dn_message(i, h, target))

    def begin(message):
        message.start()

    def left(message):
        message.wait_send()

    steps = jnp.maximum(level - lowest + 1, 0)

    @pl.loop(0, steps)
    def _(step):
        for_level(level - 1 - step, begin)

    if skipped:

        def to_group(slot):
            center, reach = group_of(slot)
            return [
                v_message(slot, which, group_side(slot), target)
                for which, target in enumerate((center - reach, center + reach, center))
            ]

        for slot in (1, 0):

            @pl.when(has_group(slot))
            def _():
                v_send[slot] = nn(dn_send[...], hwt[slot]).astype(BF)
                for message in to_group(slot):
                    message.start()

        for slot in range(2):

            @pl.when(has_group(slot))
            def _():
                for message in to_group(slot):
                    message.wait_send()

    @pl.loop(0, steps)
    def _(step):
        for_level(level - 1 - step, left)

    early(left)

    @pl.loop(steps + is_early.astype(jnp.int32), level)
    def _(step):
        for_level(level - 1 - step, begin)
        for_level(level - 1 - step, left)

    own_dup[0:HALF] = dn_send[...]
    own_dup[HALF:] = dn_send[...]

    def pulled(side, dup):
        return [
            jnp.where(low_lanes, nt(lw[side, t], dup), nt(lw[side, t + 2], dup)) for t in range(2)
        ]

    for t, value in enumerate(pulled(0, own_dup[...])):
        pull[t] = value
    for step in range(1, n_front):
        arrival(pkn, rows_of(n2), nz_send, nz_recv, step).wait_recv()

    @pl.when(jnp.logical_not(is_even))
    def _():
        dn_message(2, 0, leaf - 1).wait_recv()
        prev_dup[0:HALF] = dn_recv[2]

    @pl.when(jnp.logical_and(is_even, leaf > 0))
    def _():
        prev_dup[0:HALF] = dn_recv[0]

    @pl.when(leaf == 0)
    def _():
        prev_dup[0:HALF] = jnp.zeros((HALF, prev_dup.shape[1]), BF)

    prev_dup[HALF:] = prev_dup[0:HALF]
    for t, value in enumerate(pulled(1, prev_dup[...])):
        mixed = s2[t].astype(F32) + n2[t].astype(F32) - pull[t] - value
        mixed = jnp.where(alive[t], mixed, 0.0).astype(BF)
        drawn = jnp.where(low_lanes, tn(inv[t], mixed), tn(inv[t + 2], mixed)).astype(BF)
        for f in range(n_front):
            d2[f, t] = drawn[f * rows : f * rows + rows]

    for step in range(1, n_front):
        exchange(d2, lambda f: o2.at[f], o_send, o_recv, step).start()
    o2[front] = d2[front]
    for step in range(1, n_front):
        arrival(d2, lambda f: o2.at[f], o_send, o_recv, step).wait_recv()

    for t in range(2):
        for slab in range(n_front // 2):
            lanes = slice(slab * 128, slab * 128 + 128)
            a = o2[2 * slab, t]
            b = o2[2 * slab + 1, t]
            turned_slots[t, :, lanes] = jnp.concatenate([a[:, :HALF], b[:, :HALF]], axis=1)
            turned_slots[t + 2, :, lanes] = jnp.concatenate([a[:, HALF:], b[:, HALF:]], axis=1)
    leaf_out[...] = jnp.swapaxes(turned_slots[...], 0, 1)

    for step in range(1, n_front):
        exchange(pk, rows_of(r2), a_send, a_recv, step).wait_send()
        exchange(pkn, rows_of(n2), nz_send, nz_recv, step).wait_send()
        exchange(d2, lambda f: o2.at[f], o_send, o_recv, step).wait_send()
    gather_inv.drain()
    gather_one.drain()
    gather_two.drain()

    @pl.when(leaf > 0)
    def _():
        tl_copy(leaf - 1).wait_send()

    for i in range(2):
        target = ancestor(i)

        @pl.when(inside(target))
        def _():
            up_message(i, own_level, target).wait_send()

    if skipped:

        @pl.when(is_joined)
        def _():
            for side in range(2):

                @pl.when(inside(group_host(side)))
                def _():
                    to_host(side).wait_send()

            @pl.when(level + 1 == lowest)
            def _():
                da_message(leaf + (2 * near - 1) * half_span).wait_send()

        @pl.when(is_skipped)
        def _():
            for i in range(2):
                zp_message(i, leaf + (1 - 2 * i) * half_span).wait_send()

                @pl.when(inside(ancestor(i)))
                def _():
                    hw_copy(i, host_slot(i), ancestor(i)).wait_send()

        @pl.when(is_host)
        def _():
            gather_host.drain()


def on_device(
    leaf_rhs,
    sep_rhs,
    leaf_noise,
    sep_noise,
    leaf_inverse,
    leaf_left,
    leaf_right,
    sep_inverse,
    sep_left,
    sep_right,
    leaf_count,
):
    n_leaf = lax.axis_size("leaf")
    n_front = lax.axis_size("front")
    depth = n_leaf.bit_length() - 1
    _, rows, slots, samples = leaf_rhs.shape
    share, width = sep_rhs.shape[1:]
    order = rows * n_front
    hbm = pl.BlockSpec(memory_space=pltpu.HBM)
    vmem = pl.BlockSpec(memory_space=pltpu.VMEM)
    dma = pltpu.SemaphoreType.DMA
    leaf_draws, sep_high, sep_low = pl.pallas_call(
        functools.partial(kernel, n_leaf, n_front, depth),
        out_shape=(
            jax.ShapeDtypeStruct((rows, slots, samples), BF),
            jax.ShapeDtypeStruct((share, width), BF),
            jax.ShapeDtypeStruct((share, width), BF),
        ),
        in_specs=[pl.BlockSpec(memory_space=pltpu.SMEM)] + [hbm] * 10,
        out_specs=(vmem, vmem, vmem),
        scratch_shapes=[
            pltpu.VMEM((rows, slots, samples), BF),
            pltpu.VMEM((rows, slots, samples), BF),
            pltpu.VMEM((slots, rows, samples), BF),
            pltpu.VMEM((n_front, 2, rows, 128), BF),
            pltpu.VMEM((n_front, 2, rows, 128), BF),
            pltpu.VMEM((2, order, 128), BF),
            pltpu.VMEM((2, order, 128), BF),
            pltpu.VMEM((slots, order, order), BF),
            pltpu.VMEM((2, slots, order, width), BF),
            pltpu.VMEM((share, width), BF),
            pltpu.VMEM((share, width), BF),
            pltpu.VMEM((width, width), BF),
            pltpu.VMEM((2, width, width), BF),
            pltpu.VMEM((2, width, width), BF),
            pltpu.VMEM((2, width, width), BF),
            pltpu.VMEM((2, width, width), BF),
            pltpu.VMEM((2, width, width), BF),
            pltpu.VMEM((2, order, 128), BF),
            pltpu.VMEM((share, width), F32),
            pltpu.VMEM((share, width), BF),
            pltpu.VMEM((share, width), F32),
            pltpu.VMEM((share, width), BF),
            pltpu.VMEM((share, width), BF),
            pltpu.VMEM((2, share, width), BF),
            pltpu.VMEM((depth, 2, share, width), BF),
            pltpu.VMEM((share, width), BF),
            pltpu.VMEM((3, share, width), BF),
            pltpu.VMEM((share, width), BF),
            pltpu.VMEM((share, width), BF),
            pltpu.VMEM((2, 2, share, width), BF),
            pltpu.VMEM((2, share, width), BF),
            pltpu.VMEM((2, share, width), BF),
            pltpu.VMEM((share, width), BF),
            pltpu.VMEM((2 * share, width), BF),
            pltpu.VMEM((2 * share, width), BF),
            pltpu.VMEM((2, order, 128), F32),
            pltpu.VMEM((n_front, 2, rows, 128), BF),
            pltpu.VMEM((n_front, 2, rows, 128), BF),
            dma((10,)),
            dma((n_front - 1,)),
            dma((n_front - 1,)),
            dma((n_front - 1,)),
            dma((n_front - 1,)),
            dma((11,)),
            dma((11,)),
            dma((2, 11)),
            dma((2, 11)),
            dma,
            dma,
            dma((2, 2)),
            dma((depth, 2, 2)),
            dma((3, depth, 2)),
            dma((3, 2)),
            dma((n_front - 1,)),
            dma((n_front - 1,)),
            dma((2,)),
            dma((2,)),
            dma((11,)),
            dma((11,)),
            dma((2, 2)),
            dma((2, 2, 2)),
            dma((2, 3, 2)),
            dma((2, 2)),
            dma((2,)),
            dma((2, 2)),
            dma((2,)),
            pltpu.SemaphoreType.REGULAR,
        ],
        compiler_params=pltpu.CompilerParams(
            collective_id=0, has_side_effects=True, vmem_limit_bytes=63 * 1024 * 1024
        ),
    )(
        leaf_count,
        leaf_rhs[0],
        leaf_noise[0],
        leaf_inverse[0],
        leaf_left[0],
        leaf_right[0],
        sep_rhs[0],
        sep_noise[0],
        sep_inverse[0],
        sep_left[0],
        sep_right[0],
    )
    sep_draws = sep_high.astype(F32) + sep_low.astype(F32)
    return (leaf_draws.astype(F32)[None], sep_draws[None])


def solution(mesh):
    return jax.shard_map(
        on_device,
        mesh=mesh,
        in_specs=(
            P("leaf", "front", None, None),
            P("leaf", "front", None),
            P("leaf", "front", None, None),
            P("leaf", "front", None),
            P("leaf", None, "front", None),
            P("leaf", None, "front", None),
            P("leaf", None, "front", None),
            P("leaf", None, None),
            P("leaf", None, None),
            P("leaf", None, None),
            P("leaf"),
        ),
        out_specs=(P("leaf", "front", None, None), P("leaf", "front", None)),
        check_vma=False,
    )
```

```python
import functools

import jax
import jax.numpy as jnp
from jax import lax
from jax.experimental import pallas as pl
from jax.experimental.pallas import tpu as pltpu
from jax.sharding import PartitionSpec as P

MESH = pl.DeviceIdType.MESH
BF = jnp.bfloat16
F32 = jnp.float32
HALF = 64
SKIPPED = (3, 5)


def nn(a, b):
    return lax.dot_general(a, b, (((1,), (0,)), ((), ())), preferred_element_type=F32)


def nt(a, b):
    return lax.dot_general(a, b, (((1,), (1,)), ((), ())), preferred_element_type=F32)


def tn(a, b):
    return lax.dot_general(a, b, (((0,), (0,)), ((), ())), preferred_element_type=F32)


def pack(raw_ref, block_ref, packed_ref):
    rows, slots, samples = raw_ref.shape
    for t in range(slots):
        block_ref[t] = raw_ref[:, t, :]
    for slab in range(samples // 128):
        lanes = slice(slab * 128, slab * 128 + 128)
        a = block_ref[0:2, :, lanes].reshape(2 * rows, 128)
        b = block_ref[2:4, :, lanes].reshape(2 * rows, 128)
        for core in range(2):
            part = slice(core * HALF, core * HALF + HALF)
            both = jnp.concatenate([a[:, part], b[:, part]], axis=1)
            packed_ref[2 * slab + core] = both.reshape(2, rows, 128)


def kernel(
    n_leaf,
    n_front,
    depth,
    cnt_ref,
    rhs_hbm,
    noise_hbm,
    inv_hbm,
    left_hbm,
    right_hbm,
    srhs_hbm,
    snoise_hbm,
    sinv_hbm,
    sleft_hbm,
    sright_hbm,
    leaf_out,
    sep_high,
    sep_low,
    x_buf,
    n_buf,
    turned_slots,
    pk,
    pkn,
    r2,
    n2,
    inv,
    lw,
    srhs,
    snoise,
    sinv,
    su,
    wall,
    wt,
    hw,
    hwt,
    s2,
    res,
    rb,
    zacc,
    tl_send,
    tl_recv,
    up_send,
    up_recv,
    dn_send,
    dn_recv,
    zp_send,
    zp_recv,
    hu_recv,
    v_send,
    dv_recv,
    da,
    own_dup,
    prev_dup,
    pull,
    d2,
    o2,
    load_sem,
    a_send,
    a_recv,
    nz_send,
    nz_recv,
    gi_send,
    gi_recv,
    g_send,
    g_recv,
    tl_ssem,
    tl_rsem,
    up_ssem,
    up_rsem,
    dn_ssem,
    dn_rsem,
    o_send,
    o_recv,
    hw_ssem,
    hw_rsem,
    gh_send,
    gh_recv,
    hu_ssem,
    hu_rsem,
    v_ssem,
    dv_rsem,
    da_ssem,
    zp_ssem,
    zp_rsem,
    known_sem,
):
    leaf = lax.axis_index("leaf")
    front = lax.axis_index("front")
    chips = n_front // 2
    x = front // 2
    core = front % 2
    rows = x_buf.shape[0]
    pos = leaf + 1
    level = jnp.int32(0)
    for bit in range(1, depth + 1):
        level = level + (pos % (1 << bit) == 0).astype(jnp.int32)
    span = jnp.int32(1)
    for bit in range(1, depth + 1):
        span = jnp.where(pos % (1 << bit) == 0, jnp.int32(1 << bit), span)
    odd = leaf % 2
    is_even = odd == 0
    is_root = level == depth

    def inside(target):
        return jnp.logical_and(target >= 0, target < n_leaf)

    def any_of(value, levels):
        found = jnp.bool_(False)
        for one in levels:
            found = jnp.logical_or(found, value == one)
        return found

    skipped = tuple(one for one in SKIPPED if one < depth)
    is_skipped = any_of(level, skipped)
    is_joined = any_of(level + 1, skipped)
    joined = is_joined.astype(jnp.int32)
    near = ((pos // span) % 4 == 1).astype(jnp.int32)
    parent = leaf + (2 * near - 1) * span
    parent_near = (((parent + 1) // (2 * span)) % 4 == 1).astype(jnp.int32)
    own_level = jnp.minimum(level, depth - 1)
    half_span = jnp.maximum(span // 2, 1)
    lowest = skipped[0] if skipped else depth
    is_host = level > lowest
    is_top = leaf == n_leaf - 1
    top_hosts_two = len(skipped) == 2

    def ancestor(i):
        return leaf + (2 * i - 1) * span

    def group_host(i):
        return jnp.where(is_skipped, ancestor(i), parent + (2 * i - 1) * 2 * span)

    def host_slot(i):
        far_group = jnp.logical_or(level == skipped[-1], level + 1 == skipped[-1])
        return jnp.where(jnp.logical_and(far_group, top_hosts_two), 1, 1 - i)

    def group_of(slot):
        if slot == 0:
            return leaf - (1 << lowest), jnp.int32(1 << (lowest - 1))
        if top_hosts_two:
            other = 1 << skipped[-1]
            return (
                jnp.where(is_top, leaf - other, leaf + (1 << lowest)),
                jnp.where(is_top, jnp.int32(other // 2), jnp.int32(1 << (lowest - 1))),
            )
        return leaf + (1 << lowest), jnp.int32(1 << (lowest - 1))

    def group_side(slot):
        if slot == 0:
            return jnp.int32(1)
        return is_top.astype(jnp.int32)

    def has_group(slot):
        return jnp.logical_and(is_host, inside(group_of(slot)[0]))

    def load(i, src, dst):
        return pltpu.make_async_copy(src, dst, load_sem.at[i])

    own_rows = pl.ds(pl.multiple_of(front * rows, rows), rows)
    loads = [
        load(0, rhs_hbm, x_buf),
        load(1, inv_hbm, inv.at[:, own_rows, :]),
        load(2, right_hbm, lw.at[0, :, own_rows, :]),
        load(3, left_hbm, lw.at[1, :, own_rows, :]),
        load(4, sinv_hbm, sinv),
        load(5, sleft_hbm, su.at[0]),
        load(6, sright_hbm, su.at[1]),
        load(7, srhs_hbm, srhs),
        load(8, snoise_hbm, snoise),
        load(9, noise_hbm, n_buf),
    ]
    for copy in loads:
        copy.start()

    barrier = pltpu.get_barrier_semaphore()
    partners = jnp.int32(n_front - 1)
    for step in range(1, n_front):
        pl.semaphore_signal(
            barrier, inc=1, device_id={"front": (front + step) % n_front}, device_id_type=MESH
        )
    greeted = [(leaf - 1, leaf > 0), (leaf + 1, leaf < n_leaf - 1)]
    if skipped:
        greeted += [
            (parent, is_joined),
            (leaf - half_span, is_skipped),
            (leaf + half_span, is_skipped),
            (group_host(0), jnp.logical_and(is_joined, inside(group_host(0)))),
            (group_host(1), jnp.logical_and(is_joined, inside(group_host(1)))),
        ]
        for slot in range(2):
            center, reach = group_of(slot)
            greeted += [(center - reach, has_group(slot)), (center + reach, has_group(slot))]
    for target, reached in greeted:
        partners = partners + reached.astype(jnp.int32)

        @pl.when(reached)
        def _():
            pl.semaphore_signal(barrier, inc=1, device_id={"leaf": target}, device_id_type=MESH)

    loads[0].wait()
    pack(x_buf, turned_slots, pk)
    loads[4].wait()
    loads[5].wait()
    wall[0] = tn(sinv[...], su[0]).astype(BF)
    pl.semaphore_wait(barrier, partners)

    width = srhs.shape[1]
    share_rows = width // n_front
    share_here = pl.ds(pl.multiple_of(front * share_rows, share_rows), share_rows)

    def hw_copy(i, slot, target):
        return pltpu.make_async_remote_copy(
            src_ref=wall.at[i, share_here],
            dst_ref=hw.at[slot, share_here],
            send_sem=hw_ssem.at[i],
            recv_sem=hw_rsem.at[slot],
            device_id={"leaf": target},
            device_id_type=MESH,
        )

    if skipped:

        @pl.when(is_joined)
        def _():
            pl.semaphore_signal(known_sem, inc=1, device_id={"leaf": parent}, device_id_type=MESH)

    far_first = sorted(range(1, n_front), key=lambda step: abs(step - n_front // 2))

    def exchange(src, dst_at, sends, recvs, step):
        peer = (front + step) % n_front
        return pltpu.make_async_remote_copy(
            src_ref=src.at[peer],
            dst_ref=dst_at(front),
            send_sem=sends.at[step - 1],
            recv_sem=recvs.at[step - 1],
            device_id={"front": peer},
            device_id_type=MESH,
        )

    def arrival(src, dst_at, sends, recvs, step):
        peer = (front + n_front - step) % n_front
        return pltpu.make_async_remote_copy(
            src_ref=src.at[peer],
            dst_ref=dst_at(peer),
            send_sem=sends.at[step - 1],
            recv_sem=recvs.at[step - 1],
            device_id={"front": peer},
            device_id_type=MESH,
        )

    def rows_of(ref):
        return lambda f: ref.at[:, pl.ds(pl.multiple_of(f * rows, rows), rows), :]

    def piece(buf, dx, flip, low, high):
        chip = (x + dx + chips) % chips
        who = 2 * chip + (1 - core if flip else core)
        count, order, _ = buf.shape
        low, high = low * count // 4, high * count // 4
        some = order // n_front
        return buf.at[low:high, pl.ds(pl.multiple_of(who * some, some), some), :]

    routes = [
        (0, 0, 2, 1, False),
        (0, 2, 4, -1, False),
        (0, 0, 4, 0, True),
        (-1, 0, 4, 0, True),
        (-1, 0, 2, 1, False),
        (1, 0, 4, 0, True),
        (1, 2, 4, -1, False),
        (2, 0, 2, 0, True),
        (2, 2, 4, 0, True),
        (0, 2, 4, 1, False),
        (0, 0, 2, -1, False),
    ]

    def route(buf, sends, recvs, i):
        dx, low, high, to, flip = routes[i]
        chip = (x + to + chips) % chips
        peer = 2 * chip + (1 - core if flip else core)
        block = piece(buf, dx, False, low, high)
        return pltpu.make_async_remote_copy(
            src_ref=block,
            dst_ref=block,
            send_sem=sends.at[i],
            recv_sem=recvs.at[i],
            device_id={"front": peer},
            device_id_type=MESH,
        )

    def route_arrival(buf, sends, recvs, i):
        dx, low, high, to, flip = routes[i]
        chip = (x + to + chips) % chips
        peer = 2 * chip + (1 - core if flip else core)
        block = piece(buf, dx - to, flip, low, high)
        return pltpu.make_async_remote_copy(
            src_ref=block,
            dst_ref=block,
            send_sem=sends.at[i],
            recv_sem=recvs.at[i],
            device_id={"front": peer},
            device_id_type=MESH,
        )

    class Gather:
        def __init__(self, buf, sends, recvs):
            self.args = (buf, sends, recvs)

        def send(self, *which):
            for i in which:
                route(*self.args, i).start()

        def take(self, *which):
            for i in which:
                route_arrival(*self.args, i).wait_recv()

        def drain(self):
            for i in range(len(routes)):
                route(*self.args, i).wait_send()

    first = odd
    second = 1 - odd
    gather_inv = Gather(inv, gi_send, gi_recv)
    gather_host = Gather(hw, gh_send, gh_recv)
    gather_one = Gather(lw.at[first], g_send.at[0], g_recv.at[0])
    gather_two = Gather(lw.at[second], g_send.at[1], g_recv.at[1])

    for step in far_first:
        exchange(pk, rows_of(r2), a_send, a_recv, step).start()
    loads[1].wait()
    gather_inv.send(0, 1, 9, 10, 2)
    loads[2].wait()
    loads[3].wait()
    gather_one.send(0, 1, 9, 10, 2)
    r2[:, own_rows, :] = pk[front]

    loads[6].wait()
    wall[1] = tn(sinv[...], su[1]).astype(BF)
    gather_inv.take(0)
    gather_inv.send(4)
    gather_inv.take(1)
    gather_inv.send(6)
    gather_inv.take(9)
    gather_inv.send(3)
    gather_inv.take(10)
    gather_inv.send(5)
    if skipped:

        @pl.when(is_skipped)
        def _():
            pl.semaphore_wait(known_sem, 2)
            for i in range(2):

                @pl.when(inside(ancestor(i)))
                def _():
                    hw_copy(i, host_slot(i), ancestor(i)).start()

    gather_one.take(0)
    gather_one.send(4)
    gather_one.take(1)
    gather_one.send(6)
    gather_inv.take(4)
    gather_inv.send(7)
    gather_inv.take(6)
    gather_inv.send(8)
    gather_one.take(9)
    gather_one.send(3)
    gather_one.take(10)
    gather_one.send(5)
    gather_two.send(0, 1, 9, 10, 2)
    for step in range(1, n_front):
        arrival(pk, rows_of(r2), a_send, a_recv, step).wait_recv()
    gather_inv.take(2, 3, 5, 7, 8)

    live = cnt_ref[0]
    low_lanes = lax.broadcasted_iota(jnp.int32, (1, 128), 1) < HALF
    alive = [
        jnp.logical_or(
            jnp.logical_and(low_lanes, t < live),
            jnp.logical_and(jnp.logical_not(low_lanes), t + 2 < live),
        )
        for t in range(2)
    ]
    for t in range(2):
        block = r2[t]
        solved = jnp.where(low_lanes, nn(inv[t], block), nn(inv[t + 2], block))
        s2[t] = jnp.where(alive[t], solved, 0.0).astype(BF)

    def toward(side):
        total = jnp.zeros((HALF, srhs.shape[1]), F32)
        for t in range(2):
            turned = s2[t].T
            total = total + nn(turned[0:HALF], lw[side, t])
            total = total + nn(turned[HALF:], lw[side, t + 2])
        return total

    def tl_copy(target):
        return pltpu.make_async_remote_copy(
            src_ref=tl_send,
            dst_ref=tl_recv,
            send_sem=tl_ssem,
            recv_sem=tl_rsem,
            device_id={"leaf": target},
            device_id_type=MESH,
        )

    chunks = [(0, 256), (256, width)] if width > 256 else [(0, width)]

    class Message:
        def __init__(self, src, dst, sends, recvs, target):
            self.parts = [
                pltpu.make_async_remote_copy(
                    src_ref=src.at[:, low:high],
                    dst_ref=dst.at[:, low:high],
                    send_sem=sends.at[n],
                    recv_sem=recvs.at[n],
                    device_id={"leaf": target},
                    device_id_type=MESH,
                )
                for n, (low, high) in enumerate(chunks)
            ]

        def start(self):
            for part in self.parts:
                part.start()

        def wait_send(self):
            for part in self.parts:
                part.wait_send()

        def wait_recv(self):
            for part in self.parts:
                part.wait_recv()

    def up_message(i, h, target):
        return Message(up_send.at[i], up_recv.at[h, i], up_ssem.at[i], up_rsem.at[h, i], target)

    def hu_message(i, slot, which, target):
        return Message(
            up_send.at[near], hu_recv.at[slot, which], hu_ssem.at[i], hu_rsem.at[slot, which], target
        )

    def dn_message(i, h, target):
        return Message(dn_send, dn_recv.at[i], dn_ssem.at[i, h], dn_rsem.at[i], target)

    def v_message(slot, which, side, target):
        return Message(
            v_send.at[slot], dv_recv.at[side], v_ssem.at[slot, which], dv_rsem.at[side], target
        )

    def da_message(target):
        return Message(da, dn_recv.at[near], da_ssem, dn_rsem.at[near], target)

    def zp_message(i, target):
        return Message(zp_send, zp_recv, zp_ssem.at[i], zp_rsem, target)

    def climb():
        rb[...] = res[...].astype(BF)
        for j in range(2):
            i = near if j == 0 else 1 - near
            target = ancestor(i)

            @pl.when(inside(target))
            def _():
                message = up_message(i, own_level, target)
                for n, (low, high) in enumerate(chunks):
                    up_send[i, :, low:high] = nn(rb[...], wall[i, :, low:high]).astype(BF)
                    if j == 1 or not skipped:
                        message.parts[n].start()
                    else:

                        @pl.when(jnp.logical_not(is_joined))
                        def _():
                            message.parts[n].start()

                        @pl.when(jnp.logical_and(is_joined, inside(group_host(parent_near))))
                        def _():
                            to_host(parent_near).parts[n].start()

        if skipped:

            @pl.when(is_joined)
            def _():
                @pl.when(inside(group_host(1 - parent_near)))
                def _():
                    to_host(1 - parent_near).start()

                up_message(near, own_level, parent).start()

    def to_host(side):
        return hu_message(side, host_slot(side), 1 - near, group_host(side))

    def gather_level(h):
        below = lax.shift_left(jnp.int32(1), jnp.int32(h))
        for i in range(2):
            source = leaf + (1 - 2 * i) * below

            @pl.when(inside(source))
            def _():
                up_message(i, h, source).wait_recv()
                res[...] = res[...] - up_recv[h, i].astype(F32)

    gather_one.take(4)
    gather_one.send(7)
    gather_one.take(6)
    gather_one.send(8)
    gather_one.take(2, 3, 5, 7, 8)
    loads[7].wait()
    part_one = toward(first)

    @pl.when(jnp.logical_not(is_even))
    def _():
        tl_send[...] = part_one.astype(BF)
        tl_copy(leaf - 1).start()

    if skipped:

        @pl.when(is_host)
        def _():
            for slot in range(2):

                @pl.when(has_group(slot))
                def _():
                    hw_copy(0, slot, group_of(slot)[0]).wait_recv()

            gather_host.send(0, 1, 9, 10, 2)

    gather_two.take(0)
    gather_two.send(4)
    gather_two.take(1)
    gather_two.send(6)

    @pl.when(is_even)
    def _():
        res[...] = srhs[...].astype(F32) - part_one
        tl_copy(leaf + 1).wait_recv()
        res[...] = res[...] - tl_recv[...].astype(F32)
        climb()

    gather_two.take(9)
    gather_two.send(3)
    gather_two.take(10)
    gather_two.send(5)
    if skipped:

        @pl.when(is_host)
        def _():
            gather_host.take(0)
            gather_host.send(4)
            gather_host.take(1)
            gather_host.send(6)
            gather_host.take(9)
            gather_host.send(3)
            gather_host.take(10)
            gather_host.send(5)

    gather_two.take(4)
    gather_two.send(7)
    gather_two.take(6)
    gather_two.send(8)
    gather_two.take(2, 3, 5, 7, 8)
    part_two = toward(second)

    @pl.when(jnp.logical_and(is_even, leaf > 0))
    def _():
        tl_send[...] = part_two.astype(BF)
        tl_copy(leaf - 1).start()

    @pl.when(jnp.logical_not(is_even))
    def _():
        res[...] = srhs[...].astype(F32) - part_two

        @pl.when(leaf < n_leaf - 1)
        def _():
            tl_copy(leaf + 1).wait_recv()
            res[...] = res[...] - tl_recv[...].astype(F32)

        @pl.when(is_root)
        def _():
            loads[8].wait()
            su[0] = tn(sinv[...], sinv[...]).astype(BF)
            zacc[...] = nn(snoise[...], sinv[...])

        if skipped:

            @pl.when(is_host)
            def _():
                gather_host.take(4)
                gather_host.send(7)
                gather_host.take(6)
                gather_host.send(8)

        @pl.loop(0, level - is_skipped.astype(jnp.int32))
        def _(h):
            gather_level(h)

        if skipped:

            @pl.when(is_host)
            def _():
                gather_host.take(2, 3, 5, 7, 8)
                for slot in range(2):

                    @pl.when(has_group(slot))
                    def _():
                        center, reach = group_of(slot)
                        hu_message(0, slot, 0, center - reach).wait_recv()
                        hu_message(0, slot, 1, center + reach).wait_recv()
                        both = hu_recv[slot, 0].astype(F32) + hu_recv[slot, 1].astype(F32)
                        res[...] = res[...] + nn(both.astype(BF), hw[slot])

        climb()
        if skipped:

            @pl.when(is_skipped)
            def _():
                gather_level(level - 1)
                rb[...] = res[...].astype(BF)

    @pl.when(is_root)
    def _():
        zacc[...] = zacc[...] + nn(rb[...], su[0])

    @pl.when(jnp.logical_not(is_root))
    def _():
        loads[8].wait()
        solved_sep = nt(rb[...], sinv[...]).astype(BF).astype(F32)
        target_sep = (solved_sep + snoise[...].astype(F32)).astype(BF)
        zacc[...] = nn(target_sep, sinv[...])

    if skipped:

        @pl.when(is_skipped)
        def _():
            zp_send[...] = zacc[...].astype(BF)
            for i in range(2):
                zp_message(i, leaf + (1 - 2 * i) * half_span).start()

    loads[9].wait()
    pack(n_buf, turned_slots, pkn)
    for step in range(1, n_front):
        exchange(pkn, rows_of(n2), nz_send, nz_recv, step).start()
    n2[:, own_rows, :] = pkn[front]
    for i in range(2):
        wt[i] = wall[i].T
    if skipped:

        @pl.when(is_host)
        def _():
            for slot in range(2):

                @pl.when(has_group(slot))
                def _():
                    hwt[slot] = hw[slot].T


    is_plain = jnp.logical_not(jnp.logical_or(is_skipped, is_joined))

    def take_draws(i, wanted):
        source = ancestor(i)

        @pl.when(jnp.logical_and(wanted, inside(source)))
        def _():
            dn_message(i, 0, source).wait_recv()
            zacc[...] = zacc[...] - nn(dn_recv[i], wt[i])

    take_draws(1 - near, jnp.logical_not(is_skipped))
    if skipped:

        @pl.when(is_joined)
        def _():
            zp_message(0, parent).wait_recv()
            da[...] = zp_recv[...]

        for i in range(2):

            @pl.when(jnp.logical_and(jnp.logical_not(is_plain), inside(group_host(i))))
            def _():
                v_message(0, 0, i, group_host(i)).wait_recv()

                @pl.when(is_skipped)
                def _():
                    zacc[...] = zacc[...] - dv_recv[i].astype(F32)

                @pl.when(is_joined)
                def _():
                    da[...] = (da[...].astype(F32) - dv_recv[i].astype(F32)).astype(BF)

        @pl.when(is_joined)
        def _():
            @pl.when(level + 1 == lowest)
            def _():
                da_message(leaf + (2 * near - 1) * half_span).start()

            dn_recv[near] = da[...]

    plain_last = jnp.logical_and(is_plain, inside(ancestor(near)))

    @pl.when(plain_last)
    def _():
        dn_message(near, 0, ancestor(near)).wait_recv()

    is_early = jnp.logical_and(level > 0, level < lowest)

    def early(act):
        for i in range(2):
            target = leaf + (1 - 2 * i) * half_span

            @pl.when(jnp.logical_and(is_early, inside(target)))
            def _():
                act(dn_message(i, jnp.maximum(level - 1, 0), target))

        @pl.when(is_even)
        def _():
            act(dn_message(2, 0, leaf + 1))

    has_last = jnp.logical_or(plain_last, is_joined)

    @pl.when(has_last)
    def _():
        for n, (low, high) in enumerate(chunks):
            value = zacc[:, low:high] - nn(dn_recv[near], wt[near, :, low:high])
            zacc[:, low:high] = value
            dn_send[:, low:high] = value.astype(BF)
            early(lambda message: message.parts[n].start())

    @pl.when(jnp.logical_not(has_last))
    def _():
        dn_send[...] = zacc[...].astype(BF)

    sep_high[...] = dn_send[...]
    sep_low[...] = (zacc[...] - dn_send[...].astype(F32)).astype(BF)

    def for_level(h, act):
        below = lax.shift_left(jnp.int32(1), jnp.int32(h))
        bypassed = jnp.logical_or(
            any_of(jnp.int32(h), skipped), jnp.logical_and(is_skipped, h >= level - 2)
        )
        for i in range(2):
            target = leaf + (1 - 2 * i) * below

            @pl.when(jnp.logical_and(jnp.logical_not(bypassed), inside(target)))
            def _():
                act(dn_message(i, h, target))

    def begin(message):
        message.start()

    def left(message):
        message.wait_send()

    steps = jnp.maximum(level - lowest + 1, 0)

    @pl.loop(0, steps)
    def _(step):
        for_level(level - 1 - step, begin)

    if skipped:

        def to_group(slot):
            center, reach = group_of(slot)
            return [
                v_message(slot, which, group_side(slot), target)
                for which, target in enumerate((center - reach, center + reach, center))
            ]

        for slot in (1, 0):

            @pl.when(has_group(slot))
            def _():
                v_send[slot] = nn(dn_send[...], hwt[slot]).astype(BF)
                for message in to_group(slot):
                    message.start()

        for slot in range(2):

            @pl.when(has_group(slot))
            def _():
                for message in to_group(slot):
                    message.wait_send()

    @pl.loop(0, steps)
    def _(step):
        for_level(level - 1 - step, left)

    early(left)

    @pl.loop(steps + is_early.astype(jnp.int32), level)
    def _(step):
        for_level(level - 1 - step, begin)
        for_level(level - 1 - step, left)

    own_dup[0:HALF] = dn_send[...]
    own_dup[HALF:] = dn_send[...]

    def pulled(side, dup):
        return [
            jnp.where(low_lanes, nt(lw[side, t], dup), nt(lw[side, t + 2], dup)) for t in range(2)
        ]

    for t, value in enumerate(pulled(0, own_dup[...])):
        pull[t] = value
    for step in range(1, n_front):
        arrival(pkn, rows_of(n2), nz_send, nz_recv, step).wait_recv()

    @pl.when(jnp.logical_not(is_even))
    def _():
        dn_message(2, 0, leaf - 1).wait_recv()
        prev_dup[0:HALF] = dn_recv[2]

    @pl.when(jnp.logical_and(is_even, leaf > 0))
    def _():
        prev_dup[0:HALF] = dn_recv[0]

    @pl.when(leaf == 0)
    def _():
        prev_dup[0:HALF] = jnp.zeros((HALF, prev_dup.shape[1]), BF)

    prev_dup[HALF:] = prev_dup[0:HALF]
    for t, value in enumerate(pulled(1, prev_dup[...])):
        mixed = s2[t].astype(F32) + n2[t].astype(F32) - pull[t] - value
        mixed = jnp.where(alive[t], mixed, 0.0).astype(BF)
        drawn = jnp.where(low_lanes, tn(inv[t], mixed), tn(inv[t + 2], mixed)).astype(BF)
        for f in range(n_front):
            d2[t, f] = drawn[f * rows : f * rows + rows]
        for step in far_first:
            exchange(d2.at[t], lambda f: o2.at[t, f], o_send.at[t], o_recv.at[t], step).start()
        o2[t, front] = d2[t, front]

    for t in range(2):
        for step in range(1, n_front):
            arrival(d2.at[t], lambda f: o2.at[t, f], o_send.at[t], o_recv.at[t], step).wait_recv()

    for t in range(2):
        for slab in range(n_front // 2):
            lanes = slice(slab * 128, slab * 128 + 128)
            a = o2[t, 2 * slab]
            b = o2[t, 2 * slab + 1]
            turned_slots[t, :, lanes] = jnp.concatenate([a[:, :HALF], b[:, :HALF]], axis=1)
            turned_slots[t + 2, :, lanes] = jnp.concatenate([a[:, HALF:], b[:, HALF:]], axis=1)
    leaf_out[...] = jnp.swapaxes(turned_slots[...], 0, 1)

    for step in range(1, n_front):
        exchange(pk, rows_of(r2), a_send, a_recv, step).wait_send()
        exchange(pkn, rows_of(n2), nz_send, nz_recv, step).wait_send()
        for t in range(2):
            exchange(d2.at[t], lambda f: o2.at[t, f], o_send.at[t], o_recv.at[t], step).wait_send()
    gather_inv.drain()
    gather_one.drain()
    gather_two.drain()

    @pl.when(leaf > 0)
    def _():
        tl_copy(leaf - 1).wait_send()

    for i in range(2):
        target = ancestor(i)

        @pl.when(inside(target))
        def _():
            up_message(i, own_level, target).wait_send()

    if skipped:

        @pl.when(is_joined)
        def _():
            for side in range(2):

                @pl.when(inside(group_host(side)))
                def _():
                    to_host(side).wait_send()

            @pl.when(level + 1 == lowest)
            def _():
                da_message(leaf + (2 * near - 1) * half_span).wait_send()

        @pl.when(is_skipped)
        def _():
            for i in range(2):
                zp_message(i, leaf + (1 - 2 * i) * half_span).wait_send()

                @pl.when(inside(ancestor(i)))
                def _():
                    hw_copy(i, host_slot(i), ancestor(i)).wait_send()

        @pl.when(is_host)
        def _():
            gather_host.drain()


def on_device(
    leaf_rhs,
    sep_rhs,
    leaf_noise,
    sep_noise,
    leaf_inverse,
    leaf_left,
    leaf_right,
    sep_inverse,
    sep_left,
    sep_right,
    leaf_count,
):
    n_leaf = lax.axis_size("leaf")
    n_front = lax.axis_size("front")
    depth = n_leaf.bit_length() - 1
    _, rows, slots, samples = leaf_rhs.shape
    share, width = sep_rhs.shape[1:]
    order = rows * n_front
    hbm = pl.BlockSpec(memory_space=pltpu.HBM)
    vmem = pl.BlockSpec(memory_space=pltpu.VMEM)
    dma = pltpu.SemaphoreType.DMA
    leaf_draws, sep_high, sep_low = pl.pallas_call(
        functools.partial(kernel, n_leaf, n_front, depth),
        out_shape=(
            jax.ShapeDtypeStruct((rows, slots, samples), BF),
            jax.ShapeDtypeStruct((share, width), BF),
            jax.ShapeDtypeStruct((share, width), BF),
        ),
        in_specs=[pl.BlockSpec(memory_space=pltpu.SMEM)] + [hbm] * 10,
        out_specs=(vmem, vmem, vmem),
        scratch_shapes=[
            pltpu.VMEM((rows, slots, samples), BF),
            pltpu.VMEM((rows, slots, samples), BF),
            pltpu.VMEM((slots, rows, samples), BF),
            pltpu.VMEM((n_front, 2, rows, 128), BF),
            pltpu.VMEM((n_front, 2, rows, 128), BF),
            pltpu.VMEM((2, order, 128), BF),
            pltpu.VMEM((2, order, 128), BF),
            pltpu.VMEM((slots, order, order), BF),
            pltpu.VMEM((2, slots, order, width), BF),
            pltpu.VMEM((share, width), BF),
            pltpu.VMEM((share, width), BF),
            pltpu.VMEM((width, width), BF),
            pltpu.VMEM((2, width, width), BF),
            pltpu.VMEM((2, width, width), BF),
            pltpu.VMEM((2, width, width), BF),
            pltpu.VMEM((2, width, width), BF),
            pltpu.VMEM((2, width, width), BF),
            pltpu.VMEM((2, order, 128), BF),
            pltpu.VMEM((share, width), F32),
            pltpu.VMEM((share, width), BF),
            pltpu.VMEM((share, width), F32),
            pltpu.VMEM((share, width), BF),
            pltpu.VMEM((share, width), BF),
            pltpu.VMEM((2, share, width), BF),
            pltpu.VMEM((depth, 2, share, width), BF),
            pltpu.VMEM((share, width), BF),
            pltpu.VMEM((3, share, width), BF),
            pltpu.VMEM((share, width), BF),
            pltpu.VMEM((share, width), BF),
            pltpu.VMEM((2, 2, share, width), BF),
            pltpu.VMEM((2, share, width), BF),
            pltpu.VMEM((2, share, width), BF),
            pltpu.VMEM((share, width), BF),
            pltpu.VMEM((2 * share, width), BF),
            pltpu.VMEM((2 * share, width), BF),
            pltpu.VMEM((2, order, 128), F32),
            pltpu.VMEM((2, n_front, rows, 128), BF),
            pltpu.VMEM((2, n_front, rows, 128), BF),
            dma((10,)),
            dma((n_front - 1,)),
            dma((n_front - 1,)),
            dma((n_front - 1,)),
            dma((n_front - 1,)),
            dma((11,)),
            dma((11,)),
            dma((2, 11)),
            dma((2, 11)),
            dma,
            dma,
            dma((2, 2)),
            dma((depth, 2, 2)),
            dma((3, depth, 2)),
            dma((3, 2)),
            dma((2, n_front - 1)),
            dma((2, n_front - 1)),
            dma((2,)),
            dma((2,)),
            dma((11,)),
            dma((11,)),
            dma((2, 2)),
            dma((2, 2, 2)),
            dma((2, 3, 2)),
            dma((2, 2)),
            dma((2,)),
            dma((2, 2)),
            dma((2,)),
            pltpu.SemaphoreType.REGULAR,
        ],
        compiler_params=pltpu.CompilerParams(
            collective_id=0, has_side_effects=True, vmem_limit_bytes=63 * 1024 * 1024
        ),
    )(
        leaf_count,
        leaf_rhs[0],
        leaf_noise[0],
        leaf_inverse[0],
        leaf_left[0],
        leaf_right[0],
        sep_rhs[0],
        sep_noise[0],
        sep_inverse[0],
        sep_left[0],
        sep_right[0],
    )
    sep_draws = sep_high.astype(F32) + sep_low.astype(F32)
    return (leaf_draws.astype(F32)[None], sep_draws[None])


def solution(mesh):
    return jax.shard_map(
        on_device,
        mesh=mesh,
        in_specs=(
            P("leaf", "front", None, None),
            P("leaf", "front", None),
            P("leaf", "front", None, None),
            P("leaf", "front", None),
            P("leaf", None, "front", None),
            P("leaf", None, "front", None),
            P("leaf", None, "front", None),
            P("leaf", None, None),
            P("leaf", None, None),
            P("leaf", None, None),
            P("leaf"),
        ),
        out_specs=(P("leaf", "front", None, None), P("leaf", "front", None)),
        check_vma=False,
    )
```
